32 devices in a mesh: groups: 1, ctx: 2 (over x), fsdp: 16 (over z, y, core).
Axes of the slice: x: 2, y: 2, z: 4, core: 2. Of those that a mesh axis runs over, the one named last changes fastest.
Arguments:
- tokens: bfloat16 [16, 256, 3072], P(('groups', 'fsdp'), 'ctx'), may hold values from -600 to 600
- trace_index: int32 [16, 256], P(('groups', 'fsdp'), 'ctx'), may hold values from 0 to 1, never falling along the last dimension, each value on 1 to 192 neighbouring positions
- input_norm_scale: bfloat16 [3072], replicated, may hold values from 0.099609375 to 1.8984375
- query_weight: bfloat16 [3072, 2048], P('fsdp'), may hold values from -0.109375 to 0.109375
- key_weight: bfloat16 [3072, 1024], P('fsdp'), may hold values from -0.109375 to 0.109375
- value_weight: bfloat16 [3072, 1024], P('fsdp'), may hold values from -0.109375 to 0.109375
- query_down_weight: bfloat16 [3072, 16], replicated, may hold values from -0.109375 to 0.109375
- query_up_weight: bfloat16 [16, 2048], replicated, may hold values from -1.5 to 1.5
- value_down_weight: bfloat16 [3072, 16], replicated, may hold values from -0.109375 to 0.109375
- value_up_weight: bfloat16 [16, 1024], replicated, may hold values from -1.5 to 1.5
- output_gradient: bfloat16 [16, 256, 2048], P(('groups', 'fsdp'), 'ctx'), may hold values from -24 to 24
Outputs:
- grad_a_query: float32 [3072, 16], P('groups')
- grad_b_query: float32 [16, 2048], P('groups')
- grad_a_value: float32 [3072, 16], P('groups')
- grad_b_value: float32 [16, 1024], P('groups')
The draws below stay inside these ranges and needn't reach their ends.
Inputs may be any that keep to these rules, and one draw needn't show every extreme that they name: `trace_index`: ids never fall along a sequence; one trace holds at most 192 positions.
All inputs are finite; a program needn't handle non-finite values.
Results may differ from the reference program's by a relative error of at most 0.013.
Values may be sent and summed in bfloat16 or wider, within the bound.
No kernel may reach another device: no remote copies, remote signals or barrier semaphores. Data moves between devices by JAX's collectives and lax.ppermute only.
A program may use at most 128 MiB of HBM per device.

```python
import math
import jax
import jax.numpy as jnp
import numpy as np
from jax import lax

MODEL_FEATURES = 3072
QUERY_HEADS = 16
KEY_VALUE_HEADS = 8
HEAD_SIZE = 128
ADAPTER_RANK = 16
TOK_DEV = 128
WINDOW = 256
SEQ = 256
TRACES = 2
TRACE = 192
NSEQ = 16
TOKEN_COUNT = 4096


def draw_tokens(key, part):
    first, second, third = jax.random.split(key, 3)
    base = jnp.clip(jax.random.normal(first, (NSEQ, SEQ, MODEL_FEATURES), jnp.float32), -6.0, 6.0)
    row_scale = jnp.exp(jax.random.uniform(second, (NSEQ, SEQ, 1), jnp.float32, 0.0, math.log(10.0)))
    col_scale = jnp.exp(jax.random.uniform(third, (MODEL_FEATURES,), jnp.float32, 0.0, math.log(10.0)))
    return (base * row_scale * col_scale).astype(jnp.bfloat16)


def shard_levels(stream_key, shape, shards, least, high):
    level, own = 1.0, jax.random.fold_in(stream_key, 6)
    for position, parts in shards:
        steps = jnp.exp(jax.random.uniform(jax.random.fold_in(own, position), (parts,), jnp.float32, least / len(shards), high / len(shards)))
        level = level * jnp.repeat(steps, shape[position] // parts).reshape([-1 if axis == position else 1 for axis in range(len(shape))])
    return level


def length_profile(amount, total, limit, lean):
    weights = [(1 << 20) // math.isqrt(rank ** lean) + 1 for rank in range(2, amount + 1)]
    rest, counts = total - limit - (amount - 1), [1] * (amount - 1)
    while rest > 0:
        free = [i for i in range(amount - 1) if counts[i] < limit]
        whole, remaining = sum([weights[i] for i in free]), rest
        for i in free:
            extra = min(limit - counts[i], max(1, remaining * weights[i] // whole), rest)
            counts[i] = counts[i] + extra
            rest = rest - extra
    return np.array([limit] + counts)


def ragged_sizes(own_key, count, total, most, slope):
    if count == 2:
        one = jax.random.randint(own_key, (), max(1, total - most), min(most, total - 1) + 1)
        return jnp.stack([one, total - one])
    lengths = jnp.asarray(length_profile(count, total, most, slope), jnp.int32)
    pairs = (count - 1) // 2
    donor, sink = lengths[1:1 + 2 * pairs:2], lengths[2:2 + 2 * pairs:2]
    margin = jnp.minimum(donor - 1, most - sink)
    moved = jax.random.randint(jax.random.fold_in(own_key, 1), (pairs,), 0, 1 << 20) % (margin + 1)
    lengths = lengths.at[1:1 + 2 * pairs:2].set(donor - moved).at[2:2 + 2 * pairs:2].set(sink + moved)
    return lengths[jax.random.permutation(jax.random.fold_in(own_key, 2), count)]


def bell_draw(key, extent, deviation, reach, shards=(), kind=jnp.bfloat16):
    drawn = jax.random.normal(key, extent, jnp.float32) * deviation
    if len(shards) > 0:
        drawn = shard_levels(key, extent, shards, -0.22, 0.18) * drawn
    return jnp.clip(drawn, min=-reach, max=reach).astype(kind)


def setup_inputs(seed: int = 0, part: int = 0) -> dict:
    key_of = jax.random.split(jax.random.key(seed), 12)
    own_keys = jax.random.split(jax.random.fold_in(key_of[11], part), 12)
    return {
        "tokens": draw_tokens(jax.random.fold_in(jax.random.fold_in(key_of[11], part), 71), part),
        "trace_index": jax.vmap(lambda own: jnp.searchsorted(jnp.cumsum(ragged_sizes(own, TRACES, SEQ, TRACE, 0)), jnp.arange(SEQ), side="right"))(jax.random.split(own_keys[1], NSEQ)).reshape((NSEQ, SEQ)).astype(jnp.int32),
        "input_norm_scale": jnp.clip(1.0 + 0.18 * jax.random.normal(key_of[2], (MODEL_FEATURES,), jnp.float32), 0.099609375, 1.8984375).astype(jnp.bfloat16),
        "query_weight": bell_draw(key_of[3], (MODEL_FEATURES, QUERY_HEADS * HEAD_SIZE), MODEL_FEATURES ** -0.5, 0.109375, ((0, 16),)),
        "key_weight": bell_draw(key_of[4], (MODEL_FEATURES, KEY_VALUE_HEADS * HEAD_SIZE), MODEL_FEATURES ** -0.5, 0.109375, ((0, 16),)),
        "value_weight": bell_draw(key_of[5], (MODEL_FEATURES, KEY_VALUE_HEADS * HEAD_SIZE), MODEL_FEATURES ** -0.5, 0.109375, ((0, 16),)),
        "query_down_weight": bell_draw(key_of[6], (MODEL_FEATURES, ADAPTER_RANK), MODEL_FEATURES ** -0.5, 0.109375),
        "query_up_weight": bell_draw(key_of[7], (ADAPTER_RANK, QUERY_HEADS * HEAD_SIZE), ADAPTER_RANK ** -0.5, 1.5),
        "value_down_weight": bell_draw(key_of[8], (MODEL_FEATURES, ADAPTER_RANK), MODEL_FEATURES ** -0.5, 0.109375),
        "value_up_weight": bell_draw(key_of[9], (ADAPTER_RANK, KEY_VALUE_HEADS * HEAD_SIZE), ADAPTER_RANK ** -0.5, 1.5),
        "output_gradient": bell_draw(own_keys[10], (NSEQ, SEQ, QUERY_HEADS * HEAD_SIZE), 4.0, 24.0, ((0, 16), (1, 2))),
    }


CAP = 50.0
QSCALE = 1.0 / 12.0
ADAPTER_NAME = 0.5
EPS = 1e-06

def normed_rows(values, gain):
    flt = values.astype(jnp.float32)
    meansq = lax.optimization_barrier(jnp.mean(flt * flt, axis=-1, keepdims=True))
    return (flt * lax.rsqrt(meansq + EPS) * gain.astype(jnp.float32)).astype(jnp.bfloat16)

def earlier_blocks(stack, distance):
    filler = jnp.zeros((distance,) + stack.shape[1:], stack.dtype)
    return jnp.concatenate([filler, stack[:stack.shape[0] - distance]], 0)

def later_blocks(stack, distance):
    filler = jnp.zeros((distance,) + stack.shape[1:], stack.dtype)
    return jnp.concatenate([stack[distance:], filler], 0)

def attend_block(operands):
    q_blk, k_blk, v_blk, g_blk, mask = operands
    qf = q_blk.astype(jnp.float32)
    kf = k_blk.astype(jnp.float32)
    vf = v_blk.astype(jnp.float32)
    gf = g_blk.astype(jnp.float32)
    s = jnp.einsum('ikgd,jkd->kgij', qf, kf) * QSCALE
    t = jnp.tanh(s / CAP)
    capped = CAP * t
    expo = jnp.where(mask[None, None], jnp.exp(capped), jnp.float32(0.0))
    weights = expo / lax.optimization_barrier(jnp.sum(expo, axis=-1, keepdims=True))
    weights16 = weights.astype(jnp.bfloat16).astype(jnp.float32)
    attended = jnp.einsum('kgij,jkd->ikgd', weights16, vf)
    dweight = jnp.einsum('ikgd,jkd->kgij', gf, vf)
    delta = jnp.einsum('ikgd,ikgd->kgi', gf, attended)
    dscore = (weights * (dweight - delta[..., None]) * (1.0 - t * t) * QSCALE).astype(jnp.bfloat16)
    query_gradient = jnp.einsum('kgij,jkd->ikgd', dscore.astype(jnp.float32), kf).astype(jnp.bfloat16)
    value_gradient = jnp.einsum('kgij,ikgd->jkd', weights16, gf)
    return (query_gradient, value_gradient)

def reference(tokens, trace_index, input_norm_scale, query_weight, key_weight, value_weight, query_down_weight, query_up_weight, value_down_weight, value_up_weight, output_gradient):
    row_slice = NSEQ * SEQ
    head_group = QUERY_HEADS // KEY_VALUE_HEADS
    window_width = TOK_DEV
    block_list = row_slice // window_width
    per_seq = SEQ // window_width
    normalized_input = normed_rows(tokens.reshape(row_slice, MODEL_FEATURES), input_norm_scale)
    query_reduced = jnp.dot(normalized_input, query_down_weight, preferred_element_type=jnp.float32).astype(jnp.bfloat16)
    value_reduced = jnp.dot(normalized_input, value_down_weight, preferred_element_type=jnp.float32).astype(jnp.bfloat16)
    query_matrix = (jnp.dot(normalized_input, query_weight, preferred_element_type=jnp.float32) + ADAPTER_NAME * jnp.dot(query_reduced, query_up_weight, preferred_element_type=jnp.float32)).astype(jnp.bfloat16)
    key = jnp.dot(normalized_input, key_weight, preferred_element_type=jnp.float32).astype(jnp.bfloat16)
    value_matrix = (jnp.dot(normalized_input, value_weight, preferred_element_type=jnp.float32) + ADAPTER_NAME * jnp.dot(value_reduced, value_up_weight, preferred_element_type=jnp.float32)).astype(jnp.bfloat16)
    query_blocks = query_matrix.reshape(block_list, window_width, KEY_VALUE_HEADS, head_group, HEAD_SIZE)
    gradient_blocks = output_gradient.reshape(block_list, window_width, KEY_VALUE_HEADS, head_group, HEAD_SIZE)
    key_blocks = key.reshape(block_list, window_width, KEY_VALUE_HEADS, HEAD_SIZE)
    value_blocks = value_matrix.reshape(block_list, window_width, KEY_VALUE_HEADS, HEAD_SIZE)
    k_triples = jnp.concatenate([earlier_blocks(key_blocks, 2), earlier_blocks(key_blocks, 1), key_blocks], 1)
    v_triples = jnp.concatenate([earlier_blocks(value_blocks, 2), earlier_blocks(value_blocks, 1), value_blocks], 1)
    seg_blocks = trace_index.reshape(block_list, window_width)
    seg_keys = jnp.concatenate([earlier_blocks(seg_blocks, 2), earlier_blocks(seg_blocks, 1), seg_blocks], 1)
    pos_q = jnp.arange(window_width, dtype=jnp.int32)[:, None]
    pos_k = jnp.arange(3 * window_width, dtype=jnp.int32)[None, :]
    band = (pos_k > pos_q) & (pos_k <= pos_q + WINDOW)
    offset = jnp.arange(block_list, dtype=jnp.int32) % per_seq
    valid = (pos_k >= 2 * window_width)[None] | (pos_k >= window_width)[None] & (offset >= 1)[:, None, None] | (offset >= 2)[:, None, None]
    mask = band[None] & (seg_keys[:, None, :] == seg_blocks[:, :, None]) & valid
    query_gradient, dvalue_triples = lax.map(attend_block, (query_blocks, k_triples, v_triples, gradient_blocks, mask))
    query_gradient = query_gradient.reshape(row_slice, QUERY_HEADS * HEAD_SIZE)
    self_portion = dvalue_triples[:, 2 * window_width:]
    nearby_portion = later_blocks(dvalue_triples[:, window_width:2 * window_width], 1)
    distant_portion = later_blocks(dvalue_triples[:, :window_width], 2)
    value_gradient = (self_portion + nearby_portion + distant_portion).reshape(row_slice, KEY_VALUE_HEADS * HEAD_SIZE)
    query_backward = jnp.dot(query_gradient, query_up_weight.T, preferred_element_type=jnp.float32).astype(jnp.bfloat16)
    value_backward = jnp.dot(value_gradient, value_up_weight.astype(jnp.float32).T, precision=lax.Precision.HIGHEST)
    coefficient = ADAPTER_NAME / math.sqrt(TOKEN_COUNT)
    grad_a_query = jnp.dot(normalized_input.T, query_backward, preferred_element_type=jnp.float32) * coefficient
    grad_b_query = jnp.dot(query_reduced.T, query_gradient, preferred_element_type=jnp.float32) * coefficient
    grad_a_value = jnp.dot(normalized_input.astype(jnp.float32).T, value_backward, precision=lax.Precision.HIGHEST) * coefficient
    grad_b_value = jnp.dot(value_reduced.astype(jnp.float32).T, value_gradient, precision=lax.Precision.HIGHEST) * coefficient
    return (grad_a_query, grad_b_query, grad_a_value, grad_b_value)
```

```python
import functools
import math

import jax
import jax.numpy as jnp
from jax import lax
from jax.experimental import pallas as pl
from jax.experimental.pallas import tpu as pltpu
from jax.sharding import Mesh
from jax.sharding import PartitionSpec as P

HEAD_SIZE = 128
LANES = 128

CAP = 50.0
QSCALE = 1.0 / 12.0
ADAPTER_NAME = 0.5
EPS = 1e-06

GROUP = ("ctx", "y", "c")
ANY = pl.BlockSpec(memory_space=pl.ANY)
VMEM = pl.BlockSpec(memory_space=pltpu.VMEM)
SMEM = pl.BlockSpec(memory_space=pltpu.SMEM)

NT = (((1,), (1,)), ((), ()))
TN = (((0,), (0,)), ((), ()))


def dot(a, b, dims=(((1,), (0,)), ((), ()))):
    return lax.dot_general(a, b, dims, preferred_element_type=jnp.float32)


def swapped(value, axes, distance):
    count = 1
    for axis in axes:
        count *= lax.axis_size(axis)
    return lax.ppermute(value, axes, [(i, i ^ distance) for i in range(count)])


def run_copies(copies, sems):
    for i, (src, dst) in enumerate(copies):
        pltpu.make_async_copy(src, dst, sems.at[i]).start()
    for i, (src, dst) in enumerate(copies):
        pltpu.make_async_copy(src, dst, sems.at[i]).wait()


def pack_weights_kernel(heads, order, place, qw, kw, vw, *rest):
    outs, sems = rest[:-1], rest[-1]
    group = heads * HEAD_SIZE
    copies = []
    for step, out in zip(order, outs):
        mine = place[0] ^ step
        for src, at, wide in ((qw, 0, group), (kw, group, HEAD_SIZE), (vw, group + HEAD_SIZE, HEAD_SIZE)):
            cols = pl.ds(pl.multiple_of(mine * wide, wide), wide)
            copies.append((src.at[:, cols], out.at[:, pl.ds(at, wide)]))
    run_copies(copies, sems)


def pack_weights(place, qw, kw, vw, heads, order):
    rows = qw.shape[0]
    wide = (heads + 2) * HEAD_SIZE
    return pl.pallas_call(
        functools.partial(pack_weights_kernel, heads, order),
        out_shape=[jax.ShapeDtypeStruct((rows, wide), qw.dtype)] * len(order),
        in_specs=[SMEM, ANY, ANY, ANY],
        out_specs=[ANY] * len(order),
        scratch_shapes=[pltpu.SemaphoreType.DMA((3 * len(order),))],
        name="pack_weights",
    )(place, qw, kw, vw)


def pack_columns_kernel(wide, place, src, *rest):
    outs, sems = rest[:-1], rest[-1]
    copies = []
    for step, out in enumerate(outs):
        mine = place[0] ^ step
        copies.append((src.at[:, pl.ds(pl.multiple_of(mine * wide, wide), wide)], out))
    run_copies(copies, sems)


def pack_columns(place, value, parts):
    rows, total = value.shape
    wide = total // parts
    return pl.pallas_call(
        functools.partial(pack_columns_kernel, wide),
        out_shape=[jax.ShapeDtypeStruct((rows, wide), value.dtype)] * parts,
        in_specs=[SMEM, ANY],
        out_specs=[ANY] * parts,
        scratch_shapes=[pltpu.SemaphoreType.DMA((parts,))],
        name="pack_columns",
    )(place, value)


def norm_kernel(tokens, trace, gain, down_q, down_v, *outs):
    flt = tokens[...].astype(jnp.float32)
    meansq = jnp.mean(flt * flt, axis=-1, keepdims=True)
    normed = (flt * lax.rsqrt(meansq + EPS) * gain[...].astype(jnp.float32)).astype(jnp.bfloat16)
    rows, feats = normed.shape
    rank = down_q.shape[0]
    low_q = dot(normed, down_q[...], NT)
    low_v = dot(normed, down_v[...], NT)
    square = (rows, rows)
    diagonal = lax.broadcasted_iota(jnp.int32, square, 0) == lax.broadcasted_iota(jnp.int32, square, 1)
    ids = jnp.sum(jnp.where(diagonal, trace[...].astype(jnp.float32), 0.0), axis=1, keepdims=True)
    filler = jnp.zeros((rows, LANES - 2 * rank - 1), jnp.float32)
    extra = jnp.concatenate([low_q, low_v, ids, filler], 1).astype(jnp.bfloat16)
    part = rows // len(outs)
    for i, out in enumerate(outs):
        out[:, :feats] = normed[i * part : (i + 1) * part]
        out[:, feats:] = extra[i * part : (i + 1) * part]


def norm_tokens(tokens, trace, gain, down_q, down_v, pieces):
    rows, feats = tokens.shape
    return pl.pallas_call(
        norm_kernel,
        out_shape=[jax.ShapeDtypeStruct((rows // pieces, feats + LANES), jnp.bfloat16)] * pieces,
        in_specs=[VMEM] * 5,
        out_specs=[VMEM] * pieces,
        compiler_params=pltpu.CompilerParams(vmem_limit_bytes=32 * 2**20),
        name="norm_tokens",
    )(tokens, trace, gain, down_q, down_v)


def attend_kernel(plan, *refs):
    n_w, n_x, n_g = len(plan["w"]), len(plan["x"]), len(plan["g"])
    place, up_q, up_v = refs[:3]
    w_refs = refs[3 : 3 + n_w]
    x_refs = refs[3 + n_w : 3 + n_w + n_x]
    g_refs = refs[3 + n_w + n_x : 3 + n_w + n_x + n_g]
    rest = refs[3 + n_w + n_x + n_g :]
    n_out = plan["parts"]
    ga_outs, gb_out = rest[:n_out], rest[n_out]
    x_all, w_all, g_all, pulls, sems = rest[n_out + 1 :]

    feats, heads, seq, window = plan["feats"], plan["heads"], plan["seq"], plan["window"]
    rank = up_q.shape[0]
    group = heads * HEAD_SIZE
    tokens = x_all.shape[0]

    waits, slot = [], 0
    for kind, sources, target in (("x", x_refs, x_all), ("g", g_refs, g_all), ("w", w_refs, w_all)):
        done = {}
        for (offset, condition, key), src in zip(plan[kind], sources):
            if key not in done:
                done[key] = slot
                slot += 1
            rows = src.shape[0]
            begin = pl.multiple_of(offset(place), 16)
            copy = pltpu.make_async_copy(src, target.at[pl.ds(begin, rows), :], sems.at[done[key]])
            if condition is None:
                copy.start()
                waits.append(copy)
            else:
                pl.when(condition(place))(copy.start)
                if key == plan_first(plan[kind], key, offset):
                    waits.append(copy)

    mine = place[0]
    uq = up_q[:, pl.ds(pl.multiple_of(mine * group, group), group)]
    uv = up_v[:, pl.ds(pl.multiple_of(mine * HEAD_SIZE, HEAD_SIZE), HEAD_SIZE)]
    zero = functools.partial(jnp.zeros, dtype=jnp.float32)
    top = jnp.concatenate([ADAPTER_NAME * uq.astype(jnp.float32), zero((rank, 2 * HEAD_SIZE))], 1)
    low = jnp.concatenate([zero((rank, group + HEAD_SIZE)), ADAPTER_NAME * uv.astype(jnp.float32)], 1)
    pad = zero((LANES - 2 * rank, group + 2 * HEAD_SIZE))
    w_all[feats:, :] = jnp.concatenate([top, low, pad], 0).astype(jnp.bfloat16)
    for copy in waits:
        copy.wait()

    id_row = jnp.where(lax.broadcasted_iota(jnp.int32, (8, LANES), 1) == 2 * rank, 1.0, 0.0).astype(jnp.bfloat16)
    span = min(seq, window)
    blocks = seq // span

    def one_sequence(index, total):
        first = pl.multiple_of(index * seq, seq)
        rows = x_all[pl.ds(first, seq), :]
        qkv = dot(rows, w_all[...]).astype(jnp.bfloat16)
        extra = rows[:, feats:]
        ids_key = dot(id_row, extra, NT)[:1]
        ids_query = extra[:, 2 * rank : 2 * rank + 1].astype(jnp.float32)
        keys = qkv[:, group : group + HEAD_SIZE]
        values = qkv[:, group + HEAD_SIZE :]
        grads = g_all[pl.ds(first, seq), :]
        dq_parts = [[] for _ in range(heads)]
        dv_parts = [None] * blocks
        for block in range(blocks):
            lo, hi = block * span, (block + 1) * span
            back = max(0, lo - span)
            kb, vb = keys[back:hi], values[back:hi]
            shape = (span, hi - back)
            pos_q = lax.broadcasted_iota(jnp.int32, shape, 0) + lo
            pos_k = lax.broadcasted_iota(jnp.int32, shape, 1) + back
            mask = (pos_k <= pos_q) & (pos_k > pos_q - window)
            mask = mask & (ids_query[lo:hi] == ids_key[:, back:hi])
            for head in range(heads):
                cols = slice(head * HEAD_SIZE, (head + 1) * HEAD_SIZE)
                q, g = qkv[lo:hi, cols], grads[lo:hi, cols]
                t = jnp.tanh(dot(q, kb, NT) * (QSCALE / CAP))
                expo = jnp.where(mask, jnp.exp(CAP * t), 0.0)
                weights = expo / jnp.sum(expo, axis=-1, keepdims=True)
                weights16 = weights.astype(jnp.bfloat16)
                dweight = dot(g, vb, NT)
                delta = jnp.sum(weights16.astype(jnp.float32) * dweight, axis=-1, keepdims=True)
                dscore = (weights * (dweight - delta) * (1.0 - t * t) * QSCALE).astype(jnp.bfloat16)
                dq_parts[head].append(dot(dscore, kb).astype(jnp.bfloat16))
                dv = dot(weights16, g, TN)
                for at in range(back // span, block + 1):
                    piece = dv[at * span - back : (at + 1) * span - back]
                    dv_parts[at] = piece if dv_parts[at] is None else dv_parts[at] + piece
        dq = jnp.concatenate([jnp.concatenate(parts, 0) for parts in dq_parts], 1)
        dv = jnp.concatenate(dv_parts, 0)
        dv_hi = dv.astype(jnp.bfloat16)
        dv_lo = (dv - dv_hi.astype(jnp.float32)).astype(jnp.bfloat16)
        pull_q = dot(uq, dq, NT)
        pull_v = dot(uv, dv_hi, NT) + dot(uv, dv_lo, NT)
        pull_v_hi = pull_v.astype(jnp.bfloat16)
        pull_v_lo = (pull_v - pull_v_hi.astype(jnp.float32)).astype(jnp.bfloat16)
        stacked = jnp.concatenate([pull_q.astype(jnp.bfloat16), pull_v_hi, pull_v_lo], 0)
        pulls[:, pl.ds(first, seq)] = stacked
        return total + dot(extra, jnp.concatenate([dq, dv_hi, dv_lo], 1), TN)

    wide = group + 2 * HEAD_SIZE
    total = lax.fori_loop(0, tokens // seq, one_sequence, jnp.zeros((LANES, wide), jnp.float32))
    gb_out[:, :group] = total[:rank, :group]
    gb_out[:, group:] = (
        total[rank : 2 * rank, group : group + HEAD_SIZE] + total[rank : 2 * rank, group + HEAD_SIZE :]
    )
    part = feats // n_out
    for step, out in enumerate(ga_outs):
        begin = pl.multiple_of((mine ^ step) * part, LANES)
        piece = dot(pulls[...], x_all[:, pl.ds(begin, part)])
        out[:rank] = piece[:rank].astype(out.dtype)
        out[rank:] = (piece[rank : 2 * rank] + piece[2 * rank :]).astype(out.dtype)


def plan_first(entries, key, offset):
    for at, _, name in entries:
        if name == key:
            return key if at is offset else None
    return None


def attend(place, up_q, up_v, pieces, plan):
    feats, heads = plan["feats"], plan["heads"]
    rank = up_q.shape[0]
    wide = (heads + 2) * HEAD_SIZE
    tokens, parts = plan["tokens"], plan["parts"]
    arrays = [src for kind in ("w", "x", "g") for src in pieces[kind]]
    slots = sum(len({key for _, _, key in plan[kind]}) for kind in ("w", "x", "g"))
    return pl.pallas_call(
        functools.partial(attend_kernel, plan),
        out_shape=[jax.ShapeDtypeStruct((2 * rank, feats // parts), jnp.bfloat16)] * parts
        + [jax.ShapeDtypeStruct((rank, (heads + 1) * HEAD_SIZE), jnp.float32)],
        in_specs=[SMEM, VMEM, VMEM] + [ANY] * len(arrays),
        out_specs=[VMEM] * (parts + 1),
        scratch_shapes=[
            pltpu.VMEM((tokens, feats + LANES), jnp.bfloat16),
            pltpu.VMEM((feats + LANES, wide), jnp.bfloat16),
            pltpu.VMEM((tokens, heads * HEAD_SIZE), jnp.bfloat16),
            pltpu.VMEM((3 * rank, tokens), jnp.bfloat16),
            pltpu.SemaphoreType.DMA((slots,)),
        ],
        compiler_params=pltpu.CompilerParams(vmem_limit_bytes=48 * 2**20),
        name="attend",
    )(place, up_q, up_v, *arrays)


def sum_kernel(n_ga, *refs):
    gas, gb, out = refs[:n_ga], refs[n_ga], refs[n_ga + 1]
    total = gas[0][...].astype(jnp.float32)
    for ref in gas[1:]:
        total = total + ref[...].astype(jnp.float32)
    rows = total.shape[0]
    out[:rows] = total.astype(out.dtype)
    out[rows:] = gb[...].astype(out.dtype)


def sum_pieces(gas, gb):
    rows, wide = gas[0].shape
    return pl.pallas_call(
        functools.partial(sum_kernel, len(gas)),
        out_shape=jax.ShapeDtypeStruct((rows + gb.shape[0], wide), jnp.bfloat16),
        in_specs=[VMEM] * (len(gas) + 1),
        out_specs=VMEM,
        name="sum_pieces",
    )(*gas, gb)


def scale_kernel(coefficient, *refs):
    total = refs[0][...].astype(jnp.float32)
    for ref in refs[1:-1]:
        total = total + ref[...].astype(jnp.float32)
    refs[-1][...] = (total * coefficient).astype(refs[-1].dtype)


def scale_sum(pieces, coefficient):
    return pl.pallas_call(
        functools.partial(scale_kernel, coefficient),
        out_shape=jax.ShapeDtypeStruct(pieces[0].shape, jnp.bfloat16),
        in_specs=[VMEM] * len(pieces),
        out_specs=VMEM,
        name="scale_sum",
    )(*pieces)


def spread_kernel(rank, group, place, *refs):
    pieces, (aq, bq, av, bv) = refs[:-4], refs[-4:]
    wide = pieces[0].shape[1]
    for step, ref in enumerate(pieces):
        mine = place[0] ^ step
        value = ref[...].astype(jnp.float32)
        at = pl.ds(pl.multiple_of(mine * wide, LANES), wide)
        aq[:, at] = value[:rank]
        av[:, at] = value[rank : 2 * rank]
        bq[:, pl.ds(pl.multiple_of(mine * group, LANES), group)] = value[2 * rank :, :group]
        bv[:, pl.ds(pl.multiple_of(mine * HEAD_SIZE, LANES), HEAD_SIZE)] = value[2 * rank :, group:]


def spread(place, pieces, rank, group, shapes):
    return pl.pallas_call(
        functools.partial(spread_kernel, rank, group),
        out_shape=[jax.ShapeDtypeStruct(shape, jnp.float32) for shape in shapes],
        in_specs=[SMEM] + [VMEM] * len(pieces),
        out_specs=[VMEM] * 4,
        name="spread",
    )(place, *pieces)


def paired_weights(place, qw, kw, vw, heads):
    shards, shard = lax.axis_size("z"), qw.shape[0]
    near, over, aside, across = pack_weights(place, qw, kw, vw, heads, (0, 1, 2, 3))
    near_c = swapped(over, ("c",), 1)
    across_c = swapped(across, ("c",), 1)
    own = [near, near_c, swapped(aside, ("y",), 1), swapped(across_c, ("y",), 1)]

    def rows_of(back, step):
        def offset(p):
            source = lax.rem(p[1] - back + shards, shards)
            return (source * 4 + ((p[0] & 3) ^ step)) * shard

        return offset

    entries, arrays = [], []
    for step, value in enumerate(own):
        entries.append((rows_of(0, step), None, (0, step)))
        arrays.append(value)
    ups, downs = list(own), list(own)
    up_at, down_at = {}, {}
    for hop in range(1, shards):
        for step in range(4):
            ups[step] = lax.ppermute(ups[step], "z", [(i, i + 1) for i in range(hop - 1, shards - 1)])
            downs[step] = lax.ppermute(downs[step], "z", [(i + 1, i) for i in range(shards - hop)])
            up_at[hop, step], down_at[hop, step] = ups[step], downs[step]
    for back in range(1, shards):
        for step in range(4):
            offset = rows_of(back, step)
            entries.append((offset, lambda p, back=back: p[1] >= back, (back, step)))
            arrays.append(up_at[back, step])
            entries.append((rows_of(back, step), lambda p, back=back: p[1] < back, (back, step)))
            arrays.append(down_at[shards - back, step])
    return entries, arrays


def paired_tokens(low, high, rows):
    x_low, y_high = swapped(low, ("ctx",), 1), swapped(high, ("y",), 1)
    x_high, y_low = swapped(high, ("ctx",), 1), swapped(low, ("y",), 1)
    far_low, far_high = swapped(x_low, ("y",), 1), swapped(y_high, ("ctx",), 1)
    half = rows // 2

    def offset_of(step, part):
        def offset(p):
            x = (p[0] >> 2) ^ (step >> 2)
            return (step & 3) * 2 * rows + x * rows + part * half

        return offset

    entries, arrays = [], []
    for step, pair in ((0, (low, high)), (4, (x_low, x_high)), (2, (y_low, y_high)), (6, (far_low, far_high))):
        for part, value in enumerate(pair):
            for core, piece in enumerate((value, swapped(value, ("c",), 1))):
                entries.append((offset_of(step ^ core, part), None, (step ^ core, part)))
                arrays.append(piece)
    return entries, arrays


def paired_gradients(place, output_gradient, rows):
    packed = pack_columns(place, output_gradient, 8)

    def offset_of(step):
        def offset(p):
            return (step & 3) * 2 * rows + ((p[0] >> 2) ^ (step >> 2)) * rows

        return offset

    entries = [(offset_of(step), None, (step,)) for step in range(8)]
    arrays = [packed[0]] + [swapped(packed[step], GROUP, step) for step in range(1, 8)]
    return entries, arrays


def on_device(
    tokens,
    trace_index,
    input_norm_scale,
    query_weight,
    key_weight,
    value_weight,
    query_down_weight,
    query_up_weight,
    value_down_weight,
    value_up_weight,
    output_gradient,
):
    rows, feats = tokens.shape[1:]
    heads_kv = key_weight.shape[1] // HEAD_SIZE
    heads = query_weight.shape[1] // HEAD_SIZE // heads_kv
    group = heads * HEAD_SIZE
    rank = query_up_weight.shape[0]
    sizes = [lax.axis_size(axis) for axis in GROUP]
    parts = math.prod(sizes)
    shards = lax.axis_size("z")
    paired = sizes == [2, 2, 2]
    mine = lax.axis_index(GROUP)
    place = jnp.stack([mine, lax.axis_index("z")]).astype(jnp.int32)

    norm_args = (
        tokens.reshape(rows, feats),
        trace_index.reshape(1, rows),
        input_norm_scale.reshape(1, feats),
        query_down_weight.T,
        value_down_weight.T,
    )
    gradient = output_gradient.reshape(rows, heads_kv * group)
    if paired:
        w_plan, w_arrays = paired_weights(place, query_weight, key_weight, value_weight, heads)
        x_plan, x_arrays = paired_tokens(*norm_tokens(*norm_args, 2), rows)
        g_plan, g_arrays = paired_gradients(place, gradient, rows)
    else:
        shard = query_weight.shape[0]
        split = [
            w.reshape(shard, parts, -1) for w in (query_weight, key_weight, value_weight)
        ]
        columns = jnp.moveaxis(jnp.concatenate(split, -1), 1, 0)
        per = parts // sizes[0]
        columns = lax.dynamic_slice_in_dim(columns, lax.axis_index("ctx") * per, per, 0)
        columns = lax.all_to_all(columns, ("y", "c"), 0, 0, tiled=True).reshape(per * shard, -1)
        weights = lax.all_gather(columns, "z", axis=0, tiled=True)
        (normed,) = norm_tokens(*norm_args, 1)
        normed = lax.all_gather(normed, ("y", "c", "ctx"), axis=0, tiled=True)
        gradient = jnp.moveaxis(gradient.reshape(rows, parts, group), 1, 0)
        gradient = lax.all_to_all(gradient, GROUP, 0, 0, tiled=True)
        gradient = gradient.reshape(sizes[0], per, rows, group)
        gradient = jnp.moveaxis(gradient, 0, 1).reshape(parts * rows, group)
        whole = [(lambda p: 0, None, (0,))]
        w_plan, x_plan, g_plan = whole, whole, whole
        w_arrays, x_arrays, g_arrays = [weights], [normed], [gradient]

    plan = {
        "w": w_plan,
        "x": x_plan,
        "g": g_plan,
        "feats": feats,
        "heads": heads,
        "seq": sizes[0] * rows,
        "window": 2 * rows,
        "tokens": parts * rows,
        "parts": parts,
    }
    pieces = {"w": w_arrays, "x": x_arrays, "g": g_arrays}
    *ga, gb = attend(place, query_up_weight, value_up_weight, pieces, plan)

    coefficient = ADAPTER_NAME / math.sqrt(parts * shards * rows)
    ga = [ga[0]] + [swapped(ga[step], GROUP, step) for step in range(1, parts)]
    mixed = sum_pieces(ga, gb)
    if shards & (shards - 1) == 0 and shards <= 4:
        mixed = [mixed] + [swapped(mixed, ("z",), step) for step in range(1, shards)]
    else:
        mixed = [lax.psum(mixed.astype(jnp.float32), "z")]
    scaled = scale_sum(mixed, coefficient)
    scaled = [scaled] + [swapped(scaled, GROUP, step) for step in range(1, parts)]
    shapes = ((rank, feats), (rank, heads_kv * group), (rank, feats), (rank, heads_kv * HEAD_SIZE))
    aq, bq, av, bv = spread(place, scaled, rank, group, shapes)
    return aq.T, bq, av.T, bv


def solution(mesh):
    groups, ctx, fsdp = (mesh.shape[name] for name in ("groups", "ctx", "fsdp"))

    def run(*args):
        heads_kv = args[4].shape[1] // HEAD_SIZE
        share = heads_kv // ctx
        cores = 2 if share % 2 == 0 else 1
        split = (groups, ctx, fsdp // share, share // cores, cores)
        finer = Mesh(mesh.devices.reshape(split), ("groups", "ctx", "z", "y", "c"))
        whole = ("z", "y", "c")
        sequences = ("groups",) + whole
        by_rows = P(whole, None)
        by_tokens = P(sequences, "ctx", None)
        out = P("groups", None)
        return jax.shard_map(
            on_device,
            mesh=finer,
            in_specs=(
                by_tokens, P(sequences, "ctx"), P(), by_rows, by_rows, by_rows, P(), P(), P(), P(), by_tokens
            ),
            out_specs=(out, out, out, out),
            check_vma=False,
        )(*args)

    return run
```

```python
import functools
import math

import jax
import jax.numpy as jnp
from jax import lax
from jax.experimental import pallas as pl
from jax.experimental.pallas import tpu as pltpu
from jax.sharding import Mesh
from jax.sharding import PartitionSpec as P

HEAD_SIZE = 128
LANES = 128

CAP = 50.0
QSCALE = 1.0 / 12.0
ADAPTER_NAME = 0.5
EPS = 1e-06

GROUP = ("ctx", "y", "c")
ANY = pl.BlockSpec(memory_space=pl.ANY)
VMEM = pl.BlockSpec(memory_space=pltpu.VMEM)
SMEM = pl.BlockSpec(memory_space=pltpu.SMEM)

NT = (((1,), (1,)), ((), ()))
TN = (((0,), (0,)), ((), ()))


def dot(a, b, dims=(((1,), (0,)), ((), ()))):
    return lax.dot_general(a, b, dims, preferred_element_type=jnp.float32)


def swapped(value, axes, distance):
    count = 1
    for axis in axes:
        count *= lax.axis_size(axis)
    return lax.ppermute(value, axes, [(i, i ^ distance) for i in range(count)])


def pack_weights_kernel(heads, place, qw, kw, vw, out):
    group = heads * HEAD_SIZE
    for index in range(out.shape[0]):
        mine = (place[0] // 4) * 4 + index
        for src, at, wide in ((qw, 0, group), (kw, group, HEAD_SIZE), (vw, group + HEAD_SIZE, HEAD_SIZE)):
            out[index, :, at : at + wide] = src[:, pl.ds(pl.multiple_of(mine * wide, wide), wide)]


def pack_weights(place, qw, kw, vw, heads):
    return pl.pallas_call(
        functools.partial(pack_weights_kernel, heads),
        out_shape=jax.ShapeDtypeStruct((4, qw.shape[0], (heads + 2) * HEAD_SIZE), qw.dtype),
        in_specs=[SMEM, VMEM, VMEM, VMEM],
        out_specs=VMEM,
        name="pack_weights",
    )(place, qw, kw, vw)


def fence_kernel(*refs):
    pass


def fence(values, *earlier):
    count = len(values)
    return pl.pallas_call(
        fence_kernel,
        out_shape=[jax.ShapeDtypeStruct(value.shape, value.dtype) for value in values],
        in_specs=[ANY] * (count + len(earlier)),
        out_specs=[ANY] * count,
        input_output_aliases={i: i for i in range(count)},
        name="fence",
    )(*values, *earlier)


def norm_kernel(tokens, trace, gain, down_q, down_v, *rest):
    out = rest[-1]
    flt = tokens[...].astype(jnp.float32)
    meansq = jnp.mean(flt * flt, axis=-1, keepdims=True)
    normed = (flt * lax.rsqrt(meansq + EPS) * gain[...].astype(jnp.float32)[None, :]).astype(jnp.bfloat16)
    rows, feats = normed.shape
    rank = down_q.shape[0]
    low_q = dot(normed, down_q[...], NT)
    low_v = dot(normed, down_v[...], NT)
    square = (rows, rows)
    diagonal = lax.broadcasted_iota(jnp.int32, square, 0) == lax.broadcasted_iota(jnp.int32, square, 1)
    ids = jnp.sum(jnp.where(diagonal, trace[...].astype(jnp.float32), 0.0), axis=1, keepdims=True)
    filler = jnp.zeros((rows, LANES - 2 * rank - 1), jnp.float32)
    extra = jnp.concatenate([low_q, low_v, ids, filler], 1).astype(jnp.bfloat16)
    out[:, :feats] = normed
    out[:, feats:] = extra


def norm_tokens(tokens, trace, gain, down_q, down_v, *earlier):
    rows, feats = tokens.shape
    return pl.pallas_call(
        norm_kernel,
        out_shape=jax.ShapeDtypeStruct((rows, feats + LANES), jnp.bfloat16),
        in_specs=[VMEM] * 5 + [ANY] * len(earlier),
        out_specs=VMEM,
        compiler_params=pltpu.CompilerParams(vmem_limit_bytes=32 * 2**20),
        name="norm_tokens",
    )(tokens, trace, gain, down_q, down_v, *earlier)


class Loads:
    def __init__(self, sems):
        self.sems, self.count, self.waits = sems, 0, []

    def add(self, place, pieces, target):
        for piece, src in pieces:
            offset, sequence, choice = piece
            begin = pl.multiple_of(offset(place), 16)
            rows = src.shape[-2]
            if choice is not None and len(src.shape) == 3:
                src = src.at[choice(place)]
            copy = pltpu.make_async_copy(src, target.at[pl.ds(begin, rows), :], self.sems.at[self.count])
            copy.start()
            self.waits.append((sequence, copy))
            self.count += 1

    def add_either(self, condition, first, second, target):
        copies = [pltpu.make_async_copy(src, target, self.sems.at[self.count]) for src in (first, second)]
        pl.when(condition)(copies[0].start)
        pl.when(jnp.logical_not(condition))(copies[1].start)
        self.waits.append((0, copies[0]))
        self.count += 1

    def wait(self, sequence):
        for needed, copy in self.waits:
            if needed == sequence:
                copy.wait()


def project_kernel(plan, *refs):
    n_x, shards = len(plan["x"]), plan["shards"]
    place, up_q, up_v = refs[:3]
    x_refs, w_refs, rest = refs[3 : 3 + n_x], refs[3 + n_x : -4], refs[-4:]
    out, x_all, w_all, sems = rest
    feats, heads, seq = plan["feats"], plan["heads"], plan["seq"]
    rank, group = up_q.shape[0], heads * HEAD_SIZE
    depth = plan["depth"]

    loads, at = Loads(sems), 0
    for index, (_, condition, sources) in enumerate(shards):
        target = w_all.at[pl.ds(index * depth, depth), :]
        if condition is None:
            loads.add(place, [((lambda p, i=index: i * depth, 0, None), w_refs[at])], w_all)
        else:
            loads.add_either(condition(place), w_refs[at], w_refs[at + 1], target)
        at += len(sources)
    loads.add(place, list(zip(plan["x"], x_refs)), x_all)

    mine = place[0]
    uq = up_q[:, pl.ds(pl.multiple_of(mine * group, group), group)]
    uv = up_v[:, pl.ds(pl.multiple_of(mine * HEAD_SIZE, HEAD_SIZE), HEAD_SIZE)]
    zero = functools.partial(jnp.zeros, dtype=jnp.float32)
    top = jnp.concatenate([ADAPTER_NAME * uq.astype(jnp.float32), zero((rank, 2 * HEAD_SIZE))], 1)
    low = jnp.concatenate([zero((rank, group + HEAD_SIZE)), ADAPTER_NAME * uv.astype(jnp.float32)], 1)
    pad = zero((LANES - 2 * rank, group + 2 * HEAD_SIZE))
    ups = jnp.concatenate([top, low, pad], 0).astype(jnp.bfloat16)

    for index in range(x_all.shape[0] // seq):
        loads.wait(index)
        rows = pl.ds(index * seq, seq)
        total = dot(x_all[rows, feats:], ups)
        for number, (offset, _, _) in enumerate(shards):
            columns = pl.ds(pl.multiple_of(offset(place), LANES), depth)
            total = total + dot(x_all[rows, columns], w_all[number * depth : (number + 1) * depth])
        out[rows, :] = total


def attend_kernel(plan, *refs):
    n_x, n_g, last = len(plan["x"]), len(plan["g"]), plan["last"]
    place, up_q, up_v, base = refs[:4]
    x_refs, g_refs = refs[4 : 4 + n_x], refs[4 + n_x : 4 + n_x + n_g]
    w_refs, rest = refs[4 + n_x + n_g : -8], refs[-8:]
    ga_out, gb_out, x_all, g_all, w_all, base_all, pulls, sems = rest

    feats, heads, seq, window, depth = (plan[k] for k in ("feats", "heads", "seq", "window", "depth"))
    rank, parts = up_q.shape[0], plan["parts"]
    group = heads * HEAD_SIZE
    tokens = x_all.shape[0]
    sequences = tokens // seq

    loads = Loads(sems)
    if last is not None:
        offset, condition = last
        copy = pltpu.make_async_copy(w_refs[0], w_all, sems.at[loads.count])
        loads.count += 1
        pl.when(condition(place))(copy.start)
    for index in range(sequences):
        rows = pl.ds(index * seq, seq)
        copy_base = pltpu.make_async_copy(base.at[rows, :], base_all.at[rows, :], sems.at[loads.count])
        copy_base.start()
        loads.waits.append((index, copy_base))
        loads.count += 1
        for pieces, sources, target in ((plan["x"], x_refs, x_all), (plan["g"], g_refs, g_all)):
            chosen = [(piece, src) for piece, src in zip(pieces, sources) if piece[1] == index]
            loads.add(place, chosen, target)
    if last is not None:

        @pl.when(jnp.logical_not(condition(place)))
        def _():
            w_all[...] = w_refs[1][...]

        pl.when(condition(place))(copy.wait)

    mine = place[0]
    uq = up_q[:, pl.ds(pl.multiple_of(mine * group, group), group)]
    uv = up_v[:, pl.ds(pl.multiple_of(mine * HEAD_SIZE, HEAD_SIZE), HEAD_SIZE)]
    id_row = jnp.where(lax.broadcasted_iota(jnp.int32, (8, LANES), 1) == 2 * rank, 1.0, 0.0).astype(jnp.bfloat16)
    span = min(seq, window)
    blocks = seq // span
    sums = jnp.zeros((LANES, group + 2 * HEAD_SIZE), jnp.float32)

    for index in range(sequences):
        loads.wait(index)
        rows = pl.ds(index * seq, seq)
        qkv = base_all[rows, :]
        if last is not None:
            columns = pl.ds(pl.multiple_of(offset(place), LANES), depth)
            qkv = qkv + dot(x_all[rows, columns], w_all[...])
        qkv = qkv.astype(jnp.bfloat16)
        extra = x_all[rows, feats:]
        ids_key = dot(id_row, extra, NT)[:1]
        ids_query = extra[:, 2 * rank : 2 * rank + 1].astype(jnp.float32)
        keys = qkv[:, group : group + HEAD_SIZE]
        values = qkv[:, group + HEAD_SIZE :]
        grads = g_all[rows, :]
        dq_parts = [[] for _ in range(heads)]
        dv_parts = [None] * blocks
        for block in range(blocks):
            lo, hi = block * span, (block + 1) * span
            back = max(0, lo - span)
            kb, vb = keys[back:hi], values[back:hi]
            shape = (span, hi - back)
            pos_q = lax.broadcasted_iota(jnp.int32, shape, 0) + lo
            pos_k = lax.broadcasted_iota(jnp.int32, shape, 1) + back
            mask = (pos_k <= pos_q) & (pos_k > pos_q - window)
            mask = mask & (ids_query[lo:hi] == ids_key[:, back:hi])
            for head in range(heads):
                cols = slice(head * HEAD_SIZE, (head + 1) * HEAD_SIZE)
                q, g = qkv[lo:hi, cols], grads[lo:hi, cols]
                t = jnp.tanh(dot(q, kb, NT) * (QSCALE / CAP))
                expo = jnp.where(mask, jnp.exp(CAP * t), 0.0)
                weights = expo / jnp.sum(expo, axis=-1, keepdims=True)
                weights16 = weights.astype(jnp.bfloat16)
                dweight = dot(g, vb, NT)
                delta = jnp.sum(weights16.astype(jnp.float32) * dweight, axis=-1, keepdims=True)
                dscore = (weights * (dweight - delta) * (1.0 - t * t) * QSCALE).astype(jnp.bfloat16)
                dq_parts[head].append(dot(dscore, kb).astype(jnp.bfloat16))
                dv = dot(weights16, g, TN)
                for at in range(back // span, block + 1):
                    piece = dv[at * span - back : (at + 1) * span - back]
                    dv_parts[at] = piece if dv_parts[at] is None else dv_parts[at] + piece
        dq = jnp.concatenate([jnp.concatenate(some, 0) for some in dq_parts], 1)
        dv = jnp.concatenate(dv_parts, 0)
        dv_hi = dv.astype(jnp.bfloat16)
        dv_lo = (dv - dv_hi.astype(jnp.float32)).astype(jnp.bfloat16)
        pull_q = dot(uq, dq, NT)
        pull_v = dot(uv, dv_hi, NT) + dot(uv, dv_lo, NT)
        pull_v_hi = pull_v.astype(jnp.bfloat16)
        pull_v_lo = (pull_v - pull_v_hi.astype(jnp.float32)).astype(jnp.bfloat16)
        pulls[:, rows] = jnp.concatenate([pull_q.astype(jnp.bfloat16), pull_v_hi, pull_v_lo], 0)
        sums = sums + dot(extra, jnp.concatenate([dq, dv_hi, dv_lo], 1), TN)

    gb_out[:, :group] = sums[:rank, :group]
    gb_out[:, group:] = sums[rank : 2 * rank, group : group + HEAD_SIZE] + sums[rank : 2 * rank, group + HEAD_SIZE :]
    part = feats // parts
    for index in range(parts):
        piece = dot(pulls[...], x_all[:, index * part : (index + 1) * part])
        ga_out[index, :rank] = piece[:rank].astype(ga_out.dtype)
        ga_out[index, rank:] = (piece[rank : 2 * rank] + piece[2 * rank :]).astype(ga_out.dtype)


def attend(place, up_q, up_v, gathered, plan):
    feats, heads, tokens, parts, seq = (plan[k] for k in ("feats", "heads", "tokens", "parts", "seq"))
    rank = up_q.shape[0]
    wide = (heads + 2) * HEAD_SIZE
    x_plan, x_arrays = zip(*gathered["x"])
    g_plan, g_arrays = zip(*gathered["g"])
    shards = gathered["w"]
    w_arrays = [array for _, _, sources in shards for array in sources]
    depth = w_arrays[0].shape[0]
    plan = dict(plan, x=x_plan, g=g_plan, shards=shards, depth=depth)
    params = pltpu.CompilerParams(vmem_limit_bytes=60 * 2**20)
    base = pl.pallas_call(
        functools.partial(project_kernel, plan),
        out_shape=jax.ShapeDtypeStruct((tokens, wide), jnp.float32),
        in_specs=[SMEM, VMEM, VMEM] + [ANY] * (len(x_arrays) + len(w_arrays)),
        out_specs=VMEM,
        scratch_shapes=[
            pltpu.VMEM((tokens, feats + LANES), jnp.bfloat16),
            pltpu.VMEM((len(shards) * depth, wide), jnp.bfloat16),
            pltpu.SemaphoreType.DMA((len(x_arrays) + len(shards),)),
        ],
        compiler_params=params,
        cost_estimate=pl.CostEstimate(
            flops=2 * tokens * len(shards) * depth * wide,
            bytes_accessed=2 * tokens * feats + 2 * len(shards) * depth * wide + 4 * tokens * wide,
            transcendentals=0,
        ),
        name="project",
    )(place, up_q, up_v, *x_arrays, *w_arrays)

    offset, condition, sources = gathered["last"] or (None, None, [])
    plan["last"] = None if offset is None else (offset, condition)
    return pl.pallas_call(
        functools.partial(attend_kernel, plan),
        out_shape=[
            jax.ShapeDtypeStruct((parts, 2 * rank, feats // parts), jnp.bfloat16),
            jax.ShapeDtypeStruct((rank, (heads + 1) * HEAD_SIZE), jnp.float32),
        ],
        in_specs=[SMEM, VMEM, VMEM]
        + [ANY] * (1 + len(x_arrays) + len(g_arrays))
        + [ANY, VMEM][: len(sources)],
        out_specs=[VMEM] * 2,
        scratch_shapes=[
            pltpu.VMEM((tokens, feats + LANES), jnp.bfloat16),
            pltpu.VMEM((tokens, heads * HEAD_SIZE), jnp.bfloat16),
            pltpu.VMEM((depth, wide) if sources else (16, LANES), jnp.bfloat16),
            pltpu.VMEM((tokens, wide), jnp.float32),
            pltpu.VMEM((3 * rank, tokens), jnp.bfloat16),
            pltpu.SemaphoreType.DMA((1 + tokens // seq + len(x_arrays) + len(g_arrays),)),
        ],
        compiler_params=params,
        name="attend",
    )(place, up_q, up_v, base, *x_arrays, *g_arrays, *sources)


def sum_kernel(gas, gb, out):
    total = gas[0].astype(jnp.float32)
    for index in range(1, gas.shape[0]):
        total = total + gas[index].astype(jnp.float32)
    rows = total.shape[0]
    out[:rows] = total.astype(out.dtype)
    out[rows:] = gb[...].astype(out.dtype)


def sum_pieces(gas, gb):
    _, rows, wide = gas.shape
    return pl.pallas_call(
        sum_kernel,
        out_shape=jax.ShapeDtypeStruct((rows + gb.shape[0], wide), jnp.bfloat16),
        in_specs=[VMEM] * 2,
        out_specs=VMEM,
        name="sum_pieces",
    )(gas, gb)


def scale_kernel(coefficient, *refs):
    total = refs[0][...].astype(jnp.float32)
    for ref in refs[1:-1]:
        total = total + ref[...].astype(jnp.float32)
    refs[-1][...] = (total * coefficient).astype(refs[-1].dtype)


def scale_sum(pieces, coefficient):
    return pl.pallas_call(
        functools.partial(scale_kernel, coefficient),
        out_shape=jax.ShapeDtypeStruct(pieces[0].shape, jnp.bfloat16),
        in_specs=[VMEM] * len(pieces),
        out_specs=VMEM,
        name="scale_sum",
    )(*pieces)


def spread_kernel(rank, group, place, *refs):
    pieces, (aq, bq, av, bv) = refs[:-4], refs[-4:]
    wide = pieces[0].shape[1]
    for step, ref in enumerate(pieces):
        mine = place[0] ^ step
        value = ref[...].astype(jnp.float32)
        at = pl.ds(pl.multiple_of(mine * wide, LANES), wide)
        aq[:, at] = value[:rank]
        av[:, at] = value[rank : 2 * rank]
        bq[:, pl.ds(pl.multiple_of(mine * group, LANES), group)] = value[2 * rank :, :group]
        bv[:, pl.ds(pl.multiple_of(mine * HEAD_SIZE, LANES), HEAD_SIZE)] = value[2 * rank :, group:]


def spread(place, pieces, rank, group, shapes):
    return pl.pallas_call(
        functools.partial(spread_kernel, rank, group),
        out_shape=[jax.ShapeDtypeStruct(shape, jnp.float32) for shape in shapes],
        in_specs=[SMEM] + [VMEM] * len(pieces),
        out_specs=[VMEM] * 4,
        name="spread",
    )(place, *pieces)


def outer_pairs(value):
    return lax.ppermute(value, "z", [(0, 1), (1, 0), (2, 3), (3, 2)])


def inner_pairs(value):
    return lax.ppermute(value, "z", [(0, 0), (1, 2), (2, 1), (3, 3)])


def is_inner(p):
    return (p[1] == 1) | (p[1] == 2)


def is_outer(p):
    return (p[1] == 0) | (p[1] == 3)


def paired_gather(place, qw, kw, vw, heads, norm_args, gradient):
    shard, rows = qw.shape[0], norm_args[0].shape[0]
    packed = pack_weights(place, qw, kw, vw, heads)
    own = lax.all_to_all(packed, ("y", "c"), 0, 0, tiled=True).reshape(4 * shard, -1)
    normed = norm_tokens(*norm_args, packed)

    c_tokens = swapped(normed, ("c",), 1)
    x_tokens = swapped(normed, ("ctx",), 1)
    (later,) = fence((norm_tokens(*norm_args, normed),), own, c_tokens)
    y_tokens = swapped(later, ("y",), 1)
    hop_2, hop_1 = inner_pairs(own), outer_pairs(own)
    xc_tokens, xy_tokens = swapped(x_tokens, ("c",), 1), swapped(x_tokens, ("y",), 1)

    hop_4, hop_3 = inner_pairs(hop_1), outer_pairs(hop_2)
    (gradient,) = fence((gradient,), hop_1, xc_tokens)
    gradient = lax.all_to_all(gradient, GROUP, 0, 0, tiled=True)
    yc_tokens = swapped(y_tokens, ("c",), 1)

    hop_5 = outer_pairs(hop_4)
    (xy_tokens,) = fence((xy_tokens,), hop_3, hop_4, yc_tokens)
    xyc_tokens = swapped(xy_tokens, ("c",), 1)

    def weight_columns(back):
        return lambda p: (p[1] ^ back) * 4 * shard

    def token_rows(step):
        return lambda p: (step & 3) * 2 * rows + ((p[0] >> 2) ^ (step >> 2)) * rows

    def source(step):
        return lambda p: p[0] ^ step

    tokens = (normed, c_tokens, y_tokens, yc_tokens, x_tokens, xc_tokens, xy_tokens, xyc_tokens)
    return {
        "w": [
            (weight_columns(0), None, [own]),
            (weight_columns(1), None, [hop_1]),
            (weight_columns(2), is_inner, [hop_4, hop_3]),
        ],
        "last": (weight_columns(3), is_inner, [hop_2, hop_5]),
        "x": [((token_rows(step), step & 3, None), value) for step, value in enumerate(tokens)],
        "g": [((token_rows(step), step & 3, source(step)), gradient) for step in range(8)],
    }


def on_device(
    tokens,
    trace_index,
    input_norm_scale,
    query_weight,
    key_weight,
    value_weight,
    query_down_weight,
    query_up_weight,
    value_down_weight,
    value_up_weight,
    output_gradient,
):
    rows, feats = tokens.shape[1:]
    heads_kv = key_weight.shape[1] // HEAD_SIZE
    heads = query_weight.shape[1] // HEAD_SIZE // heads_kv
    group = heads * HEAD_SIZE
    rank = query_up_weight.shape[0]
    sizes = [lax.axis_size(axis) for axis in GROUP]
    parts = math.prod(sizes)
    shards = lax.axis_size("z")
    paired = sizes == [2, 2, 2] and shards == 4
    mine = lax.axis_index(GROUP)
    place = jnp.stack([mine, lax.axis_index("z")]).astype(jnp.int32)

    norm_args = (
        tokens.reshape(rows, feats),
        trace_index.reshape(1, rows),
        input_norm_scale,
        query_down_weight.T,
        value_down_weight.T,
    )
    gradient = jnp.moveaxis(output_gradient.reshape(rows, parts, group), 1, 0)
    if paired:
        gathered = paired_gather(
            place, query_weight, key_weight, value_weight, heads, norm_args, gradient
        )
    else:
        shard = query_weight.shape[0]
        split = [w.reshape(shard, parts, -1) for w in (query_weight, key_weight, value_weight)]
        columns = jnp.moveaxis(jnp.concatenate(split, -1), 1, 0)
        per = parts // sizes[0]
        columns = lax.dynamic_slice_in_dim(columns, lax.axis_index("ctx") * per, per, 0)
        columns = lax.all_to_all(columns, ("y", "c"), 0, 0, tiled=True).reshape(per * shard, -1)
        weights = lax.all_gather(columns, "z", axis=0, tiled=True)
        normed = lax.all_gather(norm_tokens(*norm_args), ("y", "c", "ctx"), axis=0, tiled=True)
        gradient = lax.all_to_all(gradient, GROUP, 0, 0, tiled=True)
        gradient = gradient.reshape(sizes[0], per, rows, group)
        gradient = jnp.moveaxis(gradient, 0, 1).reshape(parts * rows, group)
        gathered = {
            "w": [(lambda p: 0, None, [weights])],
            "last": None,
            "x": [((lambda p: 0, 0, None), normed)],
            "g": [((lambda p: 0, 0, None), gradient)],
        }

    plan = {
        "feats": feats,
        "heads": heads,
        "seq": sizes[0] * rows,
        "window": 2 * rows,
        "tokens": parts * rows,
        "parts": parts,
    }
    ga, gb = attend(place, query_up_weight, value_up_weight, gathered, plan)

    coefficient = ADAPTER_NAME / math.sqrt(parts * shards * rows)
    mixed = sum_pieces(lax.all_to_all(ga, GROUP, 0, 0, tiled=True), gb)
    if shards & (shards - 1) == 0 and shards <= 4:
        mixed = [mixed] + [swapped(mixed, ("z",), step) for step in range(1, shards)]
    else:
        mixed = [lax.psum(mixed.astype(jnp.float32), "z")]
    scaled = scale_sum(mixed, coefficient)
    scaled = [scaled] + [swapped(scaled, GROUP, step) for step in range(1, parts)]
    shapes = ((rank, feats), (rank, heads_kv * group), (rank, feats), (rank, heads_kv * HEAD_SIZE))
    aq, bq, av, bv = spread(place, scaled, rank, group, shapes)
    return aq.T, bq, av.T, bv


def solution(mesh):
    groups, ctx, fsdp = (mesh.shape[name] for name in ("groups", "ctx", "fsdp"))

    def run(*args):
        heads_kv = args[4].shape[1] // HEAD_SIZE
        share = heads_kv // ctx
        cores = 2 if share % 2 == 0 else 1
        split = (groups, ctx, fsdp // share, share // cores, cores)
        finer = Mesh(mesh.devices.reshape(split), ("groups", "ctx", "z", "y", "c"))
        whole = ("z", "y", "c")
        sequences = ("groups",) + whole
        by_rows = P(whole, None)
        by_tokens = P(sequences, "ctx", None)
        out = P("groups", None)
        return jax.shard_map(
            on_device,
            mesh=finer,
            in_specs=(
                by_tokens, P(sequences, "ctx"), P(), by_rows, by_rows, by_rows, P(), P(), P(), P(), by_tokens
            ),
            out_specs=(out, out, out, out),
            check_vma=False,
        )(*args)

    return run
```

```python
import functools
import math

import jax
import jax.numpy as jnp
from jax import lax
from jax.experimental import pallas as pl
from jax.experimental.pallas import tpu as pltpu
from jax.sharding import Mesh
from jax.sharding import PartitionSpec as P

HEAD_SIZE = 128
LANES = 128

CAP = 50.0
QSCALE = 1.0 / 12.0
ADAPTER_NAME = 0.5
EPS = 1e-06

GROUP = ("ctx", "y", "c")
ANY = pl.BlockSpec(memory_space=pl.ANY)
VMEM = pl.BlockSpec(memory_space=pltpu.VMEM)
SMEM = pl.BlockSpec(memory_space=pltpu.SMEM)
PARAMS = pltpu.CompilerParams(vmem_limit_bytes=60 * 2**20)

NT = (((1,), (1,)), ((), ()))
TN = (((0,), (0,)), ((), ()))


def dot(a, b, dims=(((1,), (0,)), ((), ()))):
    return lax.dot_general(a, b, dims, preferred_element_type=jnp.float32)


def swapped(value, axes, distance):
    count = 1
    for axis in axes:
        count *= lax.axis_size(axis)
    return lax.ppermute(value, axes, [(i, i ^ distance) for i in range(count)])


def pack_weights_kernel(heads, qw, kw, vw, *outs):
    group = heads * HEAD_SIZE
    for core, out in enumerate(outs):
        for chip in range(out.shape[0]):
            mine = lax.axis_index(GROUP) ^ (2 * chip + core)
            for src, at, wide in ((qw, 0, group), (kw, group, HEAD_SIZE), (vw, group + HEAD_SIZE, HEAD_SIZE)):
                out[chip, :, at : at + wide] = src[:, pl.ds(pl.multiple_of(mine * wide, wide), wide)]


def pack_weights(qw, kw, vw, heads):
    shape = (2, qw.shape[0], (heads + 2) * HEAD_SIZE)
    return pl.pallas_call(
        functools.partial(pack_weights_kernel, heads),
        out_shape=[jax.ShapeDtypeStruct(shape, qw.dtype)] * 2,
        in_specs=[VMEM] * 3,
        out_specs=[VMEM] * 2,
        compiler_params=PARAMS,
        name="pack_weights",
    )(qw, kw, vw)


def join_rows_kernel(place, kept, got, near, far):
    rows = kept.shape[1]
    core = place[0] & 1
    for chip, out in enumerate((near, far)):
        out[pl.ds(pl.multiple_of(core * rows, 16), rows), :] = kept[chip]
        out[pl.ds(pl.multiple_of((1 - core) * rows, 16), rows), :] = got[chip]


def join_rows(place, kept, got):
    _, rows, wide = kept.shape
    return pl.pallas_call(
        join_rows_kernel,
        out_shape=[jax.ShapeDtypeStruct((2 * rows, wide), kept.dtype)] * 2,
        in_specs=[SMEM, VMEM, VMEM],
        out_specs=[VMEM] * 2,
        compiler_params=PARAMS,
        name="join_rows",
    )(place, kept, got)


def join_pairs_kernel(*refs):
    count = len(refs) // 3
    for first, second, out in zip(refs[:count], refs[count : 2 * count], refs[2 * count :]):
        rows = first.shape[0]
        out[:rows] = first[...]
        out[rows:] = second[...]


def join_pairs(first, second):
    rows, wide = first[0].shape
    return pl.pallas_call(
        join_pairs_kernel,
        out_shape=[jax.ShapeDtypeStruct((2 * rows, wide), first[0].dtype)] * len(first),
        in_specs=[VMEM] * (2 * len(first)),
        out_specs=[VMEM] * len(first),
        compiler_params=PARAMS,
        name="join_pairs",
    )(*first, *second)


def fence_kernel(*refs):
    pass


def fence(values, *earlier):
    count = len(values)
    return pl.pallas_call(
        fence_kernel,
        out_shape=[jax.ShapeDtypeStruct(value.shape, value.dtype) for value in values],
        in_specs=[ANY] * (count + len(earlier)),
        out_specs=[ANY] * count,
        input_output_aliases={i: i for i in range(count)},
        compiler_params=PARAMS,
        name="fence",
    )(*values, *earlier)


def norm_kernel(copies, tokens, trace, gain, down_q, down_v, *rest):
    flt = tokens[...].astype(jnp.float32)
    meansq = jnp.mean(flt * flt, axis=-1, keepdims=True)
    normed = (flt * lax.rsqrt(meansq + EPS) * gain[...].astype(jnp.float32)[None, :]).astype(jnp.bfloat16)
    rows, feats = normed.shape
    rank = down_q.shape[0]
    low_q = dot(normed, down_q[...], NT)
    low_v = dot(normed, down_v[...], NT)
    square = (rows, rows)
    diagonal = lax.broadcasted_iota(jnp.int32, square, 0) == lax.broadcasted_iota(jnp.int32, square, 1)
    ids = jnp.sum(jnp.where(diagonal, trace[...].astype(jnp.float32), 0.0), axis=1, keepdims=True)
    filler = jnp.zeros((rows, LANES - 2 * rank - 1), jnp.float32)
    extra = jnp.concatenate([low_q, low_v, ids, filler], 1).astype(jnp.bfloat16)
    for out in rest[-copies:]:
        out[:, :feats] = normed
        out[:, feats:] = extra


def norm_tokens(tokens, trace, gain, down_q, down_v, copies, *earlier):
    rows, feats = tokens.shape
    return pl.pallas_call(
        functools.partial(norm_kernel, copies),
        out_shape=[jax.ShapeDtypeStruct((rows, feats + LANES), jnp.bfloat16)] * copies,
        in_specs=[VMEM] * 5 + [ANY] * len(earlier),
        out_specs=[VMEM] * copies,
        compiler_params=pltpu.CompilerParams(vmem_limit_bytes=16 * 2**20),
        name="norm_tokens",
    )(tokens, trace, gain, down_q, down_v, *earlier)


class Loads:
    def __init__(self, sems):
        self.sems, self.count, self.waits = sems, 0, []

    def add(self, place, pieces, target):
        for piece, src in pieces:
            offset, sequence, choice = piece
            begin = pl.multiple_of(offset(place), 16)
            rows = src.shape[-2]
            if choice is not None and len(src.shape) == 3:
                src = src.at[choice(place)]
            copy = pltpu.make_async_copy(src, target.at[pl.ds(begin, rows), :], self.sems.at[self.count])
            copy.start()
            self.waits.append((sequence, copy))
            self.count += 1

    def add_shard(self, place, condition, sources, target, at):
        copies = []
        for chunks in sources:
            some = []
            for number, (src, part, offset) in enumerate(chunks):
                begin = pl.multiple_of(at + offset(place), 16)
                src = src.at[part]
                to = target.at[pl.ds(begin, src.shape[0]), :]
                some.append(pltpu.make_async_copy(src, to, self.sems.at[self.count + number]))
            copies.append(some)
        for number, copy in enumerate(copies[0]):
            if condition is None:
                copy.start()
            else:
                pl.when(condition)(copy.start)
                pl.when(jnp.logical_not(condition))(copies[1][number].start)
            self.waits.append((0, copy))
            self.count += 1

    def wait(self, sequence):
        for needed, copy in self.waits:
            if needed == sequence:
                copy.wait()


def project_kernel(plan, *refs):
    n_x, shards = len(plan["x"]), plan["shards"]
    place, up_q, up_v = refs[:3]
    x_refs, w_refs, rest = refs[3 : 3 + n_x], refs[3 + n_x : -4], refs[-4:]
    out, x_all, w_all, sems = rest
    feats, heads, seq = plan["feats"], plan["heads"], plan["seq"]
    rank, group = up_q.shape[0], heads * HEAD_SIZE
    depth = plan["depth"]

    loads = Loads(sems)
    for index, (_, condition, sources) in enumerate(shards):
        chosen = None if condition is None else condition(place)
        sources = [[(w_refs[at], part, offset) for at, part, offset in chunks] for chunks in sources]
        loads.add_shard(place, chosen, sources, w_all, index * depth)
    loads.add(place, list(zip(plan["x"], x_refs)), x_all)

    mine = place[0]
    uq = up_q[:, pl.ds(pl.multiple_of(mine * group, group), group)]
    uv = up_v[:, pl.ds(pl.multiple_of(mine * HEAD_SIZE, HEAD_SIZE), HEAD_SIZE)]
    zero = functools.partial(jnp.zeros, dtype=jnp.float32)
    top = jnp.concatenate([ADAPTER_NAME * uq.astype(jnp.float32), zero((rank, 2 * HEAD_SIZE))], 1)
    low = jnp.concatenate([zero((rank, group + HEAD_SIZE)), ADAPTER_NAME * uv.astype(jnp.float32)], 1)
    pad = zero((LANES - 2 * rank, group + 2 * HEAD_SIZE))
    ups = jnp.concatenate([top, low, pad], 0).astype(jnp.bfloat16)

    for index in range(x_all.shape[0] // seq):
        loads.wait(index)
        rows = pl.ds(index * seq, seq)
        total = dot(x_all[rows, feats:], ups)
        for number, (offset, _, _) in enumerate(shards):
            columns = pl.ds(pl.multiple_of(offset(place), LANES), depth)
            total = total + dot(x_all[rows, columns], w_all[number * depth : (number + 1) * depth])
        out[rows, :] = total


def attend_kernel(plan, *refs):
    n_x, n_g, last = len(plan["x"]), len(plan["g"]), plan["last"]
    place, up_q, up_v, base = refs[:4]
    x_refs, g_refs = refs[4 : 4 + n_x], refs[4 + n_x : 4 + n_x + n_g]
    w_refs, rest = refs[4 + n_x + n_g : -8], refs[-8:]
    ga_out, gb_out, x_all, g_all, w_all, base_all, pulls, sems = rest

    feats, heads, seq, window, depth = (plan[k] for k in ("feats", "heads", "seq", "window", "depth"))
    rank, parts = up_q.shape[0], plan["parts"]
    group = heads * HEAD_SIZE
    tokens = x_all.shape[0]
    sequences = tokens // seq

    loads = Loads(sems)
    if last is not None:
        offset, condition, chunks = last
        inner = condition(place)
        here = []
        for part, chunk_offset in chunks:
            src = w_refs[0].at[part]
            to = w_all.at[pl.ds(pl.multiple_of(chunk_offset(place), 16), src.shape[0]), :]
            here.append(pltpu.make_async_copy(src, to, sems.at[loads.count]))
            pl.when(inner)(here[-1].start)
            loads.count += 1
    for index in range(sequences):
        rows = pl.ds(index * seq, seq)
        copy_base = pltpu.make_async_copy(base.at[rows, :], base_all.at[rows, :], sems.at[loads.count])
        copy_base.start()
        loads.waits.append((index, copy_base))
        loads.count += 1
        for pieces, sources, target in ((plan["x"], x_refs, x_all), (plan["g"], g_refs, g_all)):
            chosen = [(piece, src) for piece, src in zip(pieces, sources) if piece[1] == index]
            loads.add(place, chosen, target)
    if last is not None:

        @pl.when(jnp.logical_not(inner))
        def _():
            for part, chunk_offset in chunks:
                value = w_refs[1][part, :]
                w_all[pl.ds(pl.multiple_of(chunk_offset(place), 16), value.shape[0]), :] = value

        for copy in here:
            pl.when(inner)(copy.wait)

    mine = place[0]
    uq = up_q[:, pl.ds(pl.multiple_of(mine * group, group), group)]
    uv = up_v[:, pl.ds(pl.multiple_of(mine * HEAD_SIZE, HEAD_SIZE), HEAD_SIZE)]
    id_row = jnp.where(lax.broadcasted_iota(jnp.int32, (8, LANES), 1) == 2 * rank, 1.0, 0.0).astype(jnp.bfloat16)
    span = min(seq, window)
    blocks = seq // span
    sums = jnp.zeros((LANES, group + 2 * HEAD_SIZE), jnp.float32)

    for index in range(sequences):
        loads.wait(index)
        rows = pl.ds(index * seq, seq)
        qkv = base_all[rows, :]
        if last is not None:
            columns = pl.ds(pl.multiple_of(offset(place), LANES), depth)
            qkv = qkv + dot(x_all[rows, columns], w_all[...])
        qkv = qkv.astype(jnp.bfloat16)
        extra = x_all[rows, feats:]
        ids_key = dot(id_row, extra, NT)[:1]
        ids_query = extra[:, 2 * rank : 2 * rank + 1].astype(jnp.float32)
        keys = qkv[:, group : group + HEAD_SIZE]
        values = qkv[:, group + HEAD_SIZE :]
        grads = g_all[rows, :]
        dq_parts = [[] for _ in range(heads)]
        dv_parts = [None] * blocks
        for block in range(blocks):
            lo, hi = block * span, (block + 1) * span
            back = max(0, lo - span)
            kb, vb = keys[back:hi], values[back:hi]
            shape = (span, hi - back)
            pos_q = lax.broadcasted_iota(jnp.int32, shape, 0) + lo
            pos_k = lax.broadcasted_iota(jnp.int32, shape, 1) + back
            mask = (pos_k <= pos_q) & (pos_k > pos_q - window)
            mask = mask & (ids_query[lo:hi] == ids_key[:, back:hi])
            for head in range(heads):
                cols = slice(head * HEAD_SIZE, (head + 1) * HEAD_SIZE)
                q, g = qkv[lo:hi, cols], grads[lo:hi, cols]
                t = jnp.tanh(dot(q, kb, NT) * (QSCALE / CAP))
                expo = jnp.where(mask, jnp.exp(CAP * t), 0.0)
                weights = expo / jnp.sum(expo, axis=-1, keepdims=True)
                weights16 = weights.astype(jnp.bfloat16)
                dweight = dot(g, vb, NT)
                delta = jnp.sum(weights16.astype(jnp.float32) * dweight, axis=-1, keepdims=True)
                dscore = (weights * (dweight - delta) * (1.0 - t * t) * QSCALE).astype(jnp.bfloat16)
                dq_parts[head].append(dot(dscore, kb).astype(jnp.bfloat16))
                dv = dot(weights16, g, TN)
                for at in range(back // span, block + 1):
                    piece = dv[at * span - back : (at + 1) * span - back]
                    dv_parts[at] = piece if dv_parts[at] is None else dv_parts[at] + piece
        dq = jnp.concatenate([jnp.concatenate(some, 0) for some in dq_parts], 1)
        dv = jnp.concatenate(dv_parts, 0)
        dv_hi = dv.astype(jnp.bfloat16)
        dv_lo = (dv - dv_hi.astype(jnp.float32)).astype(jnp.bfloat16)
        pull_q = dot(uq, dq, NT)
        pull_v = dot(uv, dv_hi, NT) + dot(uv, dv_lo, NT)
        pull_v_hi = pull_v.astype(jnp.bfloat16)
        pull_v_lo = (pull_v - pull_v_hi.astype(jnp.float32)).astype(jnp.bfloat16)
        pulls[:, rows] = jnp.concatenate([pull_q.astype(jnp.bfloat16), pull_v_hi, pull_v_lo], 0)
        sums = sums + dot(extra, jnp.concatenate([dq, dv_hi, dv_lo], 1), TN)

    gb_out[:, :group] = sums[:rank, :group]
    gb_out[:, group:] = sums[rank : 2 * rank, group : group + HEAD_SIZE] + sums[rank : 2 * rank, group + HEAD_SIZE :]
    part = feats // parts
    for index in range(parts):
        piece = dot(pulls[...], x_all[:, index * part : (index + 1) * part])
        ga_out[index, :rank] = piece[:rank].astype(ga_out.dtype)
        ga_out[index, rank:] = (piece[rank : 2 * rank] + piece[2 * rank :]).astype(ga_out.dtype)


def attend(place, up_q, up_v, gathered, plan):
    feats, heads, tokens, parts, seq = (plan[k] for k in ("feats", "heads", "tokens", "parts", "seq"))
    rank = up_q.shape[0]
    wide = (heads + 2) * HEAD_SIZE
    x_plan, x_arrays = zip(*gathered["x"])
    g_plan, g_arrays = zip(*gathered["g"])
    w_arrays, shards = [], []
    for offset, condition, sources in gathered["w"]:
        shards.append((offset, condition, []))
        for chunks in sources:
            shards[-1][2].append([])
            for array, part, at in chunks:
                index = next((i for i, known in enumerate(w_arrays) if known is array), len(w_arrays))
                w_arrays += [array] if index == len(w_arrays) else []
                shards[-1][2][-1].append((index, part, at))
    depth = w_arrays[-1].shape[0]
    plan = dict(plan, x=x_plan, g=g_plan, shards=shards, depth=depth)
    base = pl.pallas_call(
        functools.partial(project_kernel, plan),
        out_shape=jax.ShapeDtypeStruct((tokens, wide), jnp.float32),
        in_specs=[SMEM, VMEM, VMEM] + [ANY] * (len(x_arrays) + len(w_arrays)),
        out_specs=VMEM,
        scratch_shapes=[
            pltpu.VMEM((tokens, feats + LANES), jnp.bfloat16),
            pltpu.VMEM((len(shards) * depth, wide), jnp.bfloat16),
            pltpu.SemaphoreType.DMA((len(x_arrays) + sum(len(sources[0]) for _, _, sources in shards),)),
        ],
        cost_estimate=pl.CostEstimate(
            flops=2 * tokens * len(shards) * depth * wide,
            bytes_accessed=2 * tokens * feats + 2 * len(shards) * depth * wide + 4 * tokens * wide,
            transcendentals=0,
        ),
        compiler_params=PARAMS,
        name="project",
    )(place, up_q, up_v, *x_arrays, *w_arrays)

    offset, condition, sources = gathered["last"] or (None, None, [])
    plan["last"] = None if offset is None else (offset, condition, [chunk[1:] for chunk in sources[0]])
    last = [chunks[0][0] for chunks in sources]
    return pl.pallas_call(
        functools.partial(attend_kernel, plan),
        out_shape=[
            jax.ShapeDtypeStruct((parts, 2 * rank, feats // parts), jnp.bfloat16),
            jax.ShapeDtypeStruct((rank, (heads + 1) * HEAD_SIZE), jnp.float32),
        ],
        in_specs=[SMEM, VMEM, VMEM]
        + [ANY] * (1 + len(x_arrays) + len(g_arrays))
        + [ANY, VMEM][: len(last)],
        out_specs=[VMEM] * 2,
        scratch_shapes=[
            pltpu.VMEM((tokens, feats + LANES), jnp.bfloat16),
            pltpu.VMEM((tokens, heads * HEAD_SIZE), jnp.bfloat16),
            pltpu.VMEM((depth, wide) if last else (16, LANES), jnp.bfloat16),
            pltpu.VMEM((tokens, wide), jnp.float32),
            pltpu.VMEM((3 * rank, tokens), jnp.bfloat16),
            pltpu.SemaphoreType.DMA((len(last) + tokens // seq + len(x_arrays) + len(g_arrays),)),
        ],
        compiler_params=PARAMS,
        name="attend",
    )(place, up_q, up_v, base, *x_arrays, *g_arrays, *last)


def sum_kernel(gas, gb, out):
    total = gas[0].astype(jnp.float32)
    for index in range(1, gas.shape[0]):
        total = total + gas[index].astype(jnp.float32)
    rows = total.shape[0]
    out[:rows] = total.astype(out.dtype)
    out[rows:] = gb[...].astype(out.dtype)


def sum_pieces(gas, gb):
    _, rows, wide = gas.shape
    return pl.pallas_call(
        sum_kernel,
        out_shape=jax.ShapeDtypeStruct((rows + gb.shape[0], wide), jnp.bfloat16),
        in_specs=[VMEM] * 2,
        out_specs=VMEM,
        compiler_params=PARAMS,
        name="sum_pieces",
    )(gas, gb)


def scale_kernel(coefficient, *refs):
    total = refs[0][...].astype(jnp.float32)
    for ref in refs[1:-1]:
        total = total + ref[...].astype(jnp.float32)
    refs[-1][...] = (total * coefficient).astype(refs[-1].dtype)


def scale_sum(pieces, coefficient):
    return pl.pallas_call(
        functools.partial(scale_kernel, coefficient),
        out_shape=jax.ShapeDtypeStruct(pieces[0].shape, jnp.bfloat16),
        in_specs=[VMEM] * len(pieces),
        out_specs=VMEM,
        compiler_params=PARAMS,
        name="scale_sum",
    )(*pieces)


def spread_kernel(rank, group, place, *refs):
    pieces, (aq, bq, av, bv) = refs[:-4], refs[-4:]
    wide = pieces[0].shape[1]
    for step, ref in enumerate(pieces):
        mine = place[0] ^ step
        value = ref[...].astype(jnp.float32)
        at = pl.ds(pl.multiple_of(mine * wide, LANES), wide)
        aq[:, at] = value[:rank]
        av[:, at] = value[rank : 2 * rank]
        bq[:, pl.ds(pl.multiple_of(mine * group, LANES), group)] = value[2 * rank :, :group]
        bv[:, pl.ds(pl.multiple_of(mine * HEAD_SIZE, LANES), HEAD_SIZE)] = value[2 * rank :, group:]


def spread(place, pieces, rank, group, shapes):
    return pl.pallas_call(
        functools.partial(spread_kernel, rank, group),
        out_shape=[jax.ShapeDtypeStruct(shape, jnp.float32) for shape in shapes],
        in_specs=[SMEM] + [VMEM] * len(pieces),
        out_specs=[VMEM] * 4,
        compiler_params=PARAMS,
        name="spread",
    )(place, *pieces)


def outer_pairs(value):
    return lax.ppermute(value, "z", [(0, 1), (1, 0), (2, 3), (3, 2)])


def inner_pairs(value):
    return lax.ppermute(value, "z", [(0, 0), (1, 2), (2, 1), (3, 3)])


def is_inner(p):
    return (p[1] == 1) | (p[1] == 2)


def is_outer(p):
    return (p[1] == 0) | (p[1] == 3)


def paired_gather(place, qw, kw, vw, heads, norm_args, gradient):
    shard, rows = qw.shape[0], norm_args[0].shape[0]
    kept, given = pack_weights(qw, kw, vw, heads)
    near, beside = join_rows(place, kept, swapped(given, ("c",), 1))
    far = swapped(beside, ("y",), 1)
    normed, later = norm_tokens(*norm_args, 2, beside)
    c_tokens, x_tokens = swapped(normed, ("c",), 1), swapped(normed, ("ctx",), 1)
    hop_1, hop_2 = outer_pairs(near), inner_pairs(near)
    (later,) = fence((later,), far, hop_1, hop_2)
    y_tokens = swapped(later, ("y",), 1)
    hop_1, hop_2 = join_pairs((hop_1, hop_2), (outer_pairs(far), inner_pairs(far)))

    hop_4, hop_3 = inner_pairs(hop_1), outer_pairs(hop_2)
    half = rows // 2
    far_low, far_high = swapped(x_tokens[:half], ("y",), 1), swapped(y_tokens[half:], ("ctx",), 1)
    xc_tokens = swapped(x_tokens, ("c",), 1)
    (gradient,) = fence((gradient,), hop_1, xc_tokens)
    gradient = lax.all_to_all(gradient, GROUP, 0, 0, tiled=True)

    (hop_4,) = fence((hop_4,), hop_3)
    hop_5 = outer_pairs(hop_4)
    y_tokens, far_low, far_high = fence((y_tokens, far_low, far_high), hop_4)
    yc_tokens, farc_low, farc_high = (swapped(value, ("c",), 1) for value in (y_tokens, far_low, far_high))

    def weight_columns(back):
        return lambda p: (p[1] ^ back) * 4 * shard

    def token_rows(step, skip=0):
        return lambda p: (step & 3) * 2 * rows + ((p[0] >> 2) ^ (step >> 2)) * rows + skip

    def source(step):
        return lambda p: p[0] ^ step

    size = 2 * shard

    def ordered(value, other=None):
        def own_chip(p):
            return ((p[0] >> 1) & 1) * size

        def chip_beside(p):
            return (1 - ((p[0] >> 1) & 1)) * size

        if other is not None:
            return [(value, slice(0, size), own_chip), (other, slice(0, size), chip_beside)]
        return [(value, slice(0, size), own_chip), (value, slice(size, 2 * size), chip_beside)]

    pieces = [(0, 0, normed), (1, 0, c_tokens), (2, 0, y_tokens), (3, 0, yc_tokens), (4, 0, x_tokens)]
    pieces += [(5, 0, xc_tokens), (6, 0, far_low), (6, half, far_high), (7, 0, farc_low), (7, half, farc_high)]
    return {
        "w": [
            (weight_columns(0), None, [ordered(near, far)]),
            (weight_columns(1), None, [ordered(hop_1)]),
            (weight_columns(2), is_inner, [ordered(hop_4), ordered(hop_3)]),
        ],
        "last": (weight_columns(3), is_inner, [ordered(hop_2), ordered(hop_5)]),
        "x": [((token_rows(step, skip), step & 3, None), value) for step, skip, value in pieces],
        "g": [((token_rows(step), step & 3, source(step)), gradient) for step in range(8)],
    }


def on_device(
    tokens,
    trace_index,
    input_norm_scale,
    query_weight,
    key_weight,
    value_weight,
    query_down_weight,
    query_up_weight,
    value_down_weight,
    value_up_weight,
    output_gradient,
):
    rows, feats = tokens.shape[1:]
    heads_kv = key_weight.shape[1] // HEAD_SIZE
    heads = query_weight.shape[1] // HEAD_SIZE // heads_kv
    group = heads * HEAD_SIZE
    rank = query_up_weight.shape[0]
    sizes = [lax.axis_size(axis) for axis in GROUP]
    parts = math.prod(sizes)
    shards = lax.axis_size("z")
    paired = sizes == [2, 2, 2] and shards == 4
    mine = lax.axis_index(GROUP)
    place = jnp.stack([mine, lax.axis_index("z")]).astype(jnp.int32)

    norm_args = (
        tokens.reshape(rows, feats),
        trace_index.reshape(1, rows),
        input_norm_scale,
        query_down_weight.T,
        value_down_weight.T,
    )
    gradient = jnp.moveaxis(output_gradient.reshape(rows, parts, group), 1, 0)
    if paired:
        gathered = paired_gather(
            place, query_weight, key_weight, value_weight, heads, norm_args, gradient
        )
    else:
        shard = query_weight.shape[0]
        split = [w.reshape(shard, parts, -1) for w in (query_weight, key_weight, value_weight)]
        columns = jnp.moveaxis(jnp.concatenate(split, -1), 1, 0)
        per = parts // sizes[0]
        columns = lax.dynamic_slice_in_dim(columns, lax.axis_index("ctx") * per, per, 0)
        columns = lax.all_to_all(columns, ("y", "c"), 0, 0, tiled=True).reshape(per * shard, -1)
        weights = lax.all_gather(columns, "z", axis=0, tiled=True)
        normed = lax.all_gather(norm_tokens(*norm_args, 1)[0], ("y", "c", "ctx"), axis=0, tiled=True)
        gradient = lax.all_to_all(gradient, GROUP, 0, 0, tiled=True)
        gradient = gradient.reshape(sizes[0], per, rows, group)
        gradient = jnp.moveaxis(gradient, 0, 1).reshape(parts * rows, group)
        gathered = {
            "w": [(lambda p: 0, None, [[(weights, slice(None), lambda p: 0)]])],
            "last": None,
            "x": [((lambda p: 0, 0, None), normed)],
            "g": [((lambda p: 0, 0, None), gradient)],
        }

    plan = {
        "feats": feats,
        "heads": heads,
        "seq": sizes[0] * rows,
        "window": 2 * rows,
        "tokens": parts * rows,
        "parts": parts,
    }
    ga, gb = attend(place, query_up_weight, value_up_weight, gathered, plan)

    coefficient = ADAPTER_NAME / math.sqrt(parts * shards * rows)
    mixed = sum_pieces(lax.all_to_all(ga, GROUP, 0, 0, tiled=True), gb)
    if shards & (shards - 1) == 0 and shards <= 4:
        mixed = [mixed] + [swapped(mixed, ("z",), step) for step in range(1, shards)]
    else:
        mixed = [lax.psum(mixed.astype(jnp.float32), "z")]
    scaled = scale_sum(mixed, coefficient)
    scaled = [scaled] + [swapped(scaled, GROUP, step) for step in range(1, parts)]
    shapes = ((rank, feats), (rank, heads_kv * group), (rank, feats), (rank, heads_kv * HEAD_SIZE))
    aq, bq, av, bv = spread(place, scaled, rank, group, shapes)
    return aq.T, bq, av.T, bv


def solution(mesh):
    groups, ctx, fsdp = (mesh.shape[name] for name in ("groups", "ctx", "fsdp"))

    def run(*args):
        heads_kv = args[4].shape[1] // HEAD_SIZE
        share = heads_kv // ctx
        cores = 2 if share % 2 == 0 else 1
        split = (groups, ctx, fsdp // share, share // cores, cores)
        finer = Mesh(mesh.devices.reshape(split), ("groups", "ctx", "z", "y", "c"))
        whole = ("z", "y", "c")
        sequences = ("groups",) + whole
        by_rows = P(whole, None)
        by_tokens = P(sequences, "ctx", None)
        out = P("groups", None)
        return jax.shard_map(
            on_device,
            mesh=finer,
            in_specs=(
                by_tokens, P(sequences, "ctx"), P(), by_rows, by_rows, by_rows, P(), P(), P(), P(), by_tokens
            ),
            out_specs=(out, out, out, out),
            check_vma=False,
        )(*args)

    return run
```

```python
import functools
import math

import jax
import jax.numpy as jnp
from jax import lax
from jax.experimental import pallas as pl
from jax.experimental.pallas import tpu as pltpu
from jax.sharding import Mesh
from jax.sharding import PartitionSpec as P

HEAD_SIZE = 128
LANES = 128

CAP = 50.0
QSCALE = 1.0 / 12.0
ADAPTER_NAME = 0.5
EPS = 1e-06

GROUP = ("ctx", "y", "c")
ANY = pl.BlockSpec(memory_space=pl.ANY)
VMEM = pl.BlockSpec(memory_space=pltpu.VMEM)
SMEM = pl.BlockSpec(memory_space=pltpu.SMEM)
PARAMS = pltpu.CompilerParams(vmem_limit_bytes=60 * 2**20)

NT = (((1,), (1,)), ((), ()))
TN = (((0,), (0,)), ((), ()))


def dot(a, b, dims=(((1,), (0,)), ((), ()))):
    return lax.dot_general(a, b, dims, preferred_element_type=jnp.float32)


def swapped(value, axes, distance):
    count = 1
    for axis in axes:
        count *= lax.axis_size(axis)
    return lax.ppermute(value, axes, [(i, i ^ distance) for i in range(count)])


def pack_weights(mine, qw, kw, vw, heads):
    def columns(owner):
        wide = heads * HEAD_SIZE
        parts = [lax.dynamic_slice_in_dim(qw, owner * wide, wide, 1)]
        parts += [lax.dynamic_slice_in_dim(w, owner * HEAD_SIZE, HEAD_SIZE, 1) for w in (kw, vw)]
        return jnp.concatenate(parts, 1)

    return [jnp.stack([columns(mine ^ (2 * chip + core)) for chip in range(2)]) for core in range(2)]


def join_rows(core, kept, got):
    first, second = jnp.where(core == 0, kept, got), jnp.where(core == 0, got, kept)
    return [jnp.concatenate([first[chip], second[chip]], 0) for chip in range(2)]


def fence_kernel(*refs):
    pass


def fence(values, *earlier):
    count = len(values)
    return pl.pallas_call(
        fence_kernel,
        out_shape=[jax.ShapeDtypeStruct(value.shape, value.dtype) for value in values],
        in_specs=[ANY] * (count + len(earlier)),
        out_specs=[ANY] * count,
        input_output_aliases={i: i for i in range(count)},
        compiler_params=PARAMS,
        name="fence",
    )(*values, *earlier)


def norm_kernel(copies, tokens, trace, gain, down_q, down_v, *rest):
    flt = tokens[...].astype(jnp.float32)
    meansq = jnp.mean(flt * flt, axis=-1, keepdims=True)
    normed = (flt * lax.rsqrt(meansq + EPS) * gain[...].astype(jnp.float32)[None, :]).astype(jnp.bfloat16)
    rows, feats = normed.shape
    rank = down_q.shape[0]
    low_q = dot(normed, down_q[...], NT)
    low_v = dot(normed, down_v[...], NT)
    square = (rows, rows)
    diagonal = lax.broadcasted_iota(jnp.int32, square, 0) == lax.broadcasted_iota(jnp.int32, square, 1)
    ids = jnp.sum(jnp.where(diagonal, trace[...].astype(jnp.float32), 0.0), axis=1, keepdims=True)
    filler = jnp.zeros((rows, LANES - 2 * rank - 1), jnp.float32)
    extra = jnp.concatenate([low_q, low_v, ids, filler], 1).astype(jnp.bfloat16)
    for out in rest[-copies:]:
        out[:, :feats] = normed
        out[:, feats:] = extra


def norm_tokens(tokens, trace, gain, down_q, down_v, copies, *earlier):
    rows, feats = tokens.shape
    return pl.pallas_call(
        functools.partial(norm_kernel, copies),
        out_shape=[jax.ShapeDtypeStruct((rows, feats + LANES), jnp.bfloat16)] * copies,
        in_specs=[VMEM] * 5 + [ANY] * len(earlier),
        out_specs=[VMEM] * copies,
        compiler_params=pltpu.CompilerParams(vmem_limit_bytes=16 * 2**20),
        name="norm_tokens",
    )(tokens, trace, gain, down_q, down_v, *earlier)


class Loads:
    def __init__(self, sems):
        self.sems, self.count, self.waits = sems, 0, []

    def add(self, place, pieces, target):
        for piece, src in pieces:
            offset, sequence, choice = piece
            begin = pl.multiple_of(offset(place), 16)
            rows = src.shape[-2]
            if choice is not None and len(src.shape) == 3:
                src = src.at[choice(place)]
            copy = pltpu.make_async_copy(src, target.at[pl.ds(begin, rows), :], self.sems.at[self.count])
            copy.start()
            self.waits.append((sequence, copy))
            self.count += 1

    def wait(self, sequence):
        for needed, copy in self.waits:
            if needed == sequence:
                copy.wait()


def project_kernel(plan, *refs):
    n_x, shards = len(plan["x"]), plan["shards"]
    place, up_q, up_v = refs[:3]
    x_refs, w_refs, rest = refs[3 : 3 + n_x], refs[3 + n_x : -4], refs[-4:]
    out, x_all, w_all, sems = rest
    feats, heads, seq = plan["feats"], plan["heads"], plan["seq"]
    rank, group = up_q.shape[0], heads * HEAD_SIZE
    depth = plan["depth"]

    loads = Loads(sems)
    for index, (_, chunks) in enumerate(shards):
        for number, part, at in chunks:
            piece = (lambda p, at=at, index=index: index * depth + at(p), 0, None)
            src = w_refs[number]
            rows = src.shape[0]
            src = src.at[slice(*part.indices(rows))]
            loads.add(place, [(piece, src)], w_all)
    loads.add(place, list(zip(plan["x"], x_refs)), x_all)

    mine = place[0]
    uq = up_q[:, pl.ds(pl.multiple_of(mine * group, group), group)]
    uv = up_v[:, pl.ds(pl.multiple_of(mine * HEAD_SIZE, HEAD_SIZE), HEAD_SIZE)]
    zero = functools.partial(jnp.zeros, dtype=jnp.float32)
    top = jnp.concatenate([ADAPTER_NAME * uq.astype(jnp.float32), zero((rank, 2 * HEAD_SIZE))], 1)
    low = jnp.concatenate([zero((rank, group + HEAD_SIZE)), ADAPTER_NAME * uv.astype(jnp.float32)], 1)
    pad = zero((LANES - 2 * rank, group + 2 * HEAD_SIZE))
    ups = jnp.concatenate([top, low, pad], 0).astype(jnp.bfloat16)

    for index in range(x_all.shape[0] // seq):
        loads.wait(index)
        rows = pl.ds(index * seq, seq)
        total = dot(x_all[rows, feats:], ups)
        for number, (offset, _) in enumerate(shards):
            columns = pl.ds(pl.multiple_of(offset(place), LANES), depth)
            total = total + dot(x_all[rows, columns], w_all[number * depth : (number + 1) * depth])
        out[rows, :] = total


def attend_kernel(plan, *refs):
    n_x, n_g, last = len(plan["x"]), len(plan["g"]), plan["last"]
    place, up_q, up_v, base = refs[:4]
    x_refs, g_refs = refs[4 : 4 + n_x], refs[4 + n_x : 4 + n_x + n_g]
    n_out = 7 + plan["cores"]
    w_refs, rest = refs[4 + n_x + n_g : -n_out], refs[-n_out:]
    ga_outs, (gb_out, x_all, g_all, w_all, base_all, pulls, sems) = rest[:-7], rest[-7:]

    feats, heads, seq, window, depth = (plan[k] for k in ("feats", "heads", "seq", "window", "depth"))
    rank, parts = up_q.shape[0], plan["parts"]
    group = heads * HEAD_SIZE
    tokens = x_all.shape[0]
    sequences = tokens // seq

    loads = Loads(sems)
    for index in range(sequences):
        rows = pl.ds(index * seq, seq)
        copy_base = pltpu.make_async_copy(base.at[rows, :], base_all.at[rows, :], sems.at[loads.count])
        copy_base.start()
        loads.waits.append((index, copy_base))
        loads.count += 1
        for pieces, sources, target in ((plan["x"], x_refs, x_all), (plan["g"], g_refs, g_all)):
            chosen = [(piece, src) for piece, src in zip(pieces, sources) if piece[1] == index]
            loads.add(place, chosen, target)
    if last is not None:
        offset, chunks = last
        for part, at in chunks:
            value = w_refs[0][part, :]
            w_all[pl.ds(pl.multiple_of(at(place), 16), value.shape[0]), :] = value

    mine = place[0]
    uq = up_q[:, pl.ds(pl.multiple_of(mine * group, group), group)]
    uv = up_v[:, pl.ds(pl.multiple_of(mine * HEAD_SIZE, HEAD_SIZE), HEAD_SIZE)]
    id_row = jnp.where(lax.broadcasted_iota(jnp.int32, (8, LANES), 1) == 2 * rank, 1.0, 0.0).astype(jnp.bfloat16)
    span = min(seq, window)
    blocks = seq // span
    sums = jnp.zeros((LANES, group + 2 * HEAD_SIZE), jnp.float32)

    for index in range(sequences):
        loads.wait(index)
        rows = pl.ds(index * seq, seq)
        qkv = base_all[rows, :]
        if last is not None:
            columns = pl.ds(pl.multiple_of(offset(place), LANES), depth)
            qkv = qkv + dot(x_all[rows, columns], w_all[...])
        qkv = qkv.astype(jnp.bfloat16)
        extra = x_all[rows, feats:]
        ids_key = dot(id_row, extra, NT)[:1]
        ids_query = extra[:, 2 * rank : 2 * rank + 1].astype(jnp.float32)
        keys = qkv[:, group : group + HEAD_SIZE]
        values = qkv[:, group + HEAD_SIZE :]
        grads = g_all[rows, :]
        dq_parts = [[] for _ in range(heads)]
        dv_parts = [None] * blocks
        for block in range(blocks):
            lo, hi = block * span, (block + 1) * span
            back = max(0, lo - span)
            kb, vb = keys[back:hi], values[back:hi]
            shape = (span, hi - back)
            pos_q = lax.broadcasted_iota(jnp.int32, shape, 0) + lo
            pos_k = lax.broadcasted_iota(jnp.int32, shape, 1) + back
            mask = (pos_k <= pos_q) & (pos_k > pos_q - window)
            mask = mask & (ids_query[lo:hi] == ids_key[:, back:hi])
            for head in range(heads):
                cols = slice(head * HEAD_SIZE, (head + 1) * HEAD_SIZE)
                q, g = qkv[lo:hi, cols], grads[lo:hi, cols]
                t = jnp.tanh(dot(q, kb, NT) * (QSCALE / CAP))
                expo = jnp.where(mask, jnp.exp(CAP * t), 0.0)
                weights = expo / jnp.sum(expo, axis=-1, keepdims=True)
                weights16 = weights.astype(jnp.bfloat16)
                dweight = dot(g, vb, NT)
                delta = jnp.sum(weights16.astype(jnp.float32) * dweight, axis=-1, keepdims=True)
                dscore = (weights * (dweight - delta) * (1.0 - t * t) * QSCALE).astype(jnp.bfloat16)
                dq_parts[head].append(dot(dscore, kb).astype(jnp.bfloat16))
                dv = dot(weights16, g, TN)
                for at in range(back // span, block + 1):
                    piece = dv[at * span - back : (at + 1) * span - back]
                    dv_parts[at] = piece if dv_parts[at] is None else dv_parts[at] + piece
        dq = jnp.concatenate([jnp.concatenate(some, 0) for some in dq_parts], 1)
        dv = jnp.concatenate(dv_parts, 0)
        dv_hi = dv.astype(jnp.bfloat16)
        dv_lo = (dv - dv_hi.astype(jnp.float32)).astype(jnp.bfloat16)
        pull_q = dot(uq, dq, NT)
        pull_v = dot(uv, dv_hi, NT) + dot(uv, dv_lo, NT)
        pull_v_hi = pull_v.astype(jnp.bfloat16)
        pull_v_lo = (pull_v - pull_v_hi.astype(jnp.float32)).astype(jnp.bfloat16)
        pulls[:, rows] = jnp.concatenate([pull_q.astype(jnp.bfloat16), pull_v_hi, pull_v_lo], 0)
        sums = sums + dot(extra, jnp.concatenate([dq, dv_hi, dv_lo], 1), TN)

    gb_out[:, :group] = sums[:rank, :group]
    gb_out[:, group:] = sums[rank : 2 * rank, group : group + HEAD_SIZE] + sums[rank : 2 * rank, group + HEAD_SIZE :]
    part = feats // parts
    for core, out in enumerate(ga_outs):
        for index in range(out.shape[0]):
            piece = dot(pulls[...], x_all[:, index * part : (index + 1) * part])
            out[index, :rank] = piece[:rank].astype(out.dtype)
            out[index, rank:] = (piece[rank : 2 * rank] + piece[2 * rank :]).astype(out.dtype)


def attend(place, up_q, up_v, gathered, plan):
    feats, heads, tokens, parts, seq = (plan[k] for k in ("feats", "heads", "tokens", "parts", "seq"))
    rank, cores = up_q.shape[0], plan["cores"]
    wide = (heads + 2) * HEAD_SIZE
    x_plan, x_arrays = zip(*gathered["x"])
    g_plan, g_arrays = zip(*gathered["g"])
    w_arrays, shards = [], []
    for offset, chunks in gathered["w"]:
        shards.append((offset, []))
        for array, part, at in chunks:
            index = next((i for i, known in enumerate(w_arrays) if known is array), len(w_arrays))
            w_arrays += [array] if index == len(w_arrays) else []
            shards[-1][1].append((index, part, at))
    depth = w_arrays[-1].shape[0]
    plan = dict(plan, x=x_plan, g=g_plan, shards=shards, depth=depth)
    base = pl.pallas_call(
        functools.partial(project_kernel, plan),
        out_shape=jax.ShapeDtypeStruct((tokens, wide), jnp.float32),
        in_specs=[SMEM, VMEM, VMEM] + [ANY] * (len(x_arrays) + len(w_arrays)),
        out_specs=VMEM,
        scratch_shapes=[
            pltpu.VMEM((tokens, feats + LANES), jnp.bfloat16),
            pltpu.VMEM((len(shards) * depth, wide), jnp.bfloat16),
            pltpu.SemaphoreType.DMA((len(x_arrays) + 2 * len(shards),)),
        ],
        cost_estimate=pl.CostEstimate(flops=0, bytes_accessed=0, transcendentals=0),
        compiler_params=PARAMS,
        name="project",
    )(place, up_q, up_v, *x_arrays, *w_arrays)

    offset, chunks = gathered["last"] or (None, [])
    plan["last"] = None if offset is None else (offset, [chunk[1:] for chunk in chunks])
    last = [chunks[0][0]] if chunks else []
    return pl.pallas_call(
        functools.partial(attend_kernel, plan),
        out_shape=[jax.ShapeDtypeStruct((parts // cores, 2 * rank, feats // parts), jnp.bfloat16)] * cores
        + [jax.ShapeDtypeStruct((rank, (heads + 1) * HEAD_SIZE), jnp.float32)],
        in_specs=[SMEM, VMEM, VMEM]
        + [ANY] * (1 + len(x_arrays) + len(g_arrays))
        + [VMEM] * len(last),
        out_specs=[VMEM] * (cores + 1),
        scratch_shapes=[
            pltpu.VMEM((tokens, feats + LANES), jnp.bfloat16),
            pltpu.VMEM((tokens, heads * HEAD_SIZE), jnp.bfloat16),
            pltpu.VMEM((depth, wide) if last else (16, LANES), jnp.bfloat16),
            pltpu.VMEM((tokens, wide), jnp.float32),
            pltpu.VMEM((3 * rank, tokens), jnp.bfloat16),
            pltpu.SemaphoreType.DMA((tokens // seq + len(x_arrays) + len(g_arrays),)),
        ],
        compiler_params=PARAMS,
        name="attend",
    )(place, up_q, up_v, base, *x_arrays, *g_arrays, *last)


def add_kernel(kept, got, *outs):
    for index, out in enumerate(outs):
        out[...] = (kept[index].astype(jnp.float32) + got[index].astype(jnp.float32)).astype(out.dtype)


def add_pieces(kept, got):
    return pl.pallas_call(
        add_kernel,
        out_shape=[jax.ShapeDtypeStruct(kept.shape[1:], kept.dtype)] * kept.shape[0],
        in_specs=[VMEM] * 2,
        out_specs=[VMEM] * kept.shape[0],
        name="add_pieces",
    )(kept, got)


def sum_kernel(gb, *refs):
    gas, out = refs[:-1], refs[-1]
    total = gas[0][...].astype(jnp.float32)
    for ref in gas[1:]:
        total = total + ref[...].astype(jnp.float32)
    rows = total.shape[0]
    out[:rows] = total.astype(out.dtype)
    out[rows:] = gb[...].astype(out.dtype)


def sum_pieces(gas, gb):
    rows, wide = gas[0].shape
    return pl.pallas_call(
        sum_kernel,
        out_shape=jax.ShapeDtypeStruct((rows + gb.shape[0], wide), jnp.bfloat16),
        in_specs=[VMEM] * (1 + len(gas)),
        out_specs=VMEM,
        name="sum_pieces",
    )(gb, *gas)


def scale_kernel(coefficient, *refs):
    total = refs[0][...].astype(jnp.float32)
    for ref in refs[1:-1]:
        total = total + ref[...].astype(jnp.float32)
    refs[-1][...] = (total * coefficient).astype(refs[-1].dtype)


def scale_sum(pieces, coefficient):
    return pl.pallas_call(
        functools.partial(scale_kernel, coefficient),
        out_shape=jax.ShapeDtypeStruct(pieces[0].shape, jnp.bfloat16),
        in_specs=[VMEM] * len(pieces),
        out_specs=VMEM,
        name="scale_sum",
    )(*pieces)


def spread_kernel(rank, group, place, *refs):
    pieces, (aq, bq, av, bv) = refs[:-4], refs[-4:]
    wide = pieces[0].shape[1]
    for step, ref in enumerate(pieces):
        mine = place[0] ^ step
        value = ref[...].astype(jnp.float32)
        at = pl.ds(pl.multiple_of(mine * wide, LANES), wide)
        aq[:, at] = value[:rank]
        av[:, at] = value[rank : 2 * rank]
        bq[:, pl.ds(pl.multiple_of(mine * group, LANES), group)] = value[2 * rank :, :group]
        bv[:, pl.ds(pl.multiple_of(mine * HEAD_SIZE, LANES), HEAD_SIZE)] = value[2 * rank :, group:]


def spread(place, pieces, rank, group, shapes):
    return pl.pallas_call(
        functools.partial(spread_kernel, rank, group),
        out_shape=[jax.ShapeDtypeStruct(shape, jnp.float32) for shape in shapes],
        in_specs=[SMEM] + [VMEM] * len(pieces),
        out_specs=[VMEM] * 4,
        name="spread",
    )(place, *pieces)


def ringed(value):
    return lax.ppermute(value, "z", [(0, 1), (1, 3), (3, 2), (2, 0)])


def paired_gather(place, qw, kw, vw, heads, norm_args, gradient):
    shard, rows = qw.shape[0], norm_args[0].shape[0]
    mine = lax.axis_index(GROUP)
    kept, given = pack_weights(mine, qw, kw, vw, heads)
    near, beside = join_rows(lax.axis_index("c"), kept, swapped(given, ("c",), 1))
    far = swapped(beside, ("y",), 1)
    normed, later = norm_tokens(*norm_args, 2, beside)
    c_tokens, x_tokens = swapped(normed, ("c",), 1), swapped(normed, ("ctx",), 1)
    (far,) = fence((far,), normed)
    near_1 = ringed(near)
    later, gradient = fence((later, gradient), far, near_1)
    y_tokens = swapped(later, ("y",), 1)
    hop_1 = jnp.concatenate([near_1, ringed(far)], 0)

    hop_2 = ringed(hop_1)
    half = rows // 2
    far_low, far_high = swapped(x_tokens[:half], ("y",), 1), swapped(y_tokens[half:], ("ctx",), 1)
    xc_tokens = swapped(x_tokens, ("c",), 1)
    (gradient,) = fence((gradient,), hop_1, xc_tokens)
    gradient = lax.all_to_all(gradient, GROUP, 0, 0, tiled=True)

    hop_3 = ringed(hop_2)
    (y_tokens,) = fence((y_tokens,), hop_2)
    yc_tokens, farc_low, farc_high = (swapped(value, ("c",), 1) for value in (y_tokens, far_low, far_high))

    def weight_columns(back):
        def columns(p):
            at = (p[1] ^ (p[1] >> 1)) - back + 4 & 3
            return (at ^ (at >> 1)) * 4 * shard

        return columns

    def token_rows(step, skip=0):
        return lambda p: (step & 3) * 2 * rows + ((p[0] >> 2) ^ (step >> 2)) * rows + skip

    def source(step):
        return lambda p: p[0] ^ step

    size = 2 * shard

    def ordered(first, second):
        return [
            (first, slice(0, size), lambda p: (p[0] & 2) * shard),
            (second, slice(-size, None), lambda p: (2 - (p[0] & 2)) * shard),
        ]

    pieces = [(0, 0, normed), (1, 0, c_tokens), (2, 0, y_tokens), (3, 0, yc_tokens), (4, 0, x_tokens)]
    pieces += [(5, 0, xc_tokens), (6, 0, far_low), (6, half, far_high), (7, 0, farc_low), (7, half, farc_high)]
    return {
        "w": [
            (weight_columns(0), ordered(near, far)),
            (weight_columns(1), ordered(hop_1, hop_1)),
            (weight_columns(2), ordered(hop_2, hop_2)),
        ],
        "last": (weight_columns(3), ordered(hop_3, hop_3)),
        "x": [((token_rows(step, skip), step & 3, None), value) for step, skip, value in pieces],
        "g": [((token_rows(step), step & 3, source(step)), gradient) for step in range(8)],
    }


def on_device(
    tokens,
    trace_index,
    input_norm_scale,
    query_weight,
    key_weight,
    value_weight,
    query_down_weight,
    query_up_weight,
    value_down_weight,
    value_up_weight,
    output_gradient,
):
    rows, feats = tokens.shape[1:]
    heads_kv = key_weight.shape[1] // HEAD_SIZE
    heads = query_weight.shape[1] // HEAD_SIZE // heads_kv
    group = heads * HEAD_SIZE
    rank = query_up_weight.shape[0]
    sizes = [lax.axis_size(axis) for axis in GROUP]
    parts = math.prod(sizes)
    shards = lax.axis_size("z")
    paired = sizes == [2, 2, 2] and shards == 4
    mine = lax.axis_index(GROUP)
    place = jnp.stack([mine, lax.axis_index("z")]).astype(jnp.int32)

    norm_args = (
        tokens.reshape(rows, feats),
        trace_index.reshape(1, rows),
        input_norm_scale,
        query_down_weight.T,
        value_down_weight.T,
    )
    gradient = jnp.moveaxis(output_gradient.reshape(rows, parts, group), 1, 0)
    if paired:
        gathered = paired_gather(
            place, query_weight, key_weight, value_weight, heads, norm_args, gradient
        )
    else:
        shard = query_weight.shape[0]
        split = [w.reshape(shard, parts, -1) for w in (query_weight, key_weight, value_weight)]
        columns = jnp.moveaxis(jnp.concatenate(split, -1), 1, 0)
        per = parts // sizes[0]
        columns = lax.dynamic_slice_in_dim(columns, lax.axis_index("ctx") * per, per, 0)
        columns = lax.all_to_all(columns, ("y", "c"), 0, 0, tiled=True).reshape(per * shard, -1)
        weights = lax.all_gather(columns, "z", axis=0, tiled=True)
        normed = lax.all_gather(norm_tokens(*norm_args, 1)[0], ("y", "c", "ctx"), axis=0, tiled=True)
        gradient = lax.all_to_all(gradient, GROUP, 0, 0, tiled=True)
        gradient = gradient.reshape(sizes[0], per, rows, group)
        gradient = jnp.moveaxis(gradient, 0, 1).reshape(parts * rows, group)
        gathered = {
            "w": [(lambda p: 0, [(weights, slice(None), lambda p: 0)])],
            "last": None,
            "x": [((lambda p: 0, 0, None), normed)],
            "g": [((lambda p: 0, 0, None), gradient)],
        }

    plan = {
        "feats": feats,
        "heads": heads,
        "seq": sizes[0] * rows,
        "window": 2 * rows,
        "tokens": parts * rows,
        "parts": parts,
        "cores": 1,
    }
    *ga, gb = attend(place, query_up_weight, value_up_weight, gathered, plan)

    coefficient = ADAPTER_NAME / math.sqrt(parts * shards * rows)
    pieces = lax.all_to_all(ga[0], GROUP, 0, 0, tiled=True)
    mixed = jnp.concatenate([jnp.sum(pieces.astype(jnp.float32), 0), gb], 0).astype(jnp.bfloat16)
    if shards & (shards - 1) == 0 and shards <= 4:
        mixed = [mixed] + [swapped(mixed, ("z",), step) for step in range(1, shards)]
    else:
        mixed = [lax.psum(mixed.astype(jnp.float32), "z")]
    scaled = (sum(piece.astype(jnp.float32) for piece in mixed) * coefficient).astype(jnp.bfloat16)
    chips = ("ctx", "y")
    scaled = [scaled] + [swapped(scaled, chips, step) for step in range(1, sizes[0] * sizes[1])]
    if sizes[2] == 2:
        scaled = [piece for value in scaled for piece in (value, swapped(value, ("c",), 1))]
    shapes = ((rank, feats), (rank, heads_kv * group), (rank, feats), (rank, heads_kv * HEAD_SIZE))
    aq, bq, av, bv = spread(place, scaled, rank, group, shapes)
    return aq.T, bq, av.T, bv


def solution(mesh):
    groups, ctx, fsdp = (mesh.shape[name] for name in ("groups", "ctx", "fsdp"))

    def run(*args):
        heads_kv = args[4].shape[1] // HEAD_SIZE
        share = heads_kv // ctx
        cores = 2 if share % 2 == 0 else 1
        split = (groups, ctx, fsdp // share, share // cores, cores)
        finer = Mesh(mesh.devices.reshape(split), ("groups", "ctx", "z", "y", "c"))
        whole = ("z", "y", "c")
        sequences = ("groups",) + whole
        by_rows = P(whole, None)
        by_tokens = P(sequences, "ctx", None)
        out = P("groups", None)
        return jax.shard_map(
            on_device,
            mesh=finer,
            in_specs=(
                by_tokens, P(sequences, "ctx"), P(), by_rows, by_rows, by_rows, P(), P(), P(), P(), by_tokens
            ),
            out_specs=(out, out, out, out),
            check_vma=False,
        )(*args)

    return run
```

```python
import functools
import math

import jax
import jax.numpy as jnp
from jax import lax
from jax.experimental import pallas as pl
from jax.experimental.pallas import tpu as pltpu
from jax.sharding import Mesh
from jax.sharding import PartitionSpec as P

HEAD_SIZE = 128
LANES = 128

CAP = 50.0
QSCALE = 1.0 / 12.0
ADAPTER_NAME = 0.5
EPS = 1e-06

GROUP = ("ctx", "y", "c")
ANY = pl.BlockSpec(memory_space=pl.ANY)
VMEM = pl.BlockSpec(memory_space=pltpu.VMEM)
SMEM = pl.BlockSpec(memory_space=pltpu.SMEM)
PARAMS = pltpu.CompilerParams(vmem_limit_bytes=63 * 2**20)

NT = (((1,), (1,)), ((), ()))
TN = (((0,), (0,)), ((), ()))


def dot(a, b, dims=(((1,), (0,)), ((), ()))):
    return lax.dot_general(a, b, dims, preferred_element_type=jnp.float32)


def add_wide(first, second):
    return first.astype(jnp.float32) + second.astype(jnp.float32)


def swapped(value, axes, distance):
    count = 1
    for axis in axes:
        count *= lax.axis_size(axis)
    return lax.ppermute(value, axes, [(i, i ^ distance) for i in range(count)])


def pack_weights(mine, qw, kw, vw, heads):
    def columns(owner):
        wide = heads * HEAD_SIZE
        parts = [lax.dynamic_slice_in_dim(qw, owner * wide, wide, 1)]
        parts += [lax.dynamic_slice_in_dim(w, owner * HEAD_SIZE, HEAD_SIZE, 1) for w in (kw, vw)]
        return jnp.concatenate(parts, 1)

    return [jnp.stack([columns(mine ^ (2 * chip + core)) for chip in range(2)]) for core in range(2)]


def join_rows(core, kept, got):
    first, second = jnp.where(core == 0, kept, got), jnp.where(core == 0, got, kept)
    return [jnp.concatenate([first[chip], second[chip]], 0) for chip in range(2)]


def fence_kernel(*refs):
    pass


def fence(values, *earlier, wait_us=0):
    count = len(values)
    return pl.pallas_call(
        fence_kernel,
        out_shape=[jax.ShapeDtypeStruct(value.shape, value.dtype) for value in values],
        in_specs=[ANY] * (count + len(earlier)),
        out_specs=[ANY] * count,
        input_output_aliases={i: i for i in range(count)},
        cost_estimate=pl.CostEstimate(
            flops=wait_us * 10**9, bytes_accessed=wait_us * 3 * 10**6, transcendentals=0
        ),
        compiler_params=PARAMS,
        name="fence",
    )(*values, *earlier)


def norm_kernel(copies, tokens, trace, gain, down_q, down_v, *rest):
    flt = tokens[...].astype(jnp.float32)
    meansq = jnp.mean(flt * flt, axis=-1, keepdims=True)
    normed = (flt * lax.rsqrt(meansq + EPS) * gain[...].astype(jnp.float32)[None, :]).astype(jnp.bfloat16)
    rows, feats = normed.shape
    rank = down_q.shape[0]
    low_q = dot(normed, down_q[...], NT)
    low_v = dot(normed, down_v[...], NT)
    square = (rows, rows)
    diagonal = lax.broadcasted_iota(jnp.int32, square, 0) == lax.broadcasted_iota(jnp.int32, square, 1)
    ids = jnp.sum(jnp.where(diagonal, trace[...].astype(jnp.float32), 0.0), axis=1, keepdims=True)
    filler = jnp.zeros((rows, LANES - 2 * rank - 1), jnp.float32)
    extra = jnp.concatenate([low_q, low_v, ids, filler], 1).astype(jnp.bfloat16)
    for out in rest[-copies:]:
        out[:, :feats] = normed
        out[:, feats:] = extra


def norm_tokens(tokens, trace, gain, down_q, down_v, copies, *earlier):
    rows, feats = tokens.shape
    return pl.pallas_call(
        functools.partial(norm_kernel, copies),
        out_shape=[jax.ShapeDtypeStruct((rows, feats + LANES), jnp.bfloat16)] * copies,
        in_specs=[VMEM] * 5 + [ANY] * len(earlier),
        out_specs=[VMEM] * copies,
        compiler_params=pltpu.CompilerParams(vmem_limit_bytes=16 * 2**20),
        name="norm_tokens",
    )(tokens, trace, gain, down_q, down_v, *earlier)


class Loads:
    def __init__(self, sems):
        self.sems, self.copies = sems, []

    def add(self, place, pieces, target):
        for piece, src in pieces:
            offset, sequence, choice = piece
            begin = pl.multiple_of(offset(place), 16)
            rows = src.shape[-2]
            if choice is not None and len(src.shape) == 3:
                src = src.at[choice(place)]
            self.add_copy(sequence, src, target.at[pl.ds(begin, rows), :])

    def add_copy(self, sequence, src, target):
        self.copies.append((sequence, pltpu.make_async_copy(src, target, self.sems.at[len(self.copies)])))

    def start(self, sequence):
        for needed, copy in self.copies:
            if needed == sequence:
                copy.start()

    def wait(self, sequence):
        for needed, copy in self.copies:
            if needed == sequence:
                copy.wait()


def project_kernel(plan, *refs):
    n_x, shards = len(plan["x"]), plan["shards"]
    place, up_q, up_v = refs[:3]
    x_refs, w_refs, rest = refs[3 : 3 + n_x], refs[3 + n_x : -4], refs[-4:]
    out, x_all, w_all, sems = rest
    feats, heads, seq = plan["feats"], plan["heads"], plan["seq"]
    rank, group = up_q.shape[0], heads * HEAD_SIZE
    depth = plan["depth"]

    loads = Loads(sems)
    for index, (_, chunks) in enumerate(shards):
        for number, part, at in chunks:
            piece = (lambda p, at=at, index=index: index * depth + at(p), 0, None)
            src = w_refs[number]
            rows = src.shape[0]
            src = src.at[slice(*part.indices(rows))]
            loads.add(place, [(piece, src)], w_all)
    loads.add(place, list(zip(plan["x"], x_refs)), x_all)
    loads.start(0)

    mine = place[0]
    uq = up_q[:, pl.ds(pl.multiple_of(mine * group, group), group)]
    uv = up_v[:, pl.ds(pl.multiple_of(mine * HEAD_SIZE, HEAD_SIZE), HEAD_SIZE)]
    zero = functools.partial(jnp.zeros, dtype=jnp.float32)
    top = jnp.concatenate([ADAPTER_NAME * uq.astype(jnp.float32), zero((rank, 2 * HEAD_SIZE))], 1)
    low = jnp.concatenate([zero((rank, group + HEAD_SIZE)), ADAPTER_NAME * uv.astype(jnp.float32)], 1)
    pad = zero((LANES - 2 * rank, group + 2 * HEAD_SIZE))
    ups = jnp.concatenate([top, low, pad], 0).astype(jnp.bfloat16)

    for index in range(x_all.shape[0] // seq):
        loads.start(index + 1)
        loads.wait(index)
        rows = pl.ds(index * seq, seq)
        total = dot(x_all[rows, feats:], ups)
        for number, (offset, _) in enumerate(shards):
            columns = pl.ds(pl.multiple_of(offset(place), LANES), depth)
            total = total + dot(x_all[rows, columns], w_all[number * depth : (number + 1) * depth])
        out[rows, :] = total


def attend_kernel(plan, *refs):
    n_x, n_g, last = len(plan["x"]), len(plan["g"]), plan["last"]
    place, up_q, up_v, base = refs[:4]
    x_refs, g_refs = refs[4 : 4 + n_x], refs[4 + n_x : 4 + n_x + n_g]
    w_refs, rest = refs[4 + n_x + n_g : -8], refs[-8:]
    ga_out, gb_out, x_all, g_all, w_all, base_all, pulls, sems = rest

    feats, heads, seq, window, depth = (plan[k] for k in ("feats", "heads", "seq", "window", "depth"))
    rank, parts = up_q.shape[0], plan["parts"]
    group = heads * HEAD_SIZE
    tokens = x_all.shape[0]
    sequences = tokens // seq

    loads = Loads(sems)
    for index in range(sequences):
        rows = pl.ds(index * seq, seq)
        loads.add_copy(index, base.at[rows, :], base_all.at[rows, :])
        for pieces, sources, target in ((plan["x"], x_refs, x_all), (plan["g"], g_refs, g_all)):
            chosen = [(piece, src) for piece, src in zip(pieces, sources) if piece[1] == index]
            loads.add(place, chosen, target)
    if last is not None:
        offset, chunks = last
        for part, at in chunks:
            src = w_refs[0].at[slice(*part.indices(depth))]
            target = w_all.at[pl.ds(pl.multiple_of(at(place), 16), src.shape[0]), :]
            loads.add_copy(0, src, target)
    loads.start(0)

    mine = place[0]
    uq = up_q[:, pl.ds(pl.multiple_of(mine * group, group), group)]
    uv = up_v[:, pl.ds(pl.multiple_of(mine * HEAD_SIZE, HEAD_SIZE), HEAD_SIZE)]
    id_row = jnp.where(lax.broadcasted_iota(jnp.int32, (8, LANES), 1) == 2 * rank, 1.0, 0.0).astype(jnp.bfloat16)
    span = plan["span"]
    blocks = seq // span
    sums = jnp.zeros((LANES, group + 2 * HEAD_SIZE), jnp.float32)

    for index in range(sequences):
        loads.start(index + 1)
        loads.wait(index)
        rows = pl.ds(index * seq, seq)
        qkv = base_all[rows, :]
        if last is not None:
            columns = pl.ds(pl.multiple_of(offset(place), LANES), depth)
            qkv = qkv + dot(x_all[rows, columns], w_all[...])
        qkv = qkv.astype(jnp.bfloat16)
        extra = x_all[rows, feats:]
        ids_key = dot(id_row, extra, NT)[:1]
        ids_query = extra[:, 2 * rank : 2 * rank + 1].astype(jnp.float32)
        keys = qkv[:, group : group + HEAD_SIZE]
        values = qkv[:, group + HEAD_SIZE :]
        grads = g_all[rows, :]
        dq_parts, dv_parts = [], [None] * blocks
        for block in range(blocks):
            lo, hi = block * span, (block + 1) * span
            back = max(0, lo - window)
            kb, vb = keys[back:hi], values[back:hi]
            shape = (span, hi - back)
            pos_q = lax.broadcasted_iota(jnp.int32, shape, 0) + lo
            pos_k = lax.broadcasted_iota(jnp.int32, shape, 1) + back
            mask = (pos_k <= pos_q) & (pos_k > pos_q - window)
            mask = mask & (ids_query[lo:hi] == ids_key[:, back:hi])
            masks = jnp.concatenate([jnp.where(mask, 1.0, 0.0)] * heads, 0)
            q, g = (
                jnp.concatenate([x[lo:hi, h * HEAD_SIZE : (h + 1) * HEAD_SIZE] for h in range(heads)], 0)
                for x in (qkv, grads)
            )
            t = jnp.tanh(dot(q, kb, NT) * (QSCALE / CAP))
            dweight = dot(g, vb, NT)
            expo = masks * jnp.exp2((CAP * math.log2(math.e)) * t)
            share = 1.0 / jnp.sum(expo, axis=-1, keepdims=True)
            weights = expo * share
            delta = jnp.sum(expo * dweight, axis=-1, keepdims=True) * share
            dscore = (weights * (dweight - delta) * (1.0 - t * t)).astype(jnp.bfloat16)
            dq = (dot(dscore, kb) * QSCALE).astype(jnp.bfloat16)
            dq_parts.append(jnp.concatenate([dq[h * span : (h + 1) * span] for h in range(heads)], 1))
            dv = dot(weights.astype(jnp.bfloat16), g, TN)
            for at in range(back // span, block + 1):
                piece = dv[at * span - back : (at + 1) * span - back]
                dv_parts[at] = piece if dv_parts[at] is None else dv_parts[at] + piece
        dq, dv = jnp.concatenate(dq_parts, 0), jnp.concatenate(dv_parts, 0)
        dv_hi = dv.astype(jnp.bfloat16)
        dv_lo = (dv - dv_hi.astype(jnp.float32)).astype(jnp.bfloat16)
        pull_q = dot(uq, dq, NT)
        pull_v = dot(uv, dv_hi, NT) + dot(uv, dv_lo, NT)
        pull_v_hi = pull_v.astype(jnp.bfloat16)
        pull_v_lo = (pull_v - pull_v_hi.astype(jnp.float32)).astype(jnp.bfloat16)
        pulls[:, rows] = jnp.concatenate([pull_q.astype(jnp.bfloat16), pull_v_hi, pull_v_lo], 0)
        sums = sums + dot(extra, jnp.concatenate([dq, dv_hi, dv_lo], 1), TN)

    gb_out[:, :group] = sums[:rank, :group]
    gb_out[:, group:] = sums[rank : 2 * rank, group : group + HEAD_SIZE] + sums[rank : 2 * rank, group + HEAD_SIZE :]
    part = feats // parts
    for index in range(parts):
        piece = dot(pulls[...], x_all[:, index * part : (index + 1) * part])
        ga_out[index, :rank] = piece[:rank].astype(ga_out.dtype)
        ga_out[index, rank:] = (piece[rank : 2 * rank] + piece[2 * rank :]).astype(ga_out.dtype)


def attend(place, up_q, up_v, gathered, plan):
    feats, heads, tokens, parts, seq = (plan[k] for k in ("feats", "heads", "tokens", "parts", "seq"))
    rank = up_q.shape[0]
    wide = (heads + 2) * HEAD_SIZE
    x_plan, x_arrays = zip(*gathered["x"])
    g_plan, g_arrays = zip(*gathered["g"])
    w_arrays, shards = [], []
    for offset, chunks in gathered["w"]:
        shards.append((offset, []))
        for array, part, at in chunks:
            index = next((i for i, known in enumerate(w_arrays) if known is array), len(w_arrays))
            w_arrays += [array] if index == len(w_arrays) else []
            shards[-1][1].append((index, part, at))
    depth = w_arrays[-1].shape[0]
    plan = dict(plan, x=x_plan, g=g_plan, shards=shards, depth=depth)
    base = pl.pallas_call(
        functools.partial(project_kernel, plan),
        out_shape=jax.ShapeDtypeStruct((tokens, wide), jnp.float32),
        in_specs=[SMEM, VMEM, VMEM] + [ANY] * (len(x_arrays) + len(w_arrays)),
        out_specs=VMEM,
        scratch_shapes=[
            pltpu.VMEM((tokens, feats + LANES), jnp.bfloat16),
            pltpu.VMEM((len(shards) * depth, wide), jnp.bfloat16),
            pltpu.SemaphoreType.DMA((len(x_arrays) + 2 * len(shards),)),
        ],
        cost_estimate=pl.CostEstimate(flops=0, bytes_accessed=0, transcendentals=0),
        compiler_params=PARAMS,
        name="project",
    )(place, up_q, up_v, *x_arrays, *w_arrays)

    offset, chunks = gathered["last"] or (None, [])
    plan["last"] = None if offset is None else (offset, [chunk[1:] for chunk in chunks])
    last = [chunks[0][0]] if chunks else []
    return pl.pallas_call(
        functools.partial(attend_kernel, plan),
        out_shape=[
            jax.ShapeDtypeStruct((parts, 2 * rank, feats // parts), jnp.bfloat16),
            jax.ShapeDtypeStruct((rank, (heads + 1) * HEAD_SIZE), jnp.float32),
        ],
        in_specs=[SMEM, VMEM, VMEM]
        + [ANY] * (1 + len(x_arrays) + len(g_arrays))
        + [ANY] * len(last),
        out_specs=[VMEM] * 2,
        scratch_shapes=[
            pltpu.VMEM((tokens, feats + LANES), jnp.bfloat16),
            pltpu.VMEM((tokens, heads * HEAD_SIZE), jnp.bfloat16),
            pltpu.VMEM((depth, wide) if last else (16, LANES), jnp.bfloat16),
            pltpu.VMEM((tokens, wide), jnp.float32),
            pltpu.VMEM((3 * rank, tokens), jnp.bfloat16),
            pltpu.SemaphoreType.DMA((len(chunks) + tokens // seq + len(x_arrays) + len(g_arrays),)),
        ],
        compiler_params=PARAMS,
        name="attend",
    )(place, up_q, up_v, base, *x_arrays, *g_arrays, *last)


def spread_kernel(rank, group, place, *refs):
    pieces, (aq, bq, av, bv) = refs[:-4], refs[-4:]
    wide = pieces[0].shape[1]
    for step, ref in enumerate(pieces):
        mine = place[0] ^ step
        value = ref[...].astype(jnp.float32)
        at = pl.ds(pl.multiple_of(mine * wide, LANES), wide)
        aq[:, at] = value[:rank]
        av[:, at] = value[rank : 2 * rank]
        bq[:, pl.ds(pl.multiple_of(mine * group, LANES), group)] = value[2 * rank :, :group]
        bv[:, pl.ds(pl.multiple_of(mine * HEAD_SIZE, LANES), HEAD_SIZE)] = value[2 * rank :, group:]


def spread(place, pieces, rank, group, shapes):
    return pl.pallas_call(
        functools.partial(spread_kernel, rank, group),
        out_shape=[jax.ShapeDtypeStruct(shape, jnp.float32) for shape in shapes],
        in_specs=[SMEM] + [VMEM] * len(pieces),
        out_specs=[VMEM] * 4,
        name="spread",
    )(place, *pieces)


def ringed(value):
    return lax.ppermute(value, "z", [(0, 1), (1, 3), (3, 2), (2, 0)])


def paired_gather(place, qw, kw, vw, heads, norm_args, gradient):
    shard, rows = qw.shape[0], norm_args[0].shape[0]
    mine = lax.axis_index(GROUP)
    kept, given = pack_weights(mine, qw, kw, vw, heads)
    near, beside = join_rows(lax.axis_index("c"), kept, swapped(given, ("c",), 1))
    far = swapped(beside, ("y",), 1)
    normed, later = norm_tokens(*norm_args, 2, beside)
    c_tokens, x_tokens = swapped(normed, ("c",), 1), swapped(normed, ("ctx",), 1)
    (near_1,) = fence((ringed(near),), wait_us=6)
    later, gradient = fence((later, gradient), far, near_1)
    y_tokens = swapped(later, ("y",), 1)
    hop_1 = jnp.concatenate([near_1, ringed(far)], 0)

    hop_2 = ringed(hop_1)
    half = rows // 2
    far_low, far_high = swapped(x_tokens[:half], ("y",), 1), swapped(y_tokens[half:], ("ctx",), 1)
    xc_tokens = swapped(x_tokens, ("c",), 1)
    (gradient,) = fence((gradient,), hop_1, xc_tokens)
    gradient = lax.all_to_all(gradient, GROUP, 0, 0, tiled=True)

    hop_3 = ringed(hop_2)
    (y_tokens,) = fence((y_tokens,), hop_2)
    yc_tokens, farc_low, farc_high = (swapped(value, ("c",), 1) for value in (y_tokens, far_low, far_high))

    def weight_columns(back):
        def columns(p):
            at = (p[1] ^ (p[1] >> 1)) - back + 4 & 3
            return (at ^ (at >> 1)) * 4 * shard

        return columns

    def token_rows(step, skip=0):
        return lambda p: (step & 3) * 2 * rows + ((p[0] >> 2) ^ (step >> 2)) * rows + skip

    def source(step):
        return lambda p: p[0] ^ step

    size = 2 * shard

    def ordered(first, second):
        return [
            (first, slice(0, size), lambda p: (p[0] & 2) * shard),
            (second, slice(-size, None), lambda p: (2 - (p[0] & 2)) * shard),
        ]

    pieces = [(0, 0, normed), (1, 0, c_tokens), (2, 0, y_tokens), (3, 0, yc_tokens), (4, 0, x_tokens)]
    pieces += [(5, 0, xc_tokens), (6, 0, far_low), (6, half, far_high), (7, 0, farc_low), (7, half, farc_high)]
    return {
        "w": [
            (weight_columns(0), ordered(near, far)),
            (weight_columns(1), ordered(hop_1, hop_1)),
            (weight_columns(2), ordered(hop_2, hop_2)),
        ],
        "last": (weight_columns(3), ordered(hop_3, hop_3)),
        "x": [((token_rows(step, skip), step & 3, None), value) for step, skip, value in pieces],
        "g": [((token_rows(step), step & 3, source(step)), gradient) for step in range(8)],
    }


def on_device(
    tokens,
    trace_index,
    input_norm_scale,
    query_weight,
    key_weight,
    value_weight,
    query_down_weight,
    query_up_weight,
    value_down_weight,
    value_up_weight,
    output_gradient,
):
    rows, feats = tokens.shape[1:]
    heads_kv = key_weight.shape[1] // HEAD_SIZE
    heads = query_weight.shape[1] // HEAD_SIZE // heads_kv
    group = heads * HEAD_SIZE
    rank = query_up_weight.shape[0]
    sizes = [lax.axis_size(axis) for axis in GROUP]
    parts = math.prod(sizes)
    shards = lax.axis_size("z")
    paired = sizes == [2, 2, 2] and shards == 4
    mine = lax.axis_index(GROUP)
    place = jnp.stack([mine, lax.axis_index("z")]).astype(jnp.int32)

    norm_args = (
        tokens.reshape(rows, feats),
        trace_index.reshape(1, rows),
        input_norm_scale,
        query_down_weight.T,
        value_down_weight.T,
    )
    gradient = jnp.moveaxis(output_gradient.reshape(rows, parts, group), 1, 0)
    if paired:
        gathered = paired_gather(
            place, query_weight, key_weight, value_weight, heads, norm_args, gradient
        )
    else:
        shard = query_weight.shape[0]
        split = [w.reshape(shard, parts, -1) for w in (query_weight, key_weight, value_weight)]
        columns = jnp.moveaxis(jnp.concatenate(split, -1), 1, 0)
        per = parts // sizes[0]
        columns = lax.dynamic_slice_in_dim(columns, lax.axis_index("ctx") * per, per, 0)
        columns = lax.all_to_all(columns, ("y", "c"), 0, 0, tiled=True).reshape(per * shard, -1)
        weights = lax.all_gather(columns, "z", axis=0, tiled=True)
        normed = lax.all_gather(norm_tokens(*norm_args, 1)[0], ("y", "c", "ctx"), axis=0, tiled=True)
        gradient = lax.all_to_all(gradient, GROUP, 0, 0, tiled=True)
        gradient = gradient.reshape(sizes[0], per, rows, group)
        gradient = jnp.moveaxis(gradient, 0, 1).reshape(parts * rows, group)
        gathered = {
            "w": [(lambda p: 0, [(weights, slice(None), lambda p: 0)])],
            "last": None,
            "x": [((lambda p: 0, 0, None), normed)],
            "g": [((lambda p: 0, 0, None), gradient)],
        }

    plan = {
        "feats": feats,
        "heads": heads,
        "seq": sizes[0] * rows,
        "window": 2 * rows,
        "span": min(sizes[0], 2) * rows,
        "tokens": parts * rows,
        "parts": parts,
    }
    ga, gb = attend(place, query_up_weight, value_up_weight, gathered, plan)

    coefficient = ADAPTER_NAME / math.sqrt(parts * shards * rows)
    part = jnp.sum(lax.all_to_all(ga, GROUP, 0, 0, tiled=True).astype(jnp.float32), 0)
    mixed = jnp.concatenate([part, gb], 0).astype(jnp.bfloat16)
    if paired:
        for step in (1, 2):
            mixed = add_wide(mixed, swapped(mixed, ("z",), step)).astype(jnp.bfloat16)
    else:
        mixed = lax.psum(mixed.astype(jnp.float32), "z")
    scaled = (mixed.astype(jnp.float32) * coefficient).astype(jnp.bfloat16)
    chips = ("ctx", "y")
    scaled = [scaled] + [swapped(scaled, chips, step) for step in range(1, sizes[0] * sizes[1])]
    if sizes[2] == 2:
        scaled = [piece for value in scaled for piece in (value, swapped(value, ("c",), 1))]
    shapes = ((rank, feats), (rank, heads_kv * group), (rank, feats), (rank, heads_kv * HEAD_SIZE))
    aq, bq, av, bv = spread(place, scaled, rank, group, shapes)
    return aq.T, bq, av.T, bv


def solution(mesh):
    groups, ctx, fsdp = (mesh.shape[name] for name in ("groups", "ctx", "fsdp"))

    def run(*args):
        heads_kv = args[4].shape[1] // HEAD_SIZE
        share = heads_kv // ctx
        cores = 2 if share % 2 == 0 else 1
        split = (groups, ctx, fsdp // share, share // cores, cores)
        finer = Mesh(mesh.devices.reshape(split), ("groups", "ctx", "z", "y", "c"))
        whole = ("z", "y", "c")
        sequences = ("groups",) + whole
        by_rows = P(whole, None)
        by_tokens = P(sequences, "ctx", None)
        out = P("groups", None)
        return jax.shard_map(
            on_device,
            mesh=finer,
            in_specs=(
                by_tokens, P(sequences, "ctx"), P(), by_rows, by_rows, by_rows, P(), P(), P(), P(), by_tokens
            ),
            out_specs=(out, out, out, out),
            check_vma=False,
        )(*args)

    return run
```

```python
import functools
import math

import jax
import jax.numpy as jnp
from jax import lax
from jax.experimental import pallas as pl
from jax.experimental.pallas import tpu as pltpu
from jax.sharding import Mesh
from jax.sharding import PartitionSpec as P

HEAD_SIZE = 128
LANES = 128

CAP = 50.0
QSCALE = 1.0 / 12.0
ADAPTER_NAME = 0.5
EPS = 1e-06

GROUP = ("ctx", "y", "c")
ANY = pl.BlockSpec(memory_space=pl.ANY)
VMEM = pl.BlockSpec(memory_space=pltpu.VMEM)
SMEM = pl.BlockSpec(memory_space=pltpu.SMEM)
PARAMS = pltpu.CompilerParams(vmem_limit_bytes=63 * 2**20)

NT = (((1,), (1,)), ((), ()))
TN = (((0,), (0,)), ((), ()))


def dot(a, b, dims=(((1,), (0,)), ((), ()))):
    return lax.dot_general(a, b, dims, preferred_element_type=jnp.float32)


def add_wide(first, second):
    return first.astype(jnp.float32) + second.astype(jnp.float32)


def swapped(value, axes, distance):
    count = 1
    for axis in axes:
        count *= lax.axis_size(axis)
    return lax.ppermute(value, axes, [(i, i ^ distance) for i in range(count)])


def pack_weights(mine, qw, kw, vw, heads):
    def columns(owner):
        wide = heads * HEAD_SIZE
        parts = [lax.dynamic_slice_in_dim(qw, owner * wide, wide, 1)]
        parts += [lax.dynamic_slice_in_dim(w, owner * HEAD_SIZE, HEAD_SIZE, 1) for w in (kw, vw)]
        return jnp.concatenate(parts, 1)

    return [jnp.stack([columns(mine ^ (2 * chip + core)) for chip in range(2)]) for core in range(2)]


def join_rows(core, kept, got):
    first, second = jnp.where(core == 0, kept, got), jnp.where(core == 0, got, kept)
    return [jnp.concatenate([first[chip], second[chip]], 0) for chip in range(2)]


def fence_kernel(*refs):
    pass


def fence(values, *earlier, wait_us=0):
    count = len(values)
    return pl.pallas_call(
        fence_kernel,
        out_shape=[jax.ShapeDtypeStruct(value.shape, value.dtype) for value in values],
        in_specs=[ANY] * (count + len(earlier)),
        out_specs=[ANY] * count,
        input_output_aliases={i: i for i in range(count)},
        cost_estimate=pl.CostEstimate(
            flops=wait_us * 10**9, bytes_accessed=wait_us * 3 * 10**6, transcendentals=0
        ),
        compiler_params=pltpu.CompilerParams(vmem_limit_bytes=60 * 2**20),
        name="fence",
    )(*values, *earlier)


def norm_kernel(copies, tokens, trace, gain, down_q, down_v, *rest):
    flt = tokens[...].astype(jnp.float32)
    meansq = jnp.mean(flt * flt, axis=-1, keepdims=True)
    normed = (flt * lax.rsqrt(meansq + EPS) * gain[...].astype(jnp.float32)[None, :]).astype(jnp.bfloat16)
    rows, feats = normed.shape
    rank = down_q.shape[0]
    low_q = dot(normed, down_q[...], NT)
    low_v = dot(normed, down_v[...], NT)
    square = (rows, rows)
    diagonal = lax.broadcasted_iota(jnp.int32, square, 0) == lax.broadcasted_iota(jnp.int32, square, 1)
    ids = jnp.sum(jnp.where(diagonal, trace[...].astype(jnp.float32), 0.0), axis=1, keepdims=True)
    filler = jnp.zeros((rows, LANES - 2 * rank - 1), jnp.float32)
    extra = jnp.concatenate([low_q, low_v, ids, filler], 1).astype(jnp.bfloat16)
    for out in rest[-copies:]:
        out[:, :feats] = normed
        out[:, feats:] = extra


def norm_tokens(tokens, trace, gain, down_q, down_v, copies, *earlier):
    rows, feats = tokens.shape
    return pl.pallas_call(
        functools.partial(norm_kernel, copies),
        out_shape=[jax.ShapeDtypeStruct((rows, feats + LANES), jnp.bfloat16)] * copies,
        in_specs=[VMEM] * 5 + [ANY] * len(earlier),
        out_specs=[VMEM] * copies,
        compiler_params=pltpu.CompilerParams(vmem_limit_bytes=16 * 2**20),
        name="norm_tokens",
    )(tokens, trace, gain, down_q, down_v, *earlier)


class Loads:
    def __init__(self, sems):
        self.sems, self.copies = sems, []

    def add(self, place, pieces, target):
        for piece, src in pieces:
            offset, sequence, choice = piece
            begin = pl.multiple_of(offset(place), 16)
            rows = src.shape[-2]
            if choice is not None and len(src.shape) == 3:
                src = src.at[choice(place)]
            self.add_copy(sequence, src, target.at[pl.ds(begin, rows), :])

    def add_copy(self, sequence, src, target):
        self.copies.append((sequence, pltpu.make_async_copy(src, target, self.sems.at[len(self.copies)])))

    def start(self, sequence):
        for needed, copy in self.copies:
            if needed == sequence:
                copy.start()

    def wait(self, sequence):
        for needed, copy in self.copies:
            if needed == sequence:
                copy.wait()


def project_kernel(plan, *refs):
    n_x, shards = len(plan["x"]), plan["shards"]
    place, up_q, up_v = refs[:3]
    x_refs, w_refs, rest = refs[3 : 3 + n_x], refs[3 + n_x : -4], refs[-4:]
    out, x_all, w_all, sems = rest
    feats, heads, seq = plan["feats"], plan["heads"], plan["seq"]
    rank, group = up_q.shape[0], heads * HEAD_SIZE
    depth = plan["depth"]

    loads = Loads(sems)
    for index, (_, chunks) in enumerate(shards):
        for number, part, at in chunks:
            piece = (lambda p, at=at, index=index: index * depth + at(p), 0, None)
            src = w_refs[number]
            rows = src.shape[0]
            src = src.at[slice(*part.indices(rows))]
            loads.add(place, [(piece, src)], w_all)
    loads.add(place, list(zip(plan["x"], x_refs)), x_all)
    loads.start(0)

    mine = place[0]
    uq = up_q[:, pl.ds(pl.multiple_of(mine * group, group), group)]
    uv = up_v[:, pl.ds(pl.multiple_of(mine * HEAD_SIZE, HEAD_SIZE), HEAD_SIZE)]
    zero = functools.partial(jnp.zeros, dtype=jnp.float32)
    top = jnp.concatenate([ADAPTER_NAME * uq.astype(jnp.float32), zero((rank, 2 * HEAD_SIZE))], 1)
    low = jnp.concatenate([zero((rank, group + HEAD_SIZE)), ADAPTER_NAME * uv.astype(jnp.float32)], 1)
    pad = zero((LANES - 2 * rank, group + 2 * HEAD_SIZE))
    ups = jnp.concatenate([top, low, pad], 0).astype(jnp.bfloat16)

    for index in range(x_all.shape[0] // seq):
        loads.start(index + 1)
        loads.wait(index)
        rows = pl.ds(index * seq, seq)
        total = dot(x_all[rows, feats:], ups)
        for number, (offset, _) in enumerate(shards):
            columns = pl.ds(pl.multiple_of(offset(place), LANES), depth)
            total = total + dot(x_all[rows, columns], w_all[number * depth : (number + 1) * depth])
        out[rows, :] = total


def attend_kernel(plan, *refs):
    n_x, n_g, last = len(plan["x"]), len(plan["g"]), plan["last"]
    place, up_q, up_v, base = refs[:4]
    x_refs, g_refs = refs[4 : 4 + n_x], refs[4 + n_x : 4 + n_x + n_g]
    w_refs, rest = refs[4 + n_x + n_g : -8], refs[-8:]
    ga_out, gb_out, x_all, g_all, w_all, base_all, pulls, sems = rest

    feats, heads, seq, window, depth = (plan[k] for k in ("feats", "heads", "seq", "window", "depth"))
    rank, parts = up_q.shape[0], plan["parts"]
    group = heads * HEAD_SIZE
    tokens = x_all.shape[0]
    sequences = tokens // seq

    loads = Loads(sems)
    for index in range(sequences):
        rows = pl.ds(index * seq, seq)
        loads.add_copy(index, base.at[rows, :], base_all.at[rows, :])
        for pieces, sources, target in ((plan["x"], x_refs, x_all), (plan["g"], g_refs, g_all)):
            chosen = [(piece, src) for piece, src in zip(pieces, sources) if piece[1] == index]
            loads.add(place, chosen, target)
    if last is not None:
        offset, chunks = last
        for part, at in chunks:
            src = w_refs[0].at[slice(*part.indices(depth))]
            target = w_all.at[pl.ds(pl.multiple_of(at(place), 16), src.shape[0]), :]
            loads.add_copy(0, src, target)
    loads.start(0)

    mine = place[0]
    uq = up_q[:, pl.ds(pl.multiple_of(mine * group, group), group)]
    uv = up_v[:, pl.ds(pl.multiple_of(mine * HEAD_SIZE, HEAD_SIZE), HEAD_SIZE)]
    id_row = jnp.where(lax.broadcasted_iota(jnp.int32, (8, LANES), 1) == 2 * rank, 1.0, 0.0).astype(jnp.bfloat16)
    span = plan["span"]
    blocks = seq // span
    sums = jnp.zeros((LANES, group + 2 * HEAD_SIZE), jnp.float32)

    for index in range(sequences):
        loads.start(index + 1)
        loads.wait(index)
        rows = pl.ds(index * seq, seq)
        qkv = base_all[rows, :]
        if last is not None:
            columns = pl.ds(pl.multiple_of(offset(place), LANES), depth)
            qkv = qkv + dot(x_all[rows, columns], w_all[...])
        qkv = qkv.astype(jnp.bfloat16)
        extra = x_all[rows, feats:]
        ids_key = dot(id_row, extra, NT)[:1]
        ids_query = extra[:, 2 * rank : 2 * rank + 1].astype(jnp.float32)
        keys = qkv[:, group : group + HEAD_SIZE]
        values = qkv[:, group + HEAD_SIZE :]
        grads = g_all[rows, :]
        dq_parts, dv_parts = [], [None] * blocks
        for block in range(blocks):
            lo, hi = block * span, (block + 1) * span
            back = max(0, lo - window)
            kb, vb = keys[back:hi], values[back:hi]
            shape = (span, hi - back)
            pos_q = lax.broadcasted_iota(jnp.int32, shape, 0) + lo
            pos_k = lax.broadcasted_iota(jnp.int32, shape, 1) + back
            mask = (pos_k <= pos_q) & (pos_k > pos_q - window)
            mask = mask & (ids_query[lo:hi] == ids_key[:, back:hi])
            masks = jnp.concatenate([jnp.where(mask, 1.0, 0.0)] * heads, 0)
            q, g = (
                jnp.concatenate([x[lo:hi, h * HEAD_SIZE : (h + 1) * HEAD_SIZE] for h in range(heads)], 0)
                for x in (qkv, grads)
            )
            t = jnp.tanh(dot(q, kb, NT) * (QSCALE / CAP))
            dweight = dot(g, vb, NT)
            expo = masks * jnp.exp2((CAP * math.log2(math.e)) * t)
            share = 1.0 / jnp.sum(expo, axis=-1, keepdims=True)
            weights = expo * share
            delta = jnp.sum(expo * dweight, axis=-1, keepdims=True) * share
            dscore = (weights * (dweight - delta) * (1.0 - t * t)).astype(jnp.bfloat16)
            dq = (dot(dscore, kb) * QSCALE).astype(jnp.bfloat16)
            dq_parts.append(jnp.concatenate([dq[h * span : (h + 1) * span] for h in range(heads)], 1))
            dv = dot(weights.astype(jnp.bfloat16), g, TN)
            for at in range(back // span, block + 1):
                piece = dv[at * span - back : (at + 1) * span - back]
                dv_parts[at] = piece if dv_parts[at] is None else dv_parts[at] + piece
        dq, dv = jnp.concatenate(dq_parts, 0), jnp.concatenate(dv_parts, 0)
        dv_hi = dv.astype(jnp.bfloat16)
        dv_lo = (dv - dv_hi.astype(jnp.float32)).astype(jnp.bfloat16)
        pull_q = dot(uq, dq, NT)
        pull_v = dot(uv, dv_hi, NT) + dot(uv, dv_lo, NT)
        pull_v_hi = pull_v.astype(jnp.bfloat16)
        pull_v_lo = (pull_v - pull_v_hi.astype(jnp.float32)).astype(jnp.bfloat16)
        pulls[:, rows] = jnp.concatenate([pull_q.astype(jnp.bfloat16), pull_v_hi, pull_v_lo], 0)
        sums = sums + dot(extra, jnp.concatenate([dq, dv_hi, dv_lo], 1), TN)

    gb_out[:, :group] = sums[:rank, :group]
    gb_out[:, group:] = sums[rank : 2 * rank, group : group + HEAD_SIZE] + sums[rank : 2 * rank, group + HEAD_SIZE :]
    part = feats // parts
    for index in range(parts):
        piece = dot(pulls[...], x_all[:, index * part : (index + 1) * part])
        ga_out[index, :rank] = piece[:rank].astype(ga_out.dtype)
        ga_out[index, rank:] = (piece[rank : 2 * rank] + piece[2 * rank :]).astype(ga_out.dtype)


def attend(place, up_q, up_v, gathered, plan):
    feats, heads, tokens, parts, seq = (plan[k] for k in ("feats", "heads", "tokens", "parts", "seq"))
    rank = up_q.shape[0]
    wide = (heads + 2) * HEAD_SIZE
    x_plan, x_arrays = zip(*gathered["x"])
    g_plan, g_arrays = zip(*gathered["g"])
    w_arrays, shards = [], []
    for offset, chunks in gathered["w"]:
        shards.append((offset, []))
        for array, part, at in chunks:
            index = next((i for i, known in enumerate(w_arrays) if known is array), len(w_arrays))
            w_arrays += [array] if index == len(w_arrays) else []
            shards[-1][1].append((index, part, at))
    depth = w_arrays[-1].shape[0]
    plan = dict(plan, x=x_plan, g=g_plan, shards=shards, depth=depth)
    base = pl.pallas_call(
        functools.partial(project_kernel, plan),
        out_shape=jax.ShapeDtypeStruct((tokens, wide), jnp.float32),
        in_specs=[SMEM, VMEM, VMEM] + [ANY] * (len(x_arrays) + len(w_arrays)),
        out_specs=VMEM,
        scratch_shapes=[
            pltpu.VMEM((tokens, feats + LANES), jnp.bfloat16),
            pltpu.VMEM((len(shards) * depth, wide), jnp.bfloat16),
            pltpu.SemaphoreType.DMA((len(x_arrays) + 2 * len(shards),)),
        ],
        cost_estimate=pl.CostEstimate(flops=0, bytes_accessed=0, transcendentals=0),
        compiler_params=PARAMS,
        name="project",
    )(place, up_q, up_v, *x_arrays, *w_arrays)

    offset, chunks = gathered["last"] or (None, [])
    plan["last"] = None if offset is None else (offset, [chunk[1:] for chunk in chunks])
    last = [chunks[0][0]] if chunks else []
    return pl.pallas_call(
        functools.partial(attend_kernel, plan),
        out_shape=[
            jax.ShapeDtypeStruct((parts, 2 * rank, feats // parts), jnp.bfloat16),
            jax.ShapeDtypeStruct((rank, (heads + 1) * HEAD_SIZE), jnp.float32),
        ],
        in_specs=[SMEM, VMEM, VMEM]
        + [ANY] * (1 + len(x_arrays) + len(g_arrays))
        + [ANY] * len(last),
        out_specs=[VMEM] * 2,
        scratch_shapes=[
            pltpu.VMEM((tokens, feats + LANES), jnp.bfloat16),
            pltpu.VMEM((tokens, heads * HEAD_SIZE), jnp.bfloat16),
            pltpu.VMEM((depth, wide) if last else (16, LANES), jnp.bfloat16),
            pltpu.VMEM((tokens, wide), jnp.float32),
            pltpu.VMEM((3 * rank, tokens), jnp.bfloat16),
            pltpu.SemaphoreType.DMA((len(chunks) + tokens // seq + len(x_arrays) + len(g_arrays),)),
        ],
        compiler_params=PARAMS,
        name="attend",
    )(place, up_q, up_v, base, *x_arrays, *g_arrays, *last)


def ringed(value):
    return lax.ppermute(value, "z", [(0, 1), (1, 3), (3, 2), (2, 0)])


def paired_gather(place, qw, kw, vw, heads, norm_args, gradient):
    shard, rows = qw.shape[0], norm_args[0].shape[0]
    mine = lax.axis_index(GROUP)
    kept, given = pack_weights(mine, qw, kw, vw, heads)
    near, beside = join_rows(lax.axis_index("c"), kept, swapped(given, ("c",), 1))
    far = swapped(beside, ("y",), 1)
    normed, later = norm_tokens(*norm_args, 2, beside)
    c_tokens, x_tokens = swapped(normed, ("c",), 1), swapped(normed, ("ctx",), 1)
    (near_1,) = fence((ringed(near),), wait_us=6)
    later, gradient = fence((later, gradient), far, near_1)
    y_tokens = swapped(later, ("y",), 1)
    hop_1 = jnp.concatenate([near_1, ringed(far)], 0)

    hop_2 = ringed(hop_1)
    half = rows // 2
    far_low, far_high = swapped(x_tokens[:half], ("y",), 1), swapped(y_tokens[half:], ("ctx",), 1)
    xc_tokens = swapped(x_tokens, ("c",), 1)
    (gradient,) = fence((gradient,), hop_1, xc_tokens)
    gradient = lax.all_to_all(gradient, GROUP, 0, 0, tiled=True)

    hop_3 = ringed(hop_2)
    (y_tokens,) = fence((y_tokens,), hop_2)
    yc_tokens, farc_low, farc_high = (swapped(value, ("c",), 1) for value in (y_tokens, far_low, far_high))

    def weight_columns(back):
        def columns(p):
            at = (p[1] ^ (p[1] >> 1)) - back + 4 & 3
            return (at ^ (at >> 1)) * 4 * shard

        return columns

    def token_rows(step, skip=0):
        return lambda p: (step & 3) * 2 * rows + ((p[0] >> 2) ^ (step >> 2)) * rows + skip

    def source(step):
        return lambda p: p[0] ^ step

    size = 2 * shard

    def ordered(first, second):
        return [
            (first, slice(0, size), lambda p: (p[0] & 2) * shard),
            (second, slice(-size, None), lambda p: (2 - (p[0] & 2)) * shard),
        ]

    pieces = [(0, 0, normed), (1, 0, c_tokens), (2, 0, y_tokens), (3, 0, yc_tokens), (4, 0, x_tokens)]
    pieces += [(5, 0, xc_tokens), (6, 0, far_low), (6, half, far_high), (7, 0, farc_low), (7, half, farc_high)]
    return {
        "w": [
            (weight_columns(0), ordered(near, far)),
            (weight_columns(1), ordered(hop_1, hop_1)),
            (weight_columns(2), ordered(hop_2, hop_2)),
        ],
        "last": (weight_columns(3), ordered(hop_3, hop_3)),
        "x": [((token_rows(step, skip), step & 3, None), value) for step, skip, value in pieces],
        "g": [((token_rows(step), step & 3, source(step)), gradient) for step in range(8)],
    }


def on_device(
    tokens,
    trace_index,
    input_norm_scale,
    query_weight,
    key_weight,
    value_weight,
    query_down_weight,
    query_up_weight,
    value_down_weight,
    value_up_weight,
    output_gradient,
):
    rows, feats = tokens.shape[1:]
    heads_kv = key_weight.shape[1] // HEAD_SIZE
    heads = query_weight.shape[1] // HEAD_SIZE // heads_kv
    group = heads * HEAD_SIZE
    rank = query_up_weight.shape[0]
    sizes = [lax.axis_size(axis) for axis in GROUP]
    parts = math.prod(sizes)
    shards = lax.axis_size("z")
    paired = sizes == [2, 2, 2] and shards == 4
    mine = lax.axis_index(GROUP)
    place = jnp.stack([mine, lax.axis_index("z")]).astype(jnp.int32)

    norm_args = (
        tokens.reshape(rows, feats),
        trace_index.reshape(1, rows),
        input_norm_scale,
        query_down_weight.T,
        value_down_weight.T,
    )
    gradient = jnp.moveaxis(output_gradient.reshape(rows, parts, group), 1, 0)
    if paired:
        gathered = paired_gather(
            place, query_weight, key_weight, value_weight, heads, norm_args, gradient
        )
    else:
        shard = query_weight.shape[0]
        split = [w.reshape(shard, parts, -1) for w in (query_weight, key_weight, value_weight)]
        columns = jnp.moveaxis(jnp.concatenate(split, -1), 1, 0)
        per = parts // sizes[0]
        columns = lax.dynamic_slice_in_dim(columns, lax.axis_index("ctx") * per, per, 0)
        columns = lax.all_to_all(columns, ("y", "c"), 0, 0, tiled=True).reshape(per * shard, -1)
        weights = lax.all_gather(columns, "z", axis=0, tiled=True)
        normed = lax.all_gather(norm_tokens(*norm_args, 1)[0], ("y", "c", "ctx"), axis=0, tiled=True)
        gradient = lax.all_to_all(gradient, GROUP, 0, 0, tiled=True)
        gradient = gradient.reshape(sizes[0], per, rows, group)
        gradient = jnp.moveaxis(gradient, 0, 1).reshape(parts * rows, group)
        gathered = {
            "w": [(lambda p: 0, [(weights, slice(None), lambda p: 0)])],
            "last": None,
            "x": [((lambda p: 0, 0, None), normed)],
            "g": [((lambda p: 0, 0, None), gradient)],
        }

    plan = {
        "feats": feats,
        "heads": heads,
        "seq": sizes[0] * rows,
        "window": 2 * rows,
        "span": min(sizes[0], 2) * rows,
        "tokens": parts * rows,
        "parts": parts,
    }
    ga, gb = attend(place, query_up_weight, value_up_weight, gathered, plan)

    coefficient = ADAPTER_NAME / math.sqrt(parts * shards * rows)
    part = jnp.sum(lax.all_to_all(ga, GROUP, 0, 0, tiled=True).astype(jnp.float32), 0)
    mixed = jnp.concatenate([part, gb], 0).astype(jnp.bfloat16)
    if paired:
        for step in (1, 2):
            mixed = add_wide(mixed, swapped(mixed, ("z",), step)).astype(jnp.bfloat16)
    else:
        mixed = lax.psum(mixed.astype(jnp.float32), "z")
    scaled = (mixed.astype(jnp.float32) * coefficient).astype(jnp.bfloat16)
    chips = ("ctx", "y")
    scaled = [scaled] + [swapped(scaled, chips, step) for step in range(1, sizes[0] * sizes[1])]
    if sizes[2] == 2:
        scaled = [piece for value in scaled for piece in (value, swapped(value, ("c",), 1))]
    for bit in range(parts.bit_length() - 1):
        one = (mine >> bit) & 1 == 1
        scaled = [jnp.where(one, scaled[at ^ (1 << bit)], scaled[at]) for at in range(parts)]
    scaled = [value.astype(jnp.float32) for value in scaled]
    aq, av, bq, bv = (
        jnp.concatenate([value[rows_of, columns] for value in scaled], 1)
        for rows_of, columns in (
            (slice(0, rank), slice(None)),
            (slice(rank, 2 * rank), slice(None)),
            (slice(2 * rank, None), slice(0, group)),
            (slice(2 * rank, None), slice(group, None)),
        )
    )
    return aq.T, bq, av.T, bv


def solution(mesh):
    groups, ctx, fsdp = (mesh.shape[name] for name in ("groups", "ctx", "fsdp"))

    def run(*args):
        heads_kv = args[4].shape[1] // HEAD_SIZE
        share = heads_kv // ctx
        cores = 2 if share % 2 == 0 else 1
        split = (groups, ctx, fsdp // share, share // cores, cores)
        finer = Mesh(mesh.devices.reshape(split), ("groups", "ctx", "z", "y", "c"))
        whole = ("z", "y", "c")
        sequences = ("groups",) + whole
        by_rows = P(whole, None)
        by_tokens = P(sequences, "ctx", None)
        out = P("groups", None)
        return jax.shard_map(
            on_device,
            mesh=finer,
            in_specs=(
                by_tokens, P(sequences, "ctx"), P(), by_rows, by_rows, by_rows, P(), P(), P(), P(), by_tokens
            ),
            out_specs=(out, out, out, out),
            check_vma=False,
        )(*args)

    return run
```

```python
import functools
import math

import jax
import jax.numpy as jnp
from jax import lax
from jax.experimental import pallas as pl
from jax.experimental.pallas import tpu as pltpu
from jax.sharding import Mesh
from jax.sharding import PartitionSpec as P

HEAD_SIZE = 128
LANES = 128

CAP = 50.0
QSCALE = 1.0 / 12.0
ADAPTER_NAME = 0.5
EPS = 1e-06

GROUP = ("ctx", "y", "c")
ANY = pl.BlockSpec(memory_space=pl.ANY)
VMEM = pl.BlockSpec(memory_space=pltpu.VMEM)
SMEM = pl.BlockSpec(memory_space=pltpu.SMEM)
PARAMS = pltpu.CompilerParams(vmem_limit_bytes=63 * 2**20)

NT = (((1,), (1,)), ((), ()))
TN = (((0,), (0,)), ((), ()))


def dot(a, b, dims=(((1,), (0,)), ((), ()))):
    return lax.dot_general(a, b, dims, preferred_element_type=jnp.float32)


def add_wide(first, second):
    return first.astype(jnp.float32) + second.astype(jnp.float32)


def swapped(value, axes, distance):
    count = 1
    for axis in axes:
        count *= lax.axis_size(axis)
    return lax.ppermute(value, axes, [(i, i ^ distance) for i in range(count)])


def pack_weights(mine, qw, kw, vw, heads):
    def columns(owner):
        wide = heads * HEAD_SIZE
        parts = [lax.dynamic_slice_in_dim(qw, owner * wide, wide, 1)]
        parts += [lax.dynamic_slice_in_dim(w, owner * HEAD_SIZE, HEAD_SIZE, 1) for w in (kw, vw)]
        return jnp.concatenate(parts, 1)

    return [jnp.stack([columns(mine ^ (2 * chip + core)) for chip in range(2)]) for core in range(2)]


def join_rows(core, kept, got):
    first, second = jnp.where(core == 0, kept, got), jnp.where(core == 0, got, kept)
    return [jnp.concatenate([first[chip], second[chip]], 0) for chip in range(2)]


def fence_kernel(*refs):
    pass


def fence(values, *earlier, wait_us=0):
    count = len(values)
    return pl.pallas_call(
        fence_kernel,
        out_shape=[jax.ShapeDtypeStruct(value.shape, value.dtype) for value in values],
        in_specs=[ANY] * (count + len(earlier)),
        out_specs=[ANY] * count,
        input_output_aliases={i: i for i in range(count)},
        cost_estimate=pl.CostEstimate(
            flops=wait_us * 10**9, bytes_accessed=wait_us * 3 * 10**6, transcendentals=0
        ),
        compiler_params=pltpu.CompilerParams(vmem_limit_bytes=60 * 2**20),
        name="fence",
    )(*values, *earlier)


def norm_kernel(copies, tokens, trace, gain, down_q, down_v, *rest):
    flt = tokens[...].astype(jnp.float32)
    meansq = jnp.mean(flt * flt, axis=-1, keepdims=True)
    normed = (flt * lax.rsqrt(meansq + EPS) * gain[...].astype(jnp.float32)[None, :]).astype(jnp.bfloat16)
    rows, feats = normed.shape
    rank = down_q.shape[0]
    low_q = dot(normed, down_q[...], NT)
    low_v = dot(normed, down_v[...], NT)
    square = (rows, rows)
    diagonal = lax.broadcasted_iota(jnp.int32, square, 0) == lax.broadcasted_iota(jnp.int32, square, 1)
    ids = jnp.sum(jnp.where(diagonal, trace[...].astype(jnp.float32), 0.0), axis=1, keepdims=True)
    filler = jnp.zeros((rows, LANES - 2 * rank - 1), jnp.float32)
    extra = jnp.concatenate([low_q, low_v, ids, filler], 1).astype(jnp.bfloat16)
    for out in rest[-copies:]:
        out[:, :feats] = normed
        out[:, feats:] = extra


def norm_tokens(tokens, trace, gain, down_q, down_v, copies, *earlier):
    rows, feats = tokens.shape
    return pl.pallas_call(
        functools.partial(norm_kernel, copies),
        out_shape=[jax.ShapeDtypeStruct((rows, feats + LANES), jnp.bfloat16)] * copies,
        in_specs=[VMEM] * 5 + [ANY] * len(earlier),
        out_specs=[VMEM] * copies,
        compiler_params=pltpu.CompilerParams(vmem_limit_bytes=16 * 2**20),
        name="norm_tokens",
    )(tokens, trace, gain, down_q, down_v, *earlier)


class Loads:
    def __init__(self, sems):
        self.sems, self.copies = sems, []

    def add(self, place, pieces, target):
        for piece, src in pieces:
            offset, sequence, choice = piece
            begin = pl.multiple_of(offset(place), 16)
            rows = src.shape[-2]
            if choice is not None and len(src.shape) == 3:
                src = src.at[choice(place)]
            self.add_copy(sequence, src, target.at[pl.ds(begin, rows), :])

    def add_copy(self, sequence, src, target):
        self.copies.append((sequence, pltpu.make_async_copy(src, target, self.sems.at[len(self.copies)])))

    def start(self, sequence):
        for needed, copy in self.copies:
            if needed == sequence:
                copy.start()

    def wait(self, sequence):
        for needed, copy in self.copies:
            if needed == sequence:
                copy.wait()


def project_kernel(plan, *refs):
    n_x, shards = len(plan["x"]), plan["shards"]
    place, up_q, up_v = refs[:3]
    x_refs, w_refs, rest = refs[3 : 3 + n_x], refs[3 + n_x : -4], refs[-4:]
    out, x_all, w_all, sems = rest
    feats, heads, seq = plan["feats"], plan["heads"], plan["seq"]
    rank, group = up_q.shape[0], heads * HEAD_SIZE
    depth = plan["depth"]

    loads = Loads(sems)
    for index, (_, chunks) in enumerate(shards):
        for number, part, at in chunks:
            piece = (lambda p, at=at, index=index: index * depth + at(p), 0, None)
            src = w_refs[number]
            rows = src.shape[0]
            src = src.at[slice(*part.indices(rows))]
            loads.add(place, [(piece, src)], w_all)
    loads.add(place, list(zip(plan["x"], x_refs)), x_all)
    loads.start(0)

    mine = place[0]
    uq = up_q[:, pl.ds(pl.multiple_of(mine * group, group), group)]
    uv = up_v[:, pl.ds(pl.multiple_of(mine * HEAD_SIZE, HEAD_SIZE), HEAD_SIZE)]
    zero = functools.partial(jnp.zeros, dtype=jnp.float32)
    top = jnp.concatenate([ADAPTER_NAME * uq.astype(jnp.float32), zero((rank, 2 * HEAD_SIZE))], 1)
    low = jnp.concatenate([zero((rank, group + HEAD_SIZE)), ADAPTER_NAME * uv.astype(jnp.float32)], 1)
    pad = zero((LANES - 2 * rank, group + 2 * HEAD_SIZE))
    ups = jnp.concatenate([top, low, pad], 0).astype(jnp.bfloat16)

    for index in range(x_all.shape[0] // seq):
        loads.start(index + 1)
        loads.wait(index)
        rows = pl.ds(index * seq, seq)
        total = dot(x_all[rows, feats:], ups)
        for number, (offset, _) in enumerate(shards):
            columns = pl.ds(pl.multiple_of(offset(place), LANES), depth)
            total = total + dot(x_all[rows, columns], w_all[number * depth : (number + 1) * depth])
        out[rows, :] = total


def attend_kernel(plan, *refs):
    n_x, n_g, last = len(plan["x"]), len(plan["g"]), plan["last"]
    place, up_q, up_v, base = refs[:4]
    x_refs, g_refs = refs[4 : 4 + n_x], refs[4 + n_x : 4 + n_x + n_g]
    w_refs, rest = refs[4 + n_x + n_g : -8], refs[-8:]
    ga_out, gb_out, x_all, g_all, w_all, base_all, pulls, sems = rest

    feats, heads, seq, window, depth = (plan[k] for k in ("feats", "heads", "seq", "window", "depth"))
    rank, parts = up_q.shape[0], plan["parts"]
    group = heads * HEAD_SIZE
    tokens = x_all.shape[0]
    sequences = tokens // seq

    loads = Loads(sems)
    for index in range(sequences):
        rows = pl.ds(index * seq, seq)
        loads.add_copy(index, base.at[rows, :], base_all.at[rows, :])
        for pieces, sources, target in ((plan["x"], x_refs, x_all), (plan["g"], g_refs, g_all)):
            chosen = [(piece, src) for piece, src in zip(pieces, sources) if piece[1] == index]
            loads.add(place, chosen, target)
    if last is not None:
        offset, chunks = last
        for part, at in chunks:
            src = w_refs[0].at[slice(*part.indices(depth))]
            target = w_all.at[pl.ds(pl.multiple_of(at(place), 16), src.shape[0]), :]
            loads.add_copy(0, src, target)
    loads.start(0)

    mine = place[0]
    uq = up_q[:, pl.ds(pl.multiple_of(mine * group, group), group)]
    uv = up_v[:, pl.ds(pl.multiple_of(mine * HEAD_SIZE, HEAD_SIZE), HEAD_SIZE)]
    id_row = jnp.where(lax.broadcasted_iota(jnp.int32, (8, LANES), 1) == 2 * rank, 1.0, 0.0).astype(jnp.bfloat16)
    span = plan["span"]
    blocks = seq // span
    sums = jnp.zeros((LANES, group + 2 * HEAD_SIZE), jnp.float32)

    for index in range(sequences):
        loads.start(index + 1)
        loads.wait(index)
        rows = pl.ds(index * seq, seq)
        qkv = base_all[rows, :]
        if last is not None:
            columns = pl.ds(pl.multiple_of(offset(place), LANES), depth)
            qkv = qkv + dot(x_all[rows, columns], w_all[...])
        qkv = qkv.astype(jnp.bfloat16)
        extra = x_all[rows, feats:]
        ids_key = dot(id_row, extra, NT)[:1]
        ids_query = extra[:, 2 * rank : 2 * rank + 1].astype(jnp.float32)
        keys = qkv[:, group : group + HEAD_SIZE]
        values = qkv[:, group + HEAD_SIZE :]
        grads = g_all[rows, :]
        dq_parts, dv_parts = [], [None] * blocks
        for block in range(blocks):
            lo, hi = block * span, (block + 1) * span
            back = max(0, lo - window)
            kb, vb = keys[back:hi], values[back:hi]
            shape = (span, hi - back)
            pos_q = lax.broadcasted_iota(jnp.int32, shape, 0) + lo
            pos_k = lax.broadcasted_iota(jnp.int32, shape, 1) + back
            mask = (pos_k <= pos_q) & (pos_k > pos_q - window)
            mask = mask & (ids_query[lo:hi] == ids_key[:, back:hi])
            masks = jnp.concatenate([jnp.where(mask, 1.0, 0.0)] * heads, 0)
            q, g = (
                jnp.concatenate([x[lo:hi, h * HEAD_SIZE : (h + 1) * HEAD_SIZE] for h in range(heads)], 0)
                for x in (qkv, grads)
            )
            t = jnp.tanh(dot(q, kb, NT) * (QSCALE / CAP))
            dweight = dot(g, vb, NT)
            expo = masks * jnp.exp2((CAP * math.log2(math.e)) * t)
            share = 1.0 / jnp.sum(expo, axis=-1, keepdims=True)
            weights = expo * share
            delta = jnp.sum(expo * dweight, axis=-1, keepdims=True) * share
            dscore = (weights * (dweight - delta) * (1.0 - t * t)).astype(jnp.bfloat16)
            dq = (dot(dscore, kb) * QSCALE).astype(jnp.bfloat16)
            dq_parts.append(jnp.concatenate([dq[h * span : (h + 1) * span] for h in range(heads)], 1))
            dv = dot(weights.astype(jnp.bfloat16), g, TN)
            for at in range(back // span, block + 1):
                piece = dv[at * span - back : (at + 1) * span - back]
                dv_parts[at] = piece if dv_parts[at] is None else dv_parts[at] + piece
        dq, dv = jnp.concatenate(dq_parts, 0), jnp.concatenate(dv_parts, 0)
        dv_hi = dv.astype(jnp.bfloat16)
        dv_lo = (dv - dv_hi.astype(jnp.float32)).astype(jnp.bfloat16)
        pull_q = dot(uq, dq, NT)
        pull_v = dot(uv, dv_hi, NT) + dot(uv, dv_lo, NT)
        pull_v_hi = pull_v.astype(jnp.bfloat16)
        pull_v_lo = (pull_v - pull_v_hi.astype(jnp.float32)).astype(jnp.bfloat16)
        pulls[:, rows] = jnp.concatenate([pull_q.astype(jnp.bfloat16), pull_v_hi, pull_v_lo], 0)
        sums = sums + dot(extra, jnp.concatenate([dq, dv_hi, dv_lo], 1), TN)

    gb_out[:, :group] = sums[:rank, :group]
    gb_out[:, group:] = sums[rank : 2 * rank, group : group + HEAD_SIZE] + sums[rank : 2 * rank, group + HEAD_SIZE :]
    part = feats // parts
    for index in range(parts):
        piece = dot(pulls[...], x_all[:, index * part : (index + 1) * part])
        ga_out[index, :rank] = piece[:rank].astype(ga_out.dtype)
        ga_out[index, rank:] = (piece[rank : 2 * rank] + piece[2 * rank :]).astype(ga_out.dtype)


def attend(place, up_q, up_v, gathered, plan):
    feats, heads, tokens, parts, seq = (plan[k] for k in ("feats", "heads", "tokens", "parts", "seq"))
    rank = up_q.shape[0]
    wide = (heads + 2) * HEAD_SIZE
    x_plan, x_arrays = zip(*gathered["x"])
    g_plan, g_arrays = zip(*gathered["g"])
    w_arrays, shards = [], []
    for offset, chunks in gathered["w"]:
        shards.append((offset, []))
        for array, part, at in chunks:
            index = next((i for i, known in enumerate(w_arrays) if known is array), len(w_arrays))
            w_arrays += [array] if index == len(w_arrays) else []
            shards[-1][1].append((index, part, at))
    depth = w_arrays[-1].shape[0]
    plan = dict(plan, x=x_plan, g=g_plan, shards=shards, depth=depth)
    base = pl.pallas_call(
        functools.partial(project_kernel, plan),
        out_shape=jax.ShapeDtypeStruct((tokens, wide), jnp.float32),
        in_specs=[SMEM, VMEM, VMEM] + [ANY] * (len(x_arrays) + len(w_arrays)),
        out_specs=VMEM,
        scratch_shapes=[
            pltpu.VMEM((tokens, feats + LANES), jnp.bfloat16),
            pltpu.VMEM((len(shards) * depth, wide), jnp.bfloat16),
            pltpu.SemaphoreType.DMA((len(x_arrays) + 2 * len(shards),)),
        ],
        cost_estimate=pl.CostEstimate(flops=0, bytes_accessed=0, transcendentals=0),
        compiler_params=PARAMS,
        name="project",
    )(place, up_q, up_v, *x_arrays, *w_arrays)

    offset, chunks = gathered["last"] or (None, [])
    plan["last"] = None if offset is None else (offset, [chunk[1:] for chunk in chunks])
    last = [chunks[0][0]] if chunks else []
    return pl.pallas_call(
        functools.partial(attend_kernel, plan),
        out_shape=[
            jax.ShapeDtypeStruct((parts, 2 * rank, feats // parts), jnp.bfloat16),
            jax.ShapeDtypeStruct((rank, (heads + 1) * HEAD_SIZE), jnp.float32),
        ],
        in_specs=[SMEM, VMEM, VMEM]
        + [ANY] * (1 + len(x_arrays) + len(g_arrays))
        + [ANY] * len(last),
        out_specs=[VMEM] * 2,
        scratch_shapes=[
            pltpu.VMEM((tokens, feats + LANES), jnp.bfloat16),
            pltpu.VMEM((tokens, heads * HEAD_SIZE), jnp.bfloat16),
            pltpu.VMEM((depth, wide) if last else (16, LANES), jnp.bfloat16),
            pltpu.VMEM((tokens, wide), jnp.float32),
            pltpu.VMEM((3 * rank, tokens), jnp.bfloat16),
            pltpu.SemaphoreType.DMA((len(chunks) + tokens // seq + len(x_arrays) + len(g_arrays),)),
        ],
        compiler_params=PARAMS,
        name="attend",
    )(place, up_q, up_v, base, *x_arrays, *g_arrays, *last)


def ringed(value):
    steps = ((0, 1), (1, 3), (3, 2), (2, 0))
    pairs = [(2 * a, 2 * b) for a, b in steps] + [(2 * b + 1, 2 * a + 1) for a, b in steps]
    return lax.ppermute(value, ("z", "c"), pairs)


def paired_gather(place, qw, kw, vw, heads, norm_args, gradient):
    shard, rows = qw.shape[0], norm_args[0].shape[0]
    mine = lax.axis_index(GROUP)
    kept, given = pack_weights(mine, qw, kw, vw, heads)
    near, beside = join_rows(lax.axis_index("c"), kept, swapped(given, ("c",), 1))
    far = swapped(beside, ("y",), 1)
    normed, later = norm_tokens(*norm_args, 2, beside)
    c_tokens, x_tokens = swapped(normed, ("c",), 1), swapped(normed, ("ctx",), 1)
    (near_1,) = fence((ringed(near),), wait_us=6)
    later, gradient = fence((later, gradient), far, near_1)
    y_tokens = swapped(later, ("y",), 1)
    hop_1 = jnp.concatenate([near_1, ringed(far)], 0)

    hop_2 = ringed(hop_1)
    half = rows // 2
    far_low, far_high = swapped(x_tokens[:half], ("y",), 1), swapped(y_tokens[half:], ("ctx",), 1)
    xc_tokens = swapped(x_tokens, ("c",), 1)
    (gradient,) = fence((gradient,), hop_1, xc_tokens)
    gradient = lax.all_to_all(gradient, GROUP, 0, 0, tiled=True)

    hop_3 = ringed(hop_2)
    (y_tokens,) = fence((y_tokens,), hop_2)
    yc_tokens, farc_low, farc_high = (swapped(value, ("c",), 1) for value in (y_tokens, far_low, far_high))

    def weight_columns(back):
        def columns(p):
            at = (p[1] ^ (p[1] >> 1)) - back * (1 - 2 * (p[0] & 1)) + 4 & 3
            return (at ^ (at >> 1)) * 4 * shard

        return columns

    def token_rows(step, skip=0):
        return lambda p: (step & 3) * 2 * rows + ((p[0] >> 2) ^ (step >> 2)) * rows + skip

    def source(step):
        return lambda p: p[0] ^ step

    size = 2 * shard

    def ordered(first, second):
        return [
            (first, slice(0, size), lambda p: (p[0] & 2) * shard),
            (second, slice(-size, None), lambda p: (2 - (p[0] & 2)) * shard),
        ]

    pieces = [(0, 0, normed), (1, 0, c_tokens), (2, 0, y_tokens), (3, 0, yc_tokens), (4, 0, x_tokens)]
    pieces += [(5, 0, xc_tokens), (6, 0, far_low), (6, half, far_high), (7, 0, farc_low), (7, half, farc_high)]
    return {
        "w": [
            (weight_columns(0), ordered(near, far)),
            (weight_columns(1), ordered(hop_1, hop_1)),
            (weight_columns(2), ordered(hop_2, hop_2)),
        ],
        "last": (weight_columns(3), ordered(hop_3, hop_3)),
        "x": [((token_rows(step, skip), step & 3, None), value) for step, skip, value in pieces],
        "g": [((token_rows(step), step & 3, source(step)), gradient) for step in range(8)],
    }


def on_device(
    tokens,
    trace_index,
    input_norm_scale,
    query_weight,
    key_weight,
    value_weight,
    query_down_weight,
    query_up_weight,
    value_down_weight,
    value_up_weight,
    output_gradient,
):
    rows, feats = tokens.shape[1:]
    heads_kv = key_weight.shape[1] // HEAD_SIZE
    heads = query_weight.shape[1] // HEAD_SIZE // heads_kv
    group = heads * HEAD_SIZE
    rank = query_up_weight.shape[0]
    sizes = [lax.axis_size(axis) for axis in GROUP]
    parts = math.prod(sizes)
    shards = lax.axis_size("z")
    paired = sizes == [2, 2, 2] and shards == 4
    mine = lax.axis_index(GROUP)
    place = jnp.stack([mine, lax.axis_index("z")]).astype(jnp.int32)

    norm_args = (
        tokens.reshape(rows, feats),
        trace_index.reshape(1, rows),
        input_norm_scale,
        query_down_weight.T,
        value_down_weight.T,
    )
    gradient = jnp.moveaxis(output_gradient.reshape(rows, parts, group), 1, 0)
    if paired:
        gathered = paired_gather(
            place, query_weight, key_weight, value_weight, heads, norm_args, gradient
        )
    else:
        shard = query_weight.shape[0]
        split = [w.reshape(shard, parts, -1) for w in (query_weight, key_weight, value_weight)]
        columns = jnp.moveaxis(jnp.concatenate(split, -1), 1, 0)
        per = parts // sizes[0]
        columns = lax.dynamic_slice_in_dim(columns, lax.axis_index("ctx") * per, per, 0)
        columns = lax.all_to_all(columns, ("y", "c"), 0, 0, tiled=True).reshape(per * shard, -1)
        weights = lax.all_gather(columns, "z", axis=0, tiled=True)
        normed = lax.all_gather(norm_tokens(*norm_args, 1)[0], ("y", "c", "ctx"), axis=0, tiled=True)
        gradient = lax.all_to_all(gradient, GROUP, 0, 0, tiled=True)
        gradient = gradient.reshape(sizes[0], per, rows, group)
        gradient = jnp.moveaxis(gradient, 0, 1).reshape(parts * rows, group)
        gathered = {
            "w": [(lambda p: 0, [(weights, slice(None), lambda p: 0)])],
            "last": None,
            "x": [((lambda p: 0, 0, None), normed)],
            "g": [((lambda p: 0, 0, None), gradient)],
        }

    plan = {
        "feats": feats,
        "heads": heads,
        "seq": sizes[0] * rows,
        "window": 2 * rows,
        "span": min(sizes[0], 2) * rows,
        "tokens": parts * rows,
        "parts": parts,
    }
    ga, gb = attend(place, query_up_weight, value_up_weight, gathered, plan)

    coefficient = ADAPTER_NAME / math.sqrt(parts * shards * rows)
    part = jnp.sum(lax.all_to_all(ga, GROUP, 0, 0, tiled=True).astype(jnp.float32), 0)
    mixed = jnp.concatenate([part, gb], 0).astype(jnp.bfloat16)
    if paired:
        for step in (1, 2):
            mixed = add_wide(mixed, swapped(mixed, ("z",), step)).astype(jnp.bfloat16)
    else:
        mixed = lax.psum(mixed.astype(jnp.float32), "z")
    scaled = (mixed.astype(jnp.float32) * coefficient).astype(jnp.bfloat16)
    chips = ("ctx", "y")
    scaled = [scaled] + [swapped(scaled, chips, step) for step in range(1, sizes[0] * sizes[1])]
    if sizes[2] == 2:
        scaled = [piece for value in scaled for piece in (value, swapped(value, ("c",), 1))]
    for bit in range(parts.bit_length() - 1):
        one = (mine >> bit) & 1 == 1
        scaled = [jnp.where(one, scaled[at ^ (1 << bit)], scaled[at]) for at in range(parts)]
    scaled = [value.astype(jnp.float32) for value in scaled]
    aq, av, bq, bv = (
        jnp.concatenate([value[rows_of, columns] for value in scaled], 1)
        for rows_of, columns in (
            (slice(0, rank), slice(None)),
            (slice(rank, 2 * rank), slice(None)),
            (slice(2 * rank, None), slice(0, group)),
            (slice(2 * rank, None), slice(group, None)),
        )
    )
    return aq.T, bq, av.T, bv


def solution(mesh):
    groups, ctx, fsdp = (mesh.shape[name] for name in ("groups", "ctx", "fsdp"))

    def run(*args):
        heads_kv = args[4].shape[1] // HEAD_SIZE
        share = heads_kv // ctx
        cores = 2 if share % 2 == 0 else 1
        split = (groups, ctx, fsdp // share, share // cores, cores)
        finer = Mesh(mesh.devices.reshape(split), ("groups", "ctx", "z", "y", "c"))
        whole = ("z", "y", "c")
        sequences = ("groups",) + whole
        by_rows = P(whole, None)
        by_tokens = P(sequences, "ctx", None)
        out = P("groups", None)
        return jax.shard_map(
            on_device,
            mesh=finer,
            in_specs=(
                by_tokens, P(sequences, "ctx"), P(), by_rows, by_rows, by_rows, P(), P(), P(), P(), by_tokens
            ),
            out_specs=(out, out, out, out),
            check_vma=False,
        )(*args)

    return run
```

```python
import functools
import math

import jax
import jax.numpy as jnp
from jax import lax
from jax.experimental import pallas as pl
from jax.experimental.pallas import tpu as pltpu
from jax.sharding import Mesh
from jax.sharding import PartitionSpec as P

HEAD_SIZE = 128
LANES = 128

CAP = 50.0
QSCALE = 1.0 / 12.0
ADAPTER_NAME = 0.5
EPS = 1e-06

GROUP = ("ctx", "y", "c")
ANY = pl.BlockSpec(memory_space=pl.ANY)
VMEM = pl.BlockSpec(memory_space=pltpu.VMEM)
SMEM = pl.BlockSpec(memory_space=pltpu.SMEM)
PARAMS = pltpu.CompilerParams(vmem_limit_bytes=63 * 2**20)

NT = (((1,), (1,)), ((), ()))
TN = (((0,), (0,)), ((), ()))


def dot(a, b, dims=(((1,), (0,)), ((), ()))):
    return lax.dot_general(a, b, dims, preferred_element_type=jnp.float32)


def add_wide(first, second):
    return first.astype(jnp.float32) + second.astype(jnp.float32)


def swapped(value, axes, distance):
    count = 1
    for axis in axes:
        count *= lax.axis_size(axis)
    return lax.ppermute(value, axes, [(i, i ^ distance) for i in range(count)])


def pack_weights(mine, qw, kw, vw, heads):
    def columns(owner):
        wide = heads * HEAD_SIZE
        parts = [lax.dynamic_slice_in_dim(qw, owner * wide, wide, 1)]
        parts += [lax.dynamic_slice_in_dim(w, owner * HEAD_SIZE, HEAD_SIZE, 1) for w in (kw, vw)]
        return jnp.concatenate(parts, 1)

    return [jnp.stack([columns(mine ^ (2 * chip + core)) for chip in range(2)]) for core in range(2)]


def join_rows(core, kept, got):
    first, second = jnp.where(core == 0, kept, got), jnp.where(core == 0, got, kept)
    return [jnp.concatenate([first[chip], second[chip]], 0) for chip in range(2)]


def fence_kernel(*refs):
    pass


def fence(values, *earlier, wait_us=0):
    count = len(values)
    return pl.pallas_call(
        fence_kernel,
        out_shape=[jax.ShapeDtypeStruct(value.shape, value.dtype) for value in values],
        in_specs=[ANY] * (count + len(earlier)),
        out_specs=[ANY] * count,
        input_output_aliases={i: i for i in range(count)},
        cost_estimate=pl.CostEstimate(
            flops=wait_us * 10**9, bytes_accessed=wait_us * 3 * 10**6, transcendentals=0
        ),
        compiler_params=pltpu.CompilerParams(vmem_limit_bytes=60 * 2**20),
        name="fence",
    )(*values, *earlier)


def norm_kernel(copies, tokens, trace, gain, down_q, down_v, *rest):
    flt = tokens[...].astype(jnp.float32)
    meansq = jnp.mean(flt * flt, axis=-1, keepdims=True)
    normed = (flt * lax.rsqrt(meansq + EPS) * gain[...].astype(jnp.float32)[None, :]).astype(jnp.bfloat16)
    rows, feats = normed.shape
    rank = down_q.shape[0]
    low_q = dot(normed, down_q[...], NT)
    low_v = dot(normed, down_v[...], NT)
    square = (rows, rows)
    diagonal = lax.broadcasted_iota(jnp.int32, square, 0) == lax.broadcasted_iota(jnp.int32, square, 1)
    ids = jnp.sum(jnp.where(diagonal, trace[...].astype(jnp.float32), 0.0), axis=1, keepdims=True)
    filler = jnp.zeros((rows, LANES - 2 * rank - 1), jnp.float32)
    extra = jnp.concatenate([low_q, low_v, ids, filler], 1).astype(jnp.bfloat16)
    for out in rest[-copies:]:
        out[:, :feats] = normed
        out[:, feats:] = extra


def norm_tokens(tokens, trace, gain, down_q, down_v, copies, *earlier):
    rows, feats = tokens.shape
    return pl.pallas_call(
        functools.partial(norm_kernel, copies),
        out_shape=[jax.ShapeDtypeStruct((rows, feats + LANES), jnp.bfloat16)] * copies,
        in_specs=[VMEM] * 5 + [ANY] * len(earlier),
        out_specs=[VMEM] * copies,
        compiler_params=pltpu.CompilerParams(vmem_limit_bytes=16 * 2**20),
        name="norm_tokens",
    )(tokens, trace, gain, down_q, down_v, *earlier)


class Loads:
    def __init__(self, sems):
        self.sems, self.copies = sems, []

    def add(self, place, pieces, target):
        for piece, src in pieces:
            offset, sequence, choice = piece
            begin = pl.multiple_of(offset(place), 16)
            rows = src.shape[-2]
            if choice is not None and len(src.shape) == 3:
                src = src.at[choice(place)]
            self.add_copy(sequence, src, target.at[pl.ds(begin, rows), :])

    def add_copy(self, sequence, src, target):
        self.copies.append((sequence, pltpu.make_async_copy(src, target, self.sems.at[len(self.copies)])))

    def start(self, sequence):
        for needed, copy in self.copies:
            if needed == sequence:
                copy.start()

    def wait(self, sequence):
        for needed, copy in self.copies:
            if needed == sequence:
                copy.wait()


def project_kernel(plan, *refs):
    n_x, shards = len(plan["x"]), plan["shards"]
    place, up_q, up_v = refs[:3]
    x_refs, w_refs, rest = refs[3 : 3 + n_x], refs[3 + n_x : -4], refs[-4:]
    out, x_all, w_all, sems = rest
    feats, heads, seq = plan["feats"], plan["heads"], plan["seq"]
    rank, group = up_q.shape[0], heads * HEAD_SIZE
    depth = plan["depth"]

    loads = Loads(sems)
    for index, (_, chunks) in enumerate(shards):
        for number, part, at in chunks:
            piece = (lambda p, at=at, index=index: index * depth + at(p), 0, None)
            src = w_refs[number]
            rows = src.shape[0]
            src = src.at[slice(*part.indices(rows))]
            loads.add(place, [(piece, src)], w_all)
    loads.add(place, list(zip(plan["x"], x_refs)), x_all)
    loads.start(0)

    mine = place[0]
    uq = up_q[:, pl.ds(pl.multiple_of(mine * group, group), group)]
    uv = up_v[:, pl.ds(pl.multiple_of(mine * HEAD_SIZE, HEAD_SIZE), HEAD_SIZE)]
    zero = functools.partial(jnp.zeros, dtype=jnp.float32)
    top = jnp.concatenate([ADAPTER_NAME * uq.astype(jnp.float32), zero((rank, 2 * HEAD_SIZE))], 1)
    low = jnp.concatenate([zero((rank, group + HEAD_SIZE)), ADAPTER_NAME * uv.astype(jnp.float32)], 1)
    pad = zero((LANES - 2 * rank, group + 2 * HEAD_SIZE))
    ups = jnp.concatenate([top, low, pad], 0).astype(jnp.bfloat16)

    for index in range(x_all.shape[0] // seq):
        loads.start(index + 1)
        loads.wait(index)
        rows = pl.ds(index * seq, seq)
        total = dot(x_all[rows, feats:], ups)
        for number, (offset, _) in enumerate(shards):
            columns = pl.ds(pl.multiple_of(offset(place), LANES), depth)
            total = total + dot(x_all[rows, columns], w_all[number * depth : (number + 1) * depth])
        out[rows, :] = total


def attend_kernel(plan, *refs):
    n_x, n_g, last = len(plan["x"]), len(plan["g"]), plan["last"]
    place, up_q, up_v, base = refs[:4]
    x_refs, g_refs = refs[4 : 4 + n_x], refs[4 + n_x : 4 + n_x + n_g]
    w_refs, rest = refs[4 + n_x + n_g : -8], refs[-8:]
    ga_out, gb_out, x_all, g_all, w_all, base_all, pulls, sems = rest

    feats, heads, seq, window, depth = (plan[k] for k in ("feats", "heads", "seq", "window", "depth"))
    rank, parts = up_q.shape[0], plan["parts"]
    group = heads * HEAD_SIZE
    tokens = x_all.shape[0]
    sequences = tokens // seq

    loads = Loads(sems)
    for index in range(sequences):
        rows = pl.ds(index * seq, seq)
        loads.add_copy(index, base.at[rows, :], base_all.at[rows, :])
        for pieces, sources, target in ((plan["x"], x_refs, x_all), (plan["g"], g_refs, g_all)):
            chosen = [(piece, src) for piece, src in zip(pieces, sources) if piece[1] == index]
            loads.add(place, chosen, target)
    if last is not None:
        offset, chunks = last
        for part, at in chunks:
            src = w_refs[0].at[slice(*part.indices(depth))]
            target = w_all.at[pl.ds(pl.multiple_of(at(place), 16), src.shape[0]), :]
            loads.add_copy(0, src, target)
    loads.start(0)

    mine = place[0]
    uq = up_q[:, pl.ds(pl.multiple_of(mine * group, group), group)]
    uv = up_v[:, pl.ds(pl.multiple_of(mine * HEAD_SIZE, HEAD_SIZE), HEAD_SIZE)]
    id_row = jnp.where(lax.broadcasted_iota(jnp.int32, (8, LANES), 1) == 2 * rank, 1.0, 0.0).astype(jnp.bfloat16)
    span = plan["span"]
    blocks = seq // span
    sums = jnp.zeros((LANES, group + 2 * HEAD_SIZE), jnp.float32)

    for index in range(sequences):
        loads.start(index + 1)
        loads.wait(index)
        rows = pl.ds(index * seq, seq)
        qkv = base_all[rows, :]
        if last is not None:
            columns = pl.ds(pl.multiple_of(offset(place), LANES), depth)
            qkv = qkv + dot(x_all[rows, columns], w_all[...])
        qkv = qkv.astype(jnp.bfloat16)
        extra = x_all[rows, feats:]
        ids_key = dot(id_row, extra, NT)[:1]
        ids_query = extra[:, 2 * rank : 2 * rank + 1].astype(jnp.float32)
        keys = qkv[:, group : group + HEAD_SIZE]
        values = qkv[:, group + HEAD_SIZE :]
        grads = g_all[rows, :]
        dq_parts, dv_parts = [], [None] * blocks
        for block in range(blocks):
            lo, hi = block * span, (block + 1) * span
            back = max(0, lo - window)
            kb, vb = keys[back:hi], values[back:hi]
            shape = (span, hi - back)
            pos_q = lax.broadcasted_iota(jnp.int32, shape, 0) + lo
            pos_k = lax.broadcasted_iota(jnp.int32, shape, 1) + back
            mask = (pos_k <= pos_q) & (pos_k > pos_q - window)
            mask = mask & (ids_query[lo:hi] == ids_key[:, back:hi])
            masks = jnp.concatenate([jnp.where(mask, 1.0, 0.0)] * heads, 0)
            q, g = (
                jnp.concatenate([x[lo:hi, h * HEAD_SIZE : (h + 1) * HEAD_SIZE] for h in range(heads)], 0)
                for x in (qkv, grads)
            )
            t = jnp.tanh(dot(q, kb, NT) * (QSCALE / CAP))
            dweight = dot(g, vb, NT)
            expo = masks * jnp.exp2((CAP * math.log2(math.e)) * t)
            share = 1.0 / jnp.sum(expo, axis=-1, keepdims=True)
            weights = expo * share
            delta = jnp.sum(expo * dweight, axis=-1, keepdims=True) * share
            dscore = (weights * (dweight - delta) * (1.0 - t * t)).astype(jnp.bfloat16)
            dq = (dot(dscore, kb) * QSCALE).astype(jnp.bfloat16)
            dq_parts.append(jnp.concatenate([dq[h * span : (h + 1) * span] for h in range(heads)], 1))
            dv = dot(weights.astype(jnp.bfloat16), g, TN)
            for at in range(back // span, block + 1):
                piece = dv[at * span - back : (at + 1) * span - back]
                dv_parts[at] = piece if dv_parts[at] is None else dv_parts[at] + piece
        dq, dv = jnp.concatenate(dq_parts, 0), jnp.concatenate(dv_parts, 0)
        dv_hi = dv.astype(jnp.bfloat16)
        dv_lo = (dv - dv_hi.astype(jnp.float32)).astype(jnp.bfloat16)
        pull_q = dot(uq, dq, NT)
        pull_v = dot(uv, dv_hi, NT) + dot(uv, dv_lo, NT)
        pull_v_hi = pull_v.astype(jnp.bfloat16)
        pull_v_lo = (pull_v - pull_v_hi.astype(jnp.float32)).astype(jnp.bfloat16)
        pulls[:, rows] = jnp.concatenate([pull_q.astype(jnp.bfloat16), pull_v_hi, pull_v_lo], 0)
        sums = sums + dot(extra, jnp.concatenate([dq, dv_hi, dv_lo], 1), TN)

    gb_out[:, :group] = sums[:rank, :group]
    gb_out[:, group:] = sums[rank : 2 * rank, group : group + HEAD_SIZE] + sums[rank : 2 * rank, group + HEAD_SIZE :]
    part = feats // parts
    for index in range(parts):
        if index % 2 == 0:
            pair = dot(pulls[...], x_all[:, index * part : min(index + 2, parts) * part])
        piece = pair[:, (index % 2) * part : (index % 2 + 1) * part]
        ga_out[index, :rank] = piece[:rank].astype(ga_out.dtype)
        ga_out[index, rank:] = (piece[rank : 2 * rank] + piece[2 * rank :]).astype(ga_out.dtype)


def attend(place, up_q, up_v, gathered, plan):
    feats, heads, tokens, parts, seq = (plan[k] for k in ("feats", "heads", "tokens", "parts", "seq"))
    rank = up_q.shape[0]
    wide = (heads + 2) * HEAD_SIZE
    x_plan, x_arrays = zip(*gathered["x"])
    g_plan, g_arrays = zip(*gathered["g"])
    w_arrays, shards = [], []
    for offset, chunks in gathered["w"]:
        shards.append((offset, []))
        for array, part, at in chunks:
            index = next((i for i, known in enumerate(w_arrays) if known is array), len(w_arrays))
            w_arrays += [array] if index == len(w_arrays) else []
            shards[-1][1].append((index, part, at))
    depth = w_arrays[-1].shape[0]
    plan = dict(plan, x=x_plan, g=g_plan, shards=shards, depth=depth)
    base = pl.pallas_call(
        functools.partial(project_kernel, plan),
        out_shape=jax.ShapeDtypeStruct((tokens, wide), jnp.float32),
        in_specs=[SMEM, VMEM, VMEM] + [ANY] * (len(x_arrays) + len(w_arrays)),
        out_specs=VMEM,
        scratch_shapes=[
            pltpu.VMEM((tokens, feats + LANES), jnp.bfloat16),
            pltpu.VMEM((len(shards) * depth, wide), jnp.bfloat16),
            pltpu.SemaphoreType.DMA((len(x_arrays) + 2 * len(shards),)),
        ],
        cost_estimate=pl.CostEstimate(flops=0, bytes_accessed=0, transcendentals=0),
        compiler_params=PARAMS,
        name="project",
    )(place, up_q, up_v, *x_arrays, *w_arrays)

    offset, chunks = gathered["last"] or (None, [])
    plan["last"] = None if offset is None else (offset, [chunk[1:] for chunk in chunks])
    last = [chunks[0][0]] if chunks else []
    return pl.pallas_call(
        functools.partial(attend_kernel, plan),
        out_shape=[
            jax.ShapeDtypeStruct((parts, 2 * rank, feats // parts), jnp.bfloat16),
            jax.ShapeDtypeStruct((rank, (heads + 1) * HEAD_SIZE), jnp.float32),
        ],
        in_specs=[SMEM, VMEM, VMEM]
        + [ANY] * (1 + len(x_arrays) + len(g_arrays))
        + [ANY] * len(last),
        out_specs=[VMEM] * 2,
        scratch_shapes=[
            pltpu.VMEM((tokens, feats + LANES), jnp.bfloat16),
            pltpu.VMEM((tokens, heads * HEAD_SIZE), jnp.bfloat16),
            pltpu.VMEM((depth, wide) if last else (16, LANES), jnp.bfloat16),
            pltpu.VMEM((tokens, wide), jnp.float32),
            pltpu.VMEM((3 * rank, tokens), jnp.bfloat16),
            pltpu.SemaphoreType.DMA((len(chunks) + tokens // seq + len(x_arrays) + len(g_arrays),)),
        ],
        compiler_params=PARAMS,
        name="attend",
    )(place, up_q, up_v, base, *x_arrays, *g_arrays, *last)


def ringed(value):
    return lax.ppermute(value, "z", [(0, 1), (1, 3), (3, 2), (2, 0)])


def paired_gather(place, qw, kw, vw, heads, norm_args, gradient):
    shard, rows = qw.shape[0], norm_args[0].shape[0]
    mine = lax.axis_index(GROUP)
    kept, given = pack_weights(mine, qw, kw, vw, heads)
    near, beside = join_rows(lax.axis_index("c"), kept, swapped(given, ("c",), 1))
    far = swapped(beside, ("y",), 1)
    normed, later = norm_tokens(*norm_args, 2, beside)
    c_tokens, x_tokens = swapped(normed, ("c",), 1), swapped(normed, ("ctx",), 1)
    (near_1,) = fence((ringed(near),), wait_us=6)
    later, gradient = fence((later, gradient), far, near_1)
    y_tokens = swapped(later, ("y",), 1)
    hop_1 = jnp.concatenate([near_1, ringed(far)], 0)

    hop_2 = ringed(hop_1)
    half = rows // 2
    far_low, far_high = swapped(x_tokens[:half], ("y",), 1), swapped(y_tokens[half:], ("ctx",), 1)
    xc_tokens = swapped(x_tokens, ("c",), 1)
    (gradient,) = fence((gradient,), hop_1, xc_tokens)
    gradient = lax.all_to_all(gradient, GROUP, 0, 0, tiled=True)

    hop_3 = ringed(hop_2)
    (y_tokens,) = fence((y_tokens,), hop_2)
    yc_tokens, farc_low, farc_high = (swapped(value, ("c",), 1) for value in (y_tokens, far_low, far_high))

    def weight_columns(back):
        def columns(p):
            at = (p[1] ^ (p[1] >> 1)) - back + 4 & 3
            return (at ^ (at >> 1)) * 4 * shard

        return columns

    def token_rows(step, skip=0):
        return lambda p: (step & 3) * 2 * rows + ((p[0] >> 2) ^ (step >> 2)) * rows + skip

    def source(step):
        return lambda p: p[0] ^ step

    size = 2 * shard

    def ordered(first, second):
        return [
            (first, slice(0, size), lambda p: (p[0] & 2) * shard),
            (second, slice(-size, None), lambda p: (2 - (p[0] & 2)) * shard),
        ]

    pieces = [(0, 0, normed), (1, 0, c_tokens), (2, 0, y_tokens), (3, 0, yc_tokens), (4, 0, x_tokens)]
    pieces += [(5, 0, xc_tokens), (6, 0, far_low), (6, half, far_high), (7, 0, farc_low), (7, half, farc_high)]
    return {
        "w": [
            (weight_columns(0), ordered(near, far)),
            (weight_columns(1), ordered(hop_1, hop_1)),
            (weight_columns(2), ordered(hop_2, hop_2)),
        ],
        "last": (weight_columns(3), ordered(hop_3, hop_3)),
        "x": [((token_rows(step, skip), step & 3, None), value) for step, skip, value in pieces],
        "g": [((token_rows(step), step & 3, source(step)), gradient) for step in range(8)],
    }


def on_device(
    tokens,
    trace_index,
    input_norm_scale,
    query_weight,
    key_weight,
    value_weight,
    query_down_weight,
    query_up_weight,
    value_down_weight,
    value_up_weight,
    output_gradient,
):
    rows, feats = tokens.shape[1:]
    heads_kv = key_weight.shape[1] // HEAD_SIZE
    heads = query_weight.shape[1] // HEAD_SIZE // heads_kv
    group = heads * HEAD_SIZE
    rank = query_up_weight.shape[0]
    sizes = [lax.axis_size(axis) for axis in GROUP]
    parts = math.prod(sizes)
    shards = lax.axis_size("z")
    paired = sizes == [2, 2, 2] and shards == 4
    mine = lax.axis_index(GROUP)
    place = jnp.stack([mine, lax.axis_index("z")]).astype(jnp.int32)

    norm_args = (
        tokens.reshape(rows, feats),
        trace_index.reshape(1, rows),
        input_norm_scale,
        query_down_weight.T,
        value_down_weight.T,
    )
    gradient = jnp.moveaxis(output_gradient.reshape(rows, parts, group), 1, 0)
    if paired:
        gathered = paired_gather(
            place, query_weight, key_weight, value_weight, heads, norm_args, gradient
        )
    else:
        shard = query_weight.shape[0]
        split = [w.reshape(shard, parts, -1) for w in (query_weight, key_weight, value_weight)]
        columns = jnp.moveaxis(jnp.concatenate(split, -1), 1, 0)
        per = parts // sizes[0]
        columns = lax.dynamic_slice_in_dim(columns, lax.axis_index("ctx") * per, per, 0)
        columns = lax.all_to_all(columns, ("y", "c"), 0, 0, tiled=True).reshape(per * shard, -1)
        weights = lax.all_gather(columns, "z", axis=0, tiled=True)
        normed = lax.all_gather(norm_tokens(*norm_args, 1)[0], ("y", "c", "ctx"), axis=0, tiled=True)
        gradient = lax.all_to_all(gradient, GROUP, 0, 0, tiled=True)
        gradient = gradient.reshape(sizes[0], per, rows, group)
        gradient = jnp.moveaxis(gradient, 0, 1).reshape(parts * rows, group)
        gathered = {
            "w": [(lambda p: 0, [(weights, slice(None), lambda p: 0)])],
            "last": None,
            "x": [((lambda p: 0, 0, None), normed)],
            "g": [((lambda p: 0, 0, None), gradient)],
        }

    plan = {
        "feats": feats,
        "heads": heads,
        "seq": sizes[0] * rows,
        "window": 2 * rows,
        "span": min(sizes[0], 2) * rows,
        "tokens": parts * rows,
        "parts": parts,
    }
    ga, gb = attend(place, query_up_weight, value_up_weight, gathered, plan)

    coefficient = ADAPTER_NAME / math.sqrt(parts * shards * rows)
    part = jnp.sum(lax.all_to_all(ga, GROUP, 0, 0, tiled=True).astype(jnp.float32), 0)
    mixed = jnp.concatenate([part, gb], 0).astype(jnp.bfloat16)
    if paired:
        for step in (1, 2):
            mixed = add_wide(mixed, swapped(mixed, ("z",), step)).astype(jnp.bfloat16)
    else:
        mixed = lax.psum(mixed.astype(jnp.float32), "z")
    scaled = (mixed.astype(jnp.float32) * coefficient).astype(jnp.bfloat16)
    chips = ("ctx", "y")
    scaled = [scaled] + [swapped(scaled, chips, step) for step in range(1, sizes[0] * sizes[1])]
    if sizes[2] == 2:
        scaled = [piece for value in scaled for piece in (value, swapped(value, ("c",), 1))]
    for bit in range(parts.bit_length() - 1):
        one = (mine >> bit) & 1 == 1
        scaled = [jnp.where(one, scaled[at ^ (1 << bit)], scaled[at]) for at in range(parts)]
    scaled = [value.astype(jnp.float32) for value in scaled]
    aq, av, bq, bv = (
        jnp.concatenate([value[rows_of, columns] for value in scaled], 1)
        for rows_of, columns in (
            (slice(0, rank), slice(None)),
            (slice(rank, 2 * rank), slice(None)),
            (slice(2 * rank, None), slice(0, group)),
            (slice(2 * rank, None), slice(group, None)),
        )
    )
    return aq.T, bq, av.T, bv


def solution(mesh):
    groups, ctx, fsdp = (mesh.shape[name] for name in ("groups", "ctx", "fsdp"))

    def run(*args):
        heads_kv = args[4].shape[1] // HEAD_SIZE
        share = heads_kv // ctx
        cores = 2 if share % 2 == 0 else 1
        split = (groups, ctx, fsdp // share, share // cores, cores)
        finer = Mesh(mesh.devices.reshape(split), ("groups", "ctx", "z", "y", "c"))
        whole = ("z", "y", "c")
        sequences = ("groups",) + whole
        by_rows = P(whole, None)
        by_tokens = P(sequences, "ctx", None)
        out = P("groups", None)
        return jax.shard_map(
            on_device,
            mesh=finer,
            in_specs=(
                by_tokens, P(sequences, "ctx"), P(), by_rows, by_rows, by_rows, P(), P(), P(), P(), by_tokens
            ),
            out_specs=(out, out, out, out),
            check_vma=False,
        )(*args)

    return run
```
